32 devices in a mesh: dp: 8 (over y, x, core), tensor: 4 (over z).
Axes of the slice: x: 2, y: 2, z: 4, core: 2. Of those that a mesh axis runs over, the one named last changes fastest.
Arguments:
- inputs: bfloat16 [16, 256, 768], P('dp'), may hold values from -6 to 6
- condition: bfloat16 [16, 768], P('dp'), may hold values from -6 to 6
- cotangent: bfloat16 [16, 256, 768], P('dp'), may hold values from -6 to 6
- w_ada: float32 [6, 768, 768], P(None, 'tensor'), may hold values from -0.21875 to 0.21875
- w_qkv: float32 [3, 768, 768], P(None, 'tensor'), may hold values from -0.21875 to 0.21875
- w_proj: float32 [768, 768], P('tensor'), may hold values from -0.625 to 0.625
- w_up: float32 [4, 768, 768], P(None, 'tensor'), may hold values from -0.21875 to 0.21875
- w_down: float32 [4, 768, 768], P(None, 'tensor'), may hold values from -0.109375 to 0.109375
- biases: float32 [14, 768], P(None, 'tensor'), may hold values from -2.5 to 2.5
- momentum_ada: float32 [6, 768, 768], P(None, 'tensor'), as said below
- momentum_qkv: float32 [3, 768, 768], P(None, 'tensor'), as said below
- momentum_proj: float32 [768, 768], P('tensor'), as said below
- momentum_up: float32 [4, 768, 768], P(None, 'tensor'), as said below
- momentum_down: float32 [4, 768, 768], P(None, 'tensor'), as said below
- bias_first: float32 [14, 768], P(None, 'tensor'), as said below
- bias_second: float32 [14, 768], P(None, 'tensor'), as said below
Outputs:
- output: bfloat16 [16, 256, 768], P('dp')
- grad_inputs: bfloat16 [16, 256, 768], P('dp')
- grad_condition: float32 [16, 768], P('dp')
- new_w_ada: float32 [6, 768, 768], P(None, 'tensor', 'dp')
- new_w_qkv: float32 [3, 768, 768], P(None, 'tensor', 'dp')
- new_w_proj: float32 [768, 768], P('tensor', 'dp')
- new_w_up: float32 [4, 768, 768], P(None, 'tensor', 'dp')
- new_w_down: float32 [4, 768, 768], P(None, 'tensor', 'dp')
- new_momentum_ada: float32 [6, 768, 768], P(None, 'tensor')
- new_momentum_qkv: float32 [3, 768, 768], P(None, 'tensor')
- new_momentum_proj: float32 [768, 768], P('tensor')
- new_momentum_up: float32 [4, 768, 768], P(None, 'tensor')
- new_momentum_down: float32 [4, 768, 768], P(None, 'tensor')
- new_biases: float32 [14, 768], P(None, 'tensor')
- new_bias_first: float32 [14, 768], P(None, 'tensor')
- new_bias_second: float32 [14, 768], P(None, 'tensor')
The draws below stay inside these ranges and needn't reach their ends.
Inputs may be any that keep to these rules, and one draw needn't show every extreme that they name: `momentum_ada`: float32 values of either sign. `momentum_qkv`: float32 values of either sign. `momentum_proj`: float32 values of either sign. `momentum_up`: float32 values of either sign. `momentum_down`: float32 values of either sign. `bias_first`: float32 values of either sign. `bias_second`: positive float32 values.
All inputs are finite; a program needn't handle non-finite values.
Results may differ from the reference program's by a relative error of at most 0.0203.
Values may be sent and summed in bfloat16 or wider, within the bound.
No kernel may reach another device: no remote copies, remote signals or barrier semaphores. Data moves between devices by JAX's collectives and lax.ppermute only.
A program may use at most 192 MiB of HBM per device.

```python
import math
import jax
import jax.numpy as jnp
from jax import lax

HEADS = 12
HEAD_DIM = 64
D = 768
FF = 3072
SEQ = 256
LATENTS = 16
TOKENS = 4096
NS_ITERS = 5
STEP = 10


def column_ramp(array_shape, axis_number, top_ratio):
    length = array_shape[axis_number]
    fraction = jnp.arange(length, dtype=jnp.float32) / max(length - 1, 1)
    ramp_curve = jnp.exp(fraction * math.log(top_ratio))
    view_shape = [1] * len(array_shape)
    view_shape[axis_number] = length
    return ramp_curve.reshape(view_shape)


def base_normal(key, array_shape):
    return jax.random.truncated_normal(key, -4.0, 4.0, array_shape, jnp.float32)


def draw_momentum_ada(key, part):
    key = jax.random.fold_in(key, 11)
    array_shape = (6, D, D)
    return base_normal(key, array_shape) * column_ramp(array_shape, 1, 6.0) * (0.3 * math.sqrt(TOKENS))


def draw_momentum_qkv(key, part):
    key = jax.random.fold_in(key, 12)
    array_shape = (3, D, D)
    return base_normal(key, array_shape) * column_ramp(array_shape, 1, 6.0) * (0.3 * math.sqrt(TOKENS))


def draw_momentum_proj(key, part):
    key = jax.random.fold_in(key, 13)
    array_shape = (D, D)
    return base_normal(key, array_shape) * column_ramp(array_shape, 0, 6.0) * (0.3 * math.sqrt(TOKENS))


def draw_momentum_up(key, part):
    key = jax.random.fold_in(key, 14)
    array_shape = (FF // D, D, D)
    return base_normal(key, array_shape) * column_ramp(array_shape, 1, 6.0) * (0.3 * math.sqrt(TOKENS))


def draw_momentum_down(key, part):
    key = jax.random.fold_in(key, 15)
    array_shape = (FF // D, D, D)
    return base_normal(key, array_shape) * column_ramp(array_shape, 1, 6.0) * (0.3 * math.sqrt(TOKENS))


def draw_bias_first(key, part):
    key = jax.random.fold_in(key, 16)
    return base_normal(key, (10 + FF // D, D)) * (0.055 * math.sqrt(TOKENS))


def draw_bias_second(key, part):
    key = jax.random.fold_in(key, 17)
    factor = jnp.exp(jax.random.uniform(key, (10 + FF // D, D), jnp.float32, 0.0, math.log(4.0)))
    return factor * (0.00025 * TOKENS)


def steps_of(rng, dims, shards, least, high):
    factor_of = 1.0
    for position, shards_of in shards:
        steps = jax.random.uniform(jax.random.fold_in(jax.random.fold_in(rng, 6), position), (shards_of,), jnp.float32, least / len(shards), high / len(shards))
        factor_of = factor_of * jnp.repeat(jnp.exp(steps), dims[position] // shards_of).reshape((-1,) + (1,) * (len(dims) - 1 - position))
    return factor_of


def bell_draw(own_key, dims, deviation, most, pieces=(), kind=jnp.bfloat16):
    factor_of = steps_of(own_key, dims, pieces, -0.22, 0.18) if pieces else 1.0
    values = jax.random.normal(own_key, dims, jnp.float32) * deviation * factor_of
    return jnp.minimum(jnp.maximum(values, -most), most).astype(kind)


def setup_inputs(seed: int = 0) -> dict:
    key_of = jax.random.split(jax.random.key(seed), 17)
    return {
        "inputs": bell_draw(key_of[0], (LATENTS, SEQ, D), 1.0, 6.0, ((0, 8),)),
        "condition": bell_draw(key_of[1], (LATENTS, D), 1.0, 6.0, ((0, 8),)),
        "cotangent": bell_draw(key_of[2], (LATENTS, SEQ, D), 1.0, 6.0, ((0, 8),)),
        "w_ada": bell_draw(key_of[3], (6, D, D), D ** -0.5, 0.21875, ((1, 4),), jnp.float32),
        "w_qkv": bell_draw(key_of[4], (3, D, D), D ** -0.5, 0.21875, ((1, 4),), jnp.float32),
        "w_proj": bell_draw(key_of[5], (D, D), (D // 8) ** -0.5, 0.625, ((0, 4),), jnp.float32),
        "w_up": bell_draw(key_of[6], (FF // D, D, D), D ** -0.5, 0.21875, ((1, 4),), jnp.float32),
        "w_down": bell_draw(key_of[7], (FF // D, D, D), FF ** -0.5, 0.109375, ((1, 4),), jnp.float32),
        "biases": bell_draw(key_of[8], (10 + FF // D, D), 0.3, 2.5, ((1, 4),), jnp.float32),
        "momentum_ada": draw_momentum_ada(jax.random.fold_in(key_of[16], 71), 0),
        "momentum_qkv": draw_momentum_qkv(jax.random.fold_in(key_of[16], 71), 0),
        "momentum_proj": draw_momentum_proj(jax.random.fold_in(key_of[16], 71), 0),
        "momentum_up": draw_momentum_up(jax.random.fold_in(key_of[16], 71), 0),
        "momentum_down": draw_momentum_down(jax.random.fold_in(key_of[16], 71), 0),
        "bias_first": draw_bias_first(jax.random.fold_in(key_of[16], 71), 0),
        "bias_second": draw_bias_second(jax.random.fold_in(key_of[16], 71), 0),
    }


HIGH = lax.Precision.HIGHEST
NS_A = 3.4445
NS_B = -4.775
NS_C = 2.0315
MUON_RATE = 0.16
MUON_DECAY = 0.01
MUON_MOMENTUM = 0.95
ADAM_RATE = 0.25
BETA_ONE = 0.9
BETA_TWO = 0.999
ADAM_EPS = 1e-08
NORM_EPS = 1e-06

@jax.custom_vjp
def low(v):
    return lax.optimization_barrier(v.astype(jnp.bfloat16)).astype(jnp.float32)

@jax.custom_vjp
def low_back(v):
    return v

def low_keep(v):
    return (low(v), None)

def low_pass(kept, grad):
    return (grad,)

def back_keep(v):
    return (v, None)

def back_low(kept, grad):
    return (low(grad),)
low.defvjp(low_keep, low_pass)
low_back.defvjp(back_keep, back_low)

def layer_norm(values):
    average = lax.optimization_barrier(jnp.mean(values, axis=-1, keepdims=True))
    centered = values - average
    variance = lax.optimization_barrier(jnp.mean(centered * centered, axis=-1, keepdims=True))
    return centered * lax.rsqrt(variance + NORM_EPS)

def modulate(values, shift_by, scale_by):
    return layer_norm(values) * (1.0 + scale_by[:, None, :]) + shift_by[:, None, :]

def forward(weights, inputs, condition):
    w_ada, w_qkv, w_proj, w_up, w_down, biases = weights
    groups = inputs.shape[0]
    seq_length = inputs.shape[1]
    cond_act = low(jax.nn.silu(condition))
    modulation = low_back(jnp.einsum('bd,ked->bke', cond_act, low(w_ada), precision=HIGH)) + biases[0:6]
    hidden_first = low(modulate(inputs, modulation[:, 0], modulation[:, 1]))
    projected = low_back(jnp.einsum('bsd,ked->bske', hidden_first, low(w_qkv), precision=HIGH))
    queries = low(projected[:, :, 0] + biases[6]).reshape(groups, seq_length, HEADS, HEAD_DIM)
    key_rows = low(projected[:, :, 1]).reshape(groups, seq_length, HEADS, HEAD_DIM)
    value_rows = low(projected[:, :, 2] + biases[7]).reshape(groups, seq_length, HEADS, HEAD_DIM)
    scale_factor = 1.0 / math.sqrt(HEAD_DIM)
    scores = low_back(jnp.einsum('bqhc,bkhc->bhqk', queries, key_rows, precision=HIGH) * scale_factor)
    probs = low(jax.nn.softmax(scores, axis=-1))
    attended = low(low_back(jnp.einsum('bhqk,bkhc->bqhc', probs, value_rows, precision=HIGH)))
    attended = attended.reshape(groups, seq_length, HEADS * HEAD_DIM)
    branch_first = low_back(jnp.einsum('bsd,de->bse', attended, low(w_proj), precision=HIGH)) + biases[8]
    middle = inputs + modulation[:, 2][:, None, :] * branch_first
    hidden_second = low(modulate(middle, modulation[:, 3], modulation[:, 4]))
    pre_act = low_back(jnp.einsum('bsd,red->bsre', hidden_second, low(w_up), precision=HIGH)) + biases[9:13]
    activated = low(jax.nn.gelu(pre_act, approximate=True))
    branch_second = low_back(jnp.einsum('bsre,red->bsd', activated, low(w_down), precision=HIGH)) + biases[13]
    return middle + modulation[:, 5][:, None, :] * branch_second

def newton_schulz(start):
    current = start
    for iteration in range(NS_ITERS):
        gram = low(jnp.dot(current, current.T, precision=HIGH, preferred_element_type=jnp.float32))
        poly = low(NS_B * gram + NS_C * jnp.dot(gram, gram, precision=HIGH, preferred_element_type=jnp.float32))
        current = low(NS_A * current + jnp.dot(poly, current, precision=HIGH, preferred_element_type=jnp.float32))
    return current

def muon_step(weight, momentum, gradient, flipped):
    new_momentum = MUON_MOMENTUM * momentum + gradient
    if flipped:
        oriented = new_momentum.reshape(-1, new_momentum.shape[-1]).T
    else:
        oriented = new_momentum.reshape(new_momentum.shape[0], -1)
    start = low(oriented / (jnp.sqrt(jnp.sum(oriented * oriented)) + 1e-07))
    ortho = newton_schulz(start)
    row_count, column_count = ortho.shape
    if flipped:
        restored = ortho.T.reshape(weight.shape)
    else:
        restored = ortho.reshape(weight.shape)
    new_weight = weight * (1.0 - MUON_RATE * MUON_DECAY) - MUON_RATE * 0.2 * math.sqrt(max(row_count, column_count)) * restored
    return (new_weight, new_momentum)

def reference(inputs, condition, cotangent, w_ada, w_qkv, w_proj, w_up, w_down, biases, momentum_ada, momentum_qkv, momentum_proj, momentum_up, momentum_down, bias_first, bias_second):
    weights = (w_ada, w_qkv, w_proj, w_up, w_down, biases)
    group = math.gcd(LATENTS, 16)
    count_groups = LATENTS // group
    inputs_all = inputs.astype(jnp.float32).reshape(count_groups, group, SEQ, D)
    cond_all = condition.astype(jnp.float32).reshape(count_groups, group, D)
    tangent_all = cotangent.astype(jnp.float32).reshape(count_groups, group, SEQ, D)

    def one_group(totals, pieces_in):
        inputs_part, cond_part, tangent_part = pieces_in
        result, pullback = jax.vjp(forward, weights, inputs_part, cond_part)
        grad_weights, grad_part, grad_cond = pullback(tangent_part)
        totals = jax.tree.map(jnp.add, totals, grad_weights)
        return (totals, (result.astype(jnp.bfloat16), grad_part.astype(jnp.bfloat16), grad_cond))
    zeros_start = jax.tree.map(jnp.zeros_like, weights)
    grads, (outputs, grads_in, grads_cond) = lax.scan(one_group, zeros_start, (inputs_all, cond_all, tangent_all))
    grad_ada, grad_qkv, grad_proj, grad_up, grad_down, grad_biases = grads
    output = outputs.reshape(LATENTS, SEQ, D)
    grad_inputs = grads_in.reshape(LATENTS, SEQ, D)
    grad_condition = grads_cond.reshape(LATENTS, D)
    new_w_ada, new_momentum_ada = muon_step(w_ada, momentum_ada, grad_ada, True)
    new_w_qkv, new_momentum_qkv = muon_step(w_qkv, momentum_qkv, grad_qkv, True)
    new_w_proj, new_momentum_proj = muon_step(w_proj, momentum_proj, grad_proj, False)
    new_w_up, new_momentum_up = muon_step(w_up, momentum_up, grad_up, True)
    new_w_down, new_momentum_down = muon_step(w_down, momentum_down, grad_down, True)
    new_bias_first = BETA_ONE * bias_first + (1.0 - BETA_ONE) * grad_biases
    new_bias_second = BETA_TWO * bias_second + (1.0 - BETA_TWO) * grad_biases * grad_biases
    first_hat = new_bias_first / (1.0 - BETA_ONE ** STEP)
    second_hat = new_bias_second / (1.0 - BETA_TWO ** STEP)
    new_biases = biases - ADAM_RATE * first_hat / (jnp.sqrt(second_hat) + ADAM_EPS)
    return (output, grad_inputs, grad_condition, new_w_ada, new_w_qkv, new_w_proj, new_w_up, new_w_down, new_momentum_ada, new_momentum_qkv, new_momentum_proj, new_momentum_up, new_momentum_down, new_biases, new_bias_first, new_bias_second)
```

```python
import math

import jax
import jax.numpy as jnp
from jax import lax
from jax.sharding import PartitionSpec as P

HEAD_DIM = 64
NS_ITERS = 5
STEP = 10


NS_A = 3.4445
NS_B = -4.775
NS_C = 2.0315
MUON_RATE = 0.16
MUON_DECAY = 0.01
MUON_MOMENTUM = 0.95
ADAM_RATE = 0.25
BETA_ONE = 0.9
BETA_TWO = 0.999
ADAM_EPS = 1e-08
NORM_EPS = 1e-06

BF = jnp.bfloat16
F32 = jnp.float32
TILE = 256
OWNERS = (0, 2, 1, 4, 6)


def layer_norm(values):
    average = jnp.mean(values, axis=-1, keepdims=True)
    centered = values - average
    variance = jnp.mean(centered * centered, axis=-1, keepdims=True)
    return centered * lax.rsqrt(variance + NORM_EPS)


def modulate(values, shift_by, scale_by):
    return layer_norm(values) * (1.0 + scale_by[:, None, :]) + shift_by[:, None, :]


def gelu_tanh(values):
    return jax.nn.gelu(values, approximate=True)


def dot(a, b):
    return jnp.dot(a, b, preferred_element_type=F32)


def dot_t(a, b):
    return lax.dot_general(a, b, (((1,), (1,)), ((), ())), preferred_element_type=F32)


def t_dot(a, b):
    return lax.dot_general(a, b, (((0,), (0,)), ((), ())), preferred_element_type=F32)


def parts(value):
    high = value.astype(BF)
    return high, (value - high.astype(F32)).astype(BF)


def newton_schulz_factor(gram):
    width = gram.shape[0]
    eye = jnp.eye(width, dtype=F32)
    scale = 1.0 / (jnp.sqrt(jnp.sum(gram * eye)) + 1e-07)
    current = gram * (scale * scale)
    factor = None
    for iteration in range(NS_ITERS):
        low = current.astype(BF)
        poly = (NS_B * current + NS_C * dot(low, low)).astype(BF)
        if factor is None:
            factor = NS_A * eye + poly.astype(F32)
        else:
            high, rest = parts(factor)
            factor = NS_A * factor + dot(high, poly) + dot(rest, poly)
        if iteration < NS_ITERS - 1:
            high, rest = parts(current)
            half = NS_A * current + dot(high, poly) + dot(rest, poly)
            high, rest = parts(half)
            current = NS_A * half + dot(poly, high) + dot(poly, rest)
    return factor * scale


def pack(gram):
    count = gram.shape[0] // TILE
    return jnp.stack(
        [
            gram[i * TILE : (i + 1) * TILE, j * TILE : (j + 1) * TILE]
            for i in range(count)
            for j in range(i, count)
        ]
    )


def unpack(blocks, width):
    count = width // TILE
    index = {}
    for i in range(count):
        for j in range(i, count):
            index[i, j] = len(index)
    rows = []
    for i in range(count):
        rows.append(
            jnp.concatenate(
                [blocks[index[i, j]] if j >= i else blocks[index[j, i]].T for j in range(count)], axis=1
            )
        )
    return jnp.concatenate(rows, axis=0)


def on_device(
    inputs,
    condition,
    cotangent,
    w_ada,
    w_qkv,
    w_proj,
    w_up,
    w_down,
    biases,
    momentum_ada,
    momentum_qkv,
    momentum_proj,
    momentum_up,
    momentum_down,
    bias_first,
    bias_second,
):
    quarter = w_ada.shape[1]
    width = w_ada.shape[-1]
    latent_count = inputs.shape[0]
    seq_length = inputs.shape[1]
    tokens = latent_count * seq_length
    heads_here = quarter // HEAD_DIM
    offset = lax.axis_index("tensor") * quarter
    scale_factor = 1.0 / math.sqrt(HEAD_DIM)
    flat = lambda w: w.reshape(-1, width)
    ada_low = flat(w_ada).astype(BF)
    qkv_low = flat(w_qkv).astype(BF)
    proj_low = w_proj.astype(BF)
    up_low = flat(w_up).astype(BF)
    down_low = flat(w_down).astype(BF)
    up_bias = biases[9:13].reshape(-1)

    cond_act, silu_pull = jax.vjp(jax.nn.silu, condition.astype(F32))
    cond_low = cond_act.astype(BF)
    mod_part = dot_t(cond_low, ada_low).reshape(latent_count, 6, quarter) + biases[0:6]
    mod_part = jnp.concatenate(
        [mod_part.reshape(-1, quarter), biases[8:9], biases[13:14]], axis=0
    )
    gathered = lax.all_gather(mod_part, "tensor", axis=1, tiled=True)
    modulation = gathered[: latent_count * 6].reshape(latent_count, 6, width)
    out_bias = gathered[latent_count * 6 :]

    inputs_f = inputs.astype(F32)
    hidden_first, first_pull = jax.vjp(modulate, inputs_f, modulation[:, 0], modulation[:, 1])
    first_low = hidden_first.astype(BF).reshape(tokens, width)
    projected = dot_t(first_low, qkv_low)
    head_shape = (latent_count, seq_length, heads_here, HEAD_DIM)
    query_heads = (projected[:, :quarter] + biases[6]).astype(BF).reshape(head_shape)
    key_heads = projected[:, quarter : 2 * quarter].astype(BF).reshape(head_shape)
    value_heads = (projected[:, 2 * quarter :] + biases[7]).astype(BF).reshape(head_shape)
    scores = (
        jnp.einsum("bqhc,bkhc->bhqk", query_heads, key_heads, preferred_element_type=F32)
        * scale_factor
    )
    row_top = jnp.max(scores, axis=-1, keepdims=True)
    log_total = row_top + jnp.log(jnp.sum(jnp.exp(scores - row_top), axis=-1, keepdims=True))
    probs_low = jnp.exp(scores - log_total).astype(BF)
    attended = jnp.einsum("bhqk,bkhc->bqhc", probs_low, value_heads, preferred_element_type=F32)
    attended_low = attended.reshape(tokens, quarter).astype(BF)
    partial_first = dot(attended_low, proj_low).reshape(latent_count, seq_length, width)
    branch_first = lax.psum(partial_first.astype(BF), "tensor").astype(F32) + out_bias[0]
    gate_first = modulation[:, 2][:, None, :]
    middle = inputs_f + gate_first * branch_first
    hidden_second, second_pull = jax.vjp(modulate, middle, modulation[:, 3], modulation[:, 4])
    second_low = hidden_second.astype(BF).reshape(tokens, width)
    pre_act = dot_t(second_low, up_low) + up_bias
    activated, gelu_pull = jax.vjp(gelu_tanh, pre_act)
    act_low = activated.astype(BF)

    gate_second = modulation[:, 5][:, None, :]
    tangent = cotangent.astype(F32)
    d_branch_second = gate_second * tangent
    d_down_bias = jnp.sum(d_branch_second, axis=(0, 1))
    d_second_low = d_branch_second.astype(BF).reshape(tokens, width)
    d_act = dot_t(d_second_low, down_low)
    d_pre = gelu_pull(d_act)[0]
    d_up_bias = jnp.sum(d_pre, axis=0).reshape(-1, quarter)
    d_pre_low = d_pre.astype(BF)
    d_second_part = dot(d_pre_low, up_low).astype(BF)
    d_second_sum = lax.psum(d_second_part, "tensor")

    partial_second = dot(act_low, down_low).astype(BF)
    partial_second, d_second_sum = lax.optimization_barrier((partial_second, d_second_sum))
    second_sum = lax.psum(partial_second, "tensor")

    grad_down = t_dot(act_low, d_second_low).astype(BF)
    grad_up = t_dot(d_pre_low, second_low).astype(BF)
    grad_up, grad_down = lax.psum((grad_up, grad_down), "dp")

    d_hidden_second = d_second_sum.reshape(latent_count, seq_length, width).astype(F32)
    d_middle_norm, d_shift_second, d_scale_second = second_pull(d_hidden_second)
    d_middle = tangent + d_middle_norm
    d_branch_first = gate_first * d_middle
    d_gate_first = jnp.sum(d_middle * branch_first, axis=1)
    d_proj_bias = jnp.sum(d_branch_first, axis=(0, 1))
    d_first_low = d_branch_first.astype(BF).reshape(tokens, width)
    grad_proj = t_dot(attended_low, d_first_low).astype(BF)
    d_attended = dot_t(d_first_low, proj_low).astype(BF).reshape(head_shape)
    probs = jnp.exp(scores - log_total)
    probs_again = probs.astype(BF)
    d_values = jnp.einsum("bhqk,bqhc->bkhc", probs_again, d_attended, preferred_element_type=F32)
    d_probs = jnp.einsum("bqhc,bkhc->bhqk", d_attended, value_heads, preferred_element_type=F32)
    d_scores = (probs * (d_probs - jnp.sum(probs * d_probs, axis=-1, keepdims=True))).astype(BF)
    d_queries = (
        jnp.einsum("bhqk,bkhc->bqhc", d_scores, key_heads, preferred_element_type=F32)
        * scale_factor
    )
    d_keys = (
        jnp.einsum("bhqk,bqhc->bkhc", d_scores, query_heads, preferred_element_type=F32)
        * scale_factor
    )
    d_queries = d_queries.reshape(tokens, quarter)
    d_keys = d_keys.reshape(tokens, quarter)
    d_values = d_values.reshape(tokens, quarter)
    d_query_bias = jnp.sum(d_queries, axis=0)
    d_value_bias = jnp.sum(d_values, axis=0)
    d_projected_low = jnp.concatenate([d_queries, d_keys, d_values], axis=1).astype(BF)
    d_first_part = dot(d_projected_low, qkv_low).astype(BF)

    d_first_part, second_sum = lax.optimization_barrier((d_first_part, second_sum))
    d_hidden_first = (
        lax.psum(d_first_part, "tensor").reshape(latent_count, seq_length, width).astype(F32)
    )
    branch_second = (
        second_sum.reshape(latent_count, seq_length, width).astype(F32) + out_bias[1]
    )
    output = (middle + gate_second * branch_second).astype(BF)
    d_gate_second = jnp.sum(tangent * branch_second, axis=1)

    grad_qkv = t_dot(d_projected_low, first_low).astype(BF)
    grad_qkv, grad_proj, grad_up, grad_down = lax.optimization_barrier(
        (grad_qkv, grad_proj, grad_up, grad_down)
    )
    grad_qkv, grad_proj = lax.psum((grad_qkv, grad_proj), "dp")

    d_inputs_norm, d_shift_first, d_scale_first = first_pull(d_hidden_first)
    grad_inputs = (d_middle + d_inputs_norm).astype(BF)
    d_modulation = jnp.stack(
        [d_shift_first, d_scale_first, d_gate_first, d_shift_second, d_scale_second, d_gate_second],
        axis=1,
    )
    d_mod_own = lax.dynamic_slice_in_dim(d_modulation, offset, quarter, 2)
    d_cond_part = dot(d_mod_own.reshape(latent_count, -1).astype(BF), ada_low)
    d_proj_own = lax.dynamic_slice_in_dim(d_proj_bias, offset, quarter, 0)
    d_down_own = lax.dynamic_slice_in_dim(d_down_bias, offset, quarter, 0)
    small = jnp.concatenate(
        [
            d_mod_own.reshape(-1, quarter),
            d_query_bias[None],
            d_value_bias[None],
            d_proj_own[None],
            d_up_bias,
            d_down_own[None],
        ],
        axis=0,
    )
    cond_all = lax.all_gather(cond_low, "dp", axis=0, tiled=True)
    small_all = lax.all_gather(small, "dp", axis=0)
    d_mod_all = small_all[:, : 6 * latent_count].reshape(-1, 6, quarter)
    grad_biases = jnp.concatenate(
        [jnp.sum(d_mod_all, axis=0), jnp.sum(small_all[:, 6 * latent_count :], axis=0)], axis=0
    )
    grad_ada = t_dot(d_mod_all.reshape(d_mod_all.shape[0], -1).astype(BF), cond_all)
    d_cond_act = lax.psum(d_cond_part, "tensor")
    grad_condition = silu_pull(d_cond_act)[0]

    moments = (
        MUON_MOMENTUM * flat(momentum_ada) + grad_ada,
        MUON_MOMENTUM * flat(momentum_qkv) + grad_qkv.astype(F32),
        MUON_MOMENTUM * momentum_proj + grad_proj.astype(F32),
        MUON_MOMENTUM * flat(momentum_up) + grad_up.astype(F32),
        MUON_MOMENTUM * flat(momentum_down) + grad_down.astype(F32),
    )
    starts = tuple(m.astype(BF) for m in moments)

    dp_size = lax.axis_size("dp")
    dp_rank = lax.axis_index("dp")
    chosen = jnp.int32(2)
    for matrix_index, owner in enumerate(OWNERS):
        chosen = jnp.where(dp_rank == owner, matrix_index, chosen)
    gram_of = [
        (lambda kept, matrix_index=matrix_index: t_dot(kept[matrix_index], kept[matrix_index]))
        for matrix_index in range(5)
    ]
    gram = lax.switch(chosen, gram_of, starts)
    gram = unpack(lax.psum(pack(gram), "tensor"), width)
    factor = newton_schulz_factor(gram).astype(BF)
    column_width = width // dp_size
    column_start = dp_rank * column_width
    pieces = jnp.moveaxis(factor.reshape(width, dp_size, column_width), 1, 0)
    factors = lax.all_to_all(pieces, "dp", 0, 0, tiled=True)

    weights_old = (w_ada, w_qkv, w_proj, w_up, w_down)
    new_weights = []
    for matrix_index, weight in enumerate(weights_old):
        rows = weight.size // width * lax.axis_size("tensor")
        ortho = dot(starts[matrix_index], factors[OWNERS[matrix_index]])
        weight_columns = lax.dynamic_slice_in_dim(flat(weight), column_start, column_width, 1)
        updated = (
            weight_columns * (1.0 - MUON_RATE * MUON_DECAY)
            - MUON_RATE * 0.2 * math.sqrt(max(rows, width)) * ortho
        )
        new_weights.append(updated.reshape(weight.shape[:-1] + (column_width,)))
    new_bias_first = BETA_ONE * bias_first + (1.0 - BETA_ONE) * grad_biases
    new_bias_second = BETA_TWO * bias_second + (1.0 - BETA_TWO) * grad_biases * grad_biases
    first_hat = new_bias_first / (1.0 - BETA_ONE**STEP)
    second_hat = new_bias_second / (1.0 - BETA_TWO**STEP)
    new_biases = biases - ADAM_RATE * first_hat / (jnp.sqrt(second_hat) + ADAM_EPS)
    return (
        output,
        grad_inputs,
        grad_condition,
        *new_weights,
        moments[0].reshape(momentum_ada.shape),
        moments[1].reshape(momentum_qkv.shape),
        moments[2],
        moments[3].reshape(momentum_up.shape),
        moments[4].reshape(momentum_down.shape),
        new_biases,
        new_bias_first,
        new_bias_second,
    )


def solution(mesh):
    placed = (
        P("dp", None, None),
        P("dp", None),
        P("dp", None, None),
        P(None, "tensor", None),
        P(None, "tensor", None),
        P("tensor", None),
        P(None, "tensor", None),
        P(None, "tensor", None),
        P(None, "tensor"),
        P(None, "tensor", None),
        P(None, "tensor", None),
        P("tensor", None),
        P(None, "tensor", None),
        P(None, "tensor", None),
        P(None, "tensor"),
        P(None, "tensor"),
    )
    return jax.shard_map(
        on_device,
        mesh=mesh,
        in_specs=placed,
        out_specs=(
            P("dp", None, None),
            P("dp", None, None),
            P("dp", None),
            P(None, "tensor", "dp"),
            P(None, "tensor", "dp"),
            P("tensor", "dp"),
            P(None, "tensor", "dp"),
            P(None, "tensor", "dp"),
            P(None, "tensor", None),
            P(None, "tensor", None),
            P("tensor", None),
            P(None, "tensor", None),
            P(None, "tensor", None),
            P(None, "tensor"),
            P(None, "tensor"),
            P(None, "tensor"),
        ),
        check_vma=False,
    )
```

```python
import functools
import math

import jax
import jax.numpy as jnp
from jax import lax
from jax.experimental import pallas as pl
from jax.experimental.pallas import tpu as pltpu
from jax.sharding import PartitionSpec as P

HEAD_DIM = 64
NS_ITERS = 5
STEP = 10


NS_A = 3.4445
NS_B = -4.775
NS_C = 2.0315
MUON_RATE = 0.16
MUON_DECAY = 0.01
MUON_MOMENTUM = 0.95
ADAM_RATE = 0.25
BETA_ONE = 0.9
BETA_TWO = 0.999
ADAM_EPS = 1e-08
NORM_EPS = 1e-06

BF = jnp.bfloat16
F32 = jnp.float32
TILE = 256
VMEM_LIMIT = 48 * 1024 * 1024
OWNERS = (0, 2, 1, 4, 6)


def gelu_tanh(values):
    return jax.nn.gelu(values, approximate=True)


def dot(a, b):
    return jnp.dot(a, b, preferred_element_type=F32)


def dot_t(a, b):
    return lax.dot_general(a, b, (((1,), (1,)), ((), ())), preferred_element_type=F32)


def t_dot(a, b):
    return lax.dot_general(a, b, (((0,), (0,)), ((), ())), preferred_element_type=F32)


def parts(value):
    high = value.astype(BF)
    return high, (value - high.astype(F32)).astype(BF)


def blocks_of(count):
    return [(i, j) for i in range(count) for j in range(i, count)]


def gram_kernel(rows_ref, out_ref):
    count = rows_ref.shape[1] // TILE
    low = rows_ref[...].astype(BF)
    for k, (i, j) in enumerate(blocks_of(count)):
        out_ref[k * TILE : (k + 1) * TILE, :] = t_dot(
            low[:, i * TILE : (i + 1) * TILE], low[:, j * TILE : (j + 1) * TILE]
        )


def gram_blocks(rows):
    depth, width = rows.shape
    count = len(blocks_of(width // TILE))
    return pl.pallas_call(
        gram_kernel,
        out_shape=jax.ShapeDtypeStruct((count * TILE, TILE), F32),
        compiler_params=pltpu.CompilerParams(vmem_limit_bytes=VMEM_LIMIT),
        cost_estimate=pl.CostEstimate(
            flops=2 * depth * width * width, bytes_accessed=depth * width * 6, transcendentals=0
        ),
    )(rows)


def newton_schulz_kernel(
    blocks_ref, cond_ref, corr_ref, out_ref, cur, high, rest, poly, mid_h, mid_l, f_h, f_l, g_h, g_l
):
    width = cur.shape[0]
    spans = [slice(i * TILE, (i + 1) * TILE) for i in range(width // TILE)]
    corr = corr_ref[...]
    corr_h, corr_l = parts(corr)
    cond = cond_ref[...]
    for k, (i, j) in enumerate(blocks_of(width // TILE)):
        block = (
            blocks_ref[k * TILE : (k + 1) * TILE, :]
            + t_dot(cond[:, spans[i]], corr_h[:, spans[j]])
            + t_dot(cond[:, spans[i]], corr_l[:, spans[j]])
            + t_dot(corr_h[:, spans[i]], cond[:, spans[j]])
            + t_dot(corr_l[:, spans[i]], cond[:, spans[j]])
        )
        cur[spans[i], spans[j]] = block
        if i != j:
            cur[spans[j], spans[i]] = block.T
    square_norm = jnp.zeros((1, 1), F32)
    row = lax.broadcasted_iota(jnp.int32, (TILE, TILE), 0)
    col = lax.broadcasted_iota(jnp.int32, (TILE, TILE), 1)
    for span in spans:
        square_norm += jnp.sum(jnp.where(row == col, cur[span, span], 0.0), keepdims=True)
    scale = 1.0 / (jnp.sqrt(square_norm) + 1e-07)
    for span in spans:
        cur[span, :] = cur[span, :] * (scale * scale)

    def make_poly():
        for span in spans:
            high[span, :], rest[span, :] = parts(cur[span, :])
        for span in spans:
            poly[span, :] = (NS_B * cur[span, :] + NS_C * dot(high[span, :], high[...])).astype(BF)

    def step_gram():
        for span in spans:
            half = (
                NS_A * cur[span, :] + dot(high[span, :], poly[...]) + dot(rest[span, :], poly[...])
            )
            mid_h[span, :], mid_l[span, :] = parts(half)
        for span in spans:
            half = mid_h[span, :].astype(F32) + mid_l[span, :].astype(F32)
            cur[span, :] = (
                NS_A * half + dot(poly[span, :], mid_h[...]) + dot(poly[span, :], mid_l[...])
            )

    def stepped_factor(span):
        before = f_h[span, :].astype(F32) + f_l[span, :].astype(F32)
        return NS_A * before + dot(poly[span, :], f_h[...]) + dot(poly[span, :], f_l[...])

    make_poly()
    wide_row = lax.broadcasted_iota(jnp.int32, (TILE, width), 0)
    wide_col = lax.broadcasted_iota(jnp.int32, (TILE, width), 1)
    for i, span in enumerate(spans):
        start = poly[span, :].astype(F32) + jnp.where(wide_row + i * TILE == wide_col, NS_A, 0.0)
        f_h[span, :], f_l[span, :] = parts(start)
    step_gram()

    def middle(_, carry):
        make_poly()
        for span in spans:
            g_h[span, :], g_l[span, :] = parts(stepped_factor(span))
        f_h[...] = g_h[...]
        f_l[...] = g_l[...]
        step_gram()
        return carry

    lax.fori_loop(0, NS_ITERS - 2, middle, 0)
    make_poly()
    for span in spans:
        out_ref[span, :] = (stepped_factor(span) * scale).astype(out_ref.dtype)


def newton_schulz_factor(blocks, cond, corr, width):
    whole = lambda kind: pltpu.VMEM((width, width), kind)
    return pl.pallas_call(
        newton_schulz_kernel,
        out_shape=jax.ShapeDtypeStruct((width, width), BF),
        scratch_shapes=[whole(F32)] + [whole(BF)] * 9,
        compiler_params=pltpu.CompilerParams(vmem_limit_bytes=VMEM_LIMIT),
        cost_estimate=pl.CostEstimate(
            flops=2 * 29 * width**3, bytes_accessed=width * width * 6, transcendentals=0
        ),
    )(blocks, cond, corr)


def update_kernel(sizes, *refs):
    count = len(sizes)
    rows, weights, factor, outs = refs[:count], refs[count : 2 * count], refs[2 * count], refs[2 * count + 1 :]
    for k, size in enumerate(sizes):
        ortho = dot_t(rows[k][...], factor[OWNERS[k]])
        outs[k][...] = (
            weights[k][...] * (1.0 - MUON_RATE * MUON_DECAY)
            - MUON_RATE * 0.2 * math.sqrt(size) * ortho
        )


def update_weights(rows, weights, factors, sizes):
    return pl.pallas_call(
        functools.partial(update_kernel, sizes),
        out_shape=[jax.ShapeDtypeStruct(w.shape, F32) for w in weights],
        compiler_params=pltpu.CompilerParams(vmem_limit_bytes=VMEM_LIMIT),
        cost_estimate=pl.CostEstimate(
            flops=sum(2 * r.size * w.shape[1] for r, w in zip(rows, weights)),
            bytes_accessed=sum(2 * r.size + 12 * w.size for r, w in zip(rows, weights)),
            transcendentals=0,
        ),
    )(*rows, *weights, factors)


def swap(piece, mask, ranks=None):
    size = lax.axis_size("tensor")
    if ranks is None:
        return lax.ppermute(piece, "tensor", [(i, i ^ mask) for i in range(size)])
    pairs = [(r * size + i, r * size + (i ^ mask)) for r in ranks for i in range(size)]
    return lax.ppermute(piece, ("dp", "tensor"), pairs)


def scatter_sum(value, ranks=None):
    size = lax.axis_size("tensor")
    rows = value.shape[0] // size
    total = value[:rows].astype(F32)
    for mask in range(1, size):
        total = total + swap(value[mask * rows : (mask + 1) * rows], mask, ranks).astype(F32)
    return total


def collect(piece, ranks=None):
    size = lax.axis_size("tensor")
    return jnp.concatenate([piece] + [swap(piece, mask, ranks) for mask in range(1, size)], axis=0)


def reorder(value, count, index):
    rows = value.shape[0] // count
    return jnp.concatenate(
        [lax.dynamic_slice_in_dim(value, (index ^ p) * rows, rows, 0) for p in range(count)], axis=0
    )


def normed_of(values):
    average = jnp.mean(values, axis=-1, keepdims=True)
    centered = values - average
    variance = jnp.mean(centered * centered, axis=-1, keepdims=True)
    inverse = lax.rsqrt(variance + NORM_EPS)
    return centered * inverse, inverse


def norm_back(normed, inverse, grad):
    return (
        grad
        - jnp.mean(grad, axis=-1, keepdims=True)
        - normed * jnp.mean(grad * normed, axis=-1, keepdims=True)
    ) * inverse


def on_device(
    inputs,
    condition,
    cotangent,
    w_ada,
    w_qkv,
    w_proj,
    w_up,
    w_down,
    biases,
    momentum_ada,
    momentum_qkv,
    momentum_proj,
    momentum_up,
    momentum_down,
    bias_first,
    bias_second,
):
    quarter = w_ada.shape[1]
    width = w_ada.shape[-1]
    latent_count = inputs.shape[0]
    seq_length = inputs.shape[1]
    tokens = latent_count * seq_length
    heads_here = quarter // HEAD_DIM
    size = lax.axis_size("tensor")
    me = lax.axis_index("tensor")
    dp_size = lax.axis_size("dp")
    dp_rank = lax.axis_index("dp")
    chunk = tokens // size
    my_latent = me // (size // latent_count)
    scale_factor = 1.0 / math.sqrt(HEAD_DIM)
    flat = lambda w: w.reshape(-1, width)
    ada_low = flat(w_ada).astype(BF)
    qkv_low = flat(w_qkv).astype(BF)
    proj_low = w_proj.astype(BF)
    up_low = flat(w_up).astype(BF)
    down_low = flat(w_down).astype(BF)
    up_bias = biases[9:13].reshape(-1)

    cond_act, silu_pull = jax.vjp(jax.nn.silu, condition.astype(F32))
    cond_low = cond_act.astype(BF)
    mod_part = dot_t(cond_low, ada_low).reshape(latent_count * 6, quarter) + jnp.tile(
        biases[0:6], (latent_count, 1)
    )
    mod_part = jnp.concatenate([mod_part, biases[8:9], biases[13:14]], axis=0)
    gathered = collect(mod_part[None])
    gathered = reorder(gathered, size, me)
    gathered = jnp.moveaxis(gathered, 0, 1).reshape(-1, width)
    modulation = reorder(gathered[: latent_count * 6], latent_count, my_latent).reshape(
        latent_count, 6, width
    )
    bias_proj = gathered[latent_count * 6]
    bias_down = gathered[latent_count * 6 + 1]
    shift_first, scale_first, gate_first = modulation[0, 0], modulation[0, 1], modulation[0, 2]
    shift_second, scale_second, gate_second = modulation[0, 3], modulation[0, 4], modulation[0, 5]

    tokens_in = reorder(inputs.reshape(tokens, width), size, me).astype(F32)
    tangent = reorder(cotangent.reshape(tokens, width), size, me).astype(F32)
    per_latent = (latent_count, seq_length, width)
    normed_first, inverse_first = normed_of(tokens_in)
    first_low = (
        (
            normed_first.reshape(per_latent) * (1.0 + modulation[:, 1][:, None, :])
            + modulation[:, 0][:, None, :]
        )
        .astype(BF)
        .reshape(tokens, width)
    )
    projected = dot_t(first_low, qkv_low)
    head_shape = (latent_count, seq_length, heads_here, HEAD_DIM)
    query_heads = (projected[:, :quarter] + biases[6]).astype(BF).reshape(head_shape)
    key_heads = projected[:, quarter : 2 * quarter].astype(BF).reshape(head_shape)
    value_heads = (projected[:, 2 * quarter :] + biases[7]).astype(BF).reshape(head_shape)
    scores = (
        jnp.einsum("bqhc,bkhc->bhqk", query_heads, key_heads, preferred_element_type=F32)
        * scale_factor
    )
    row_top = jnp.max(scores, axis=-1, keepdims=True)
    log_total = row_top + jnp.log(jnp.sum(jnp.exp(scores - row_top), axis=-1, keepdims=True))
    probs_low = jnp.exp(scores - log_total).astype(BF)
    attended = jnp.einsum("bhqk,bkhc->bqhc", probs_low, value_heads, preferred_element_type=F32)
    attended_low = attended.reshape(tokens, quarter).astype(BF)
    partial_first = dot(attended_low, proj_low).astype(BF)

    branch_first = scatter_sum(partial_first) + bias_proj
    middle = tokens_in[:chunk] + gate_first * branch_first
    normed_second, inverse_second = normed_of(middle)
    second_low = collect((normed_second * (1.0 + scale_second) + shift_second).astype(BF))

    pre_act = dot_t(second_low, up_low) + up_bias
    activated, gelu_pull = jax.vjp(gelu_tanh, pre_act)
    act_low = activated.astype(BF)
    d_branch_second = (
        tangent.reshape(per_latent) * modulation[:, 5][:, None, :]
    ).reshape(tokens, width)
    d_down_bias = jnp.sum(d_branch_second, axis=0)
    d_second_low = d_branch_second.astype(BF)
    d_act = dot_t(d_second_low, down_low)
    d_pre = gelu_pull(d_act)[0]
    d_up_bias = jnp.sum(d_pre, axis=0).reshape(-1, quarter)
    d_pre_low = d_pre.astype(BF)
    d_hidden_second = scatter_sum(dot(d_pre_low, up_low).astype(BF))

    grad_down = t_dot(act_low, d_second_low).astype(BF)
    grad_up = t_dot(d_pre_low, second_low).astype(BF)
    grad_up, grad_down = lax.psum((grad_up, grad_down), "dp")

    tangent_own = tangent[:chunk]
    d_shift_second = jnp.sum(d_hidden_second, axis=0)
    d_scale_second = jnp.sum(d_hidden_second * normed_second, axis=0)
    d_middle = tangent_own + norm_back(
        normed_second, inverse_second, d_hidden_second * (1.0 + scale_second)
    )
    d_branch_first = gate_first * d_middle
    d_gate_first = jnp.sum(d_middle * branch_first, axis=0)
    d_proj_bias = jnp.sum(d_branch_first, axis=0)
    d_first_low = collect(d_branch_first.astype(BF))

    partial_second = dot(act_low, down_low).astype(BF)
    partial_second, d_first_low = lax.optimization_barrier((partial_second, d_first_low))
    branch_second = scatter_sum(partial_second) + bias_down
    output = collect((middle + gate_second * branch_second).astype(BF))
    output = reorder(output, size, me).reshape(inputs.shape)
    d_gate_second = jnp.sum(tangent_own * branch_second, axis=0)

    grad_proj = t_dot(attended_low, d_first_low).astype(BF)
    d_attended = dot_t(d_first_low, proj_low).astype(BF).reshape(head_shape)
    probs = jnp.exp(scores - log_total)
    probs_again = probs.astype(BF)
    d_values = jnp.einsum("bhqk,bqhc->bkhc", probs_again, d_attended, preferred_element_type=F32)
    d_probs = jnp.einsum("bqhc,bkhc->bhqk", d_attended, value_heads, preferred_element_type=F32)
    d_scores = (probs * (d_probs - jnp.sum(probs * d_probs, axis=-1, keepdims=True))).astype(BF)
    d_queries = (
        jnp.einsum("bhqk,bkhc->bqhc", d_scores, key_heads, preferred_element_type=F32)
        * scale_factor
    )
    d_keys = (
        jnp.einsum("bhqk,bqhc->bkhc", d_scores, query_heads, preferred_element_type=F32)
        * scale_factor
    )
    d_queries = d_queries.reshape(tokens, quarter)
    d_keys = d_keys.reshape(tokens, quarter)
    d_values = d_values.reshape(tokens, quarter)
    d_query_bias = jnp.sum(d_queries, axis=0)
    d_value_bias = jnp.sum(d_values, axis=0)
    d_projected_low = jnp.concatenate([d_queries, d_keys, d_values], axis=1).astype(BF)
    d_hidden_first = scatter_sum(dot(d_projected_low, qkv_low).astype(BF))
    grad_qkv = t_dot(d_projected_low, first_low).astype(BF)
    grad_qkv, grad_proj, grad_up, grad_down = lax.optimization_barrier(
        (grad_qkv, grad_proj, grad_up, grad_down)
    )
    grad_qkv, grad_proj = lax.psum((grad_qkv, grad_proj), "dp")

    normed_own, inverse_own = normed_first[:chunk], inverse_first[:chunk]
    d_shift_first = jnp.sum(d_hidden_first, axis=0)
    d_scale_first = jnp.sum(d_hidden_first * normed_own, axis=0)
    grad_inputs = d_middle + norm_back(
        normed_own, inverse_own, d_hidden_first * (1.0 + scale_first)
    )
    grad_inputs = reorder(collect(grad_inputs.astype(BF)), size, me).reshape(inputs.shape)

    sums = jnp.stack(
        [
            d_shift_first,
            d_scale_first,
            d_gate_first,
            d_shift_second,
            d_scale_second,
            d_gate_second,
            d_proj_bias,
        ]
    )
    of_device = [
        lax.dynamic_slice_in_dim(sums, (me ^ mask) * quarter, quarter, 1) for mask in range(size)
    ]
    arrived = jnp.stack(
        [of_device[0]] + [swap(of_device[mask], mask) for mask in range(1, size)]
    )
    d_proj_own = jnp.sum(arrived[:, 6], axis=0)
    d_mod_own = jnp.sum(
        arrived[:, :6].reshape(latent_count, size // latent_count, 6, quarter), axis=1
    )
    d_mod_own = reorder(d_mod_own, latent_count, my_latent)
    d_cond_part = dot(d_mod_own.reshape(latent_count, -1).astype(BF), ada_low)
    d_down_own = lax.dynamic_slice_in_dim(d_down_bias, me * quarter, quarter, 0)
    small = jnp.concatenate(
        [
            d_mod_own.reshape(-1, quarter),
            d_query_bias[None],
            d_value_bias[None],
            d_proj_own[None],
            d_up_bias,
            d_down_own[None],
        ],
        axis=0,
    )
    cond_all = lax.all_gather(cond_low, "dp", axis=0, tiled=True)
    small_all = lax.all_gather(small, "dp", axis=0)
    d_mod_all = small_all[:, : 6 * latent_count].reshape(-1, 6, quarter)
    grad_biases = jnp.concatenate(
        [jnp.sum(d_mod_all, axis=0), jnp.sum(small_all[:, 6 * latent_count :], axis=0)], axis=0
    )
    d_mod_low = d_mod_all.reshape(d_mod_all.shape[0], -1).astype(BF)
    grad_ada = t_dot(d_mod_low, cond_all)

    cross = jnp.dot(
        d_mod_low.astype(F32), flat(momentum_ada), precision=lax.Precision.HIGHEST
    )
    summed = jnp.concatenate([d_cond_part, cross, dot_t(d_mod_low, d_mod_low) @ jnp.eye(d_mod_low.shape[0], width, dtype=F32)], axis=0)
    summed = sum([swap(summed, mask) for mask in range(1, size)], summed)
    d_cond_act, cross, square = (
        summed[:latent_count],
        summed[latent_count : latent_count + d_mod_low.shape[0]],
        summed[latent_count + d_mod_low.shape[0] :, : d_mod_low.shape[0]],
    )
    grad_condition = silu_pull(d_cond_act)[0]
    corr = MUON_MOMENTUM * cross + 0.5 * jnp.dot(
        square, cond_all.astype(F32), precision=lax.Precision.HIGHEST
    )
    corr = jnp.where(dp_rank == OWNERS[0], corr, 0.0)

    moments = (
        MUON_MOMENTUM * flat(momentum_ada) + grad_ada,
        MUON_MOMENTUM * flat(momentum_qkv) + grad_qkv.astype(F32),
        MUON_MOMENTUM * momentum_proj + grad_proj.astype(F32),
        MUON_MOMENTUM * flat(momentum_up) + grad_up.astype(F32),
        MUON_MOMENTUM * flat(momentum_down) + grad_down.astype(F32),
    )
    starts = tuple(m.astype(BF) for m in moments)

    block_rows = len(blocks_of(width // TILE)) * TILE
    none = jnp.zeros((block_rows, TILE), F32)
    turn = jnp.int32(0)
    for place, matrix_index in enumerate((0, 2, 3, 4)):
        turn = jnp.where(dp_rank == OWNERS[matrix_index], place + 1, turn)
    early = lax.switch(
        turn,
        [lambda *rows: none] + [(lambda *rows, k=k: gram_blocks(rows[k])) for k in range(4)],
        flat(momentum_ada),
        starts[2],
        starts[3],
        starts[4],
    )
    late = lax.cond(
        dp_rank == OWNERS[1], lambda rows: gram_blocks(rows), lambda rows: none, starts[1]
    )
    early_ranks = [OWNERS[k] for k in (0, 2, 3, 4)]
    early = collect(scatter_sum(reorder(early, size, me), early_ranks), early_ranks)
    late = collect(scatter_sum(reorder(late, size, me), OWNERS[1:2]), OWNERS[1:2])
    coefficient = jnp.where(dp_rank == OWNERS[0], MUON_MOMENTUM**2, 1.0)
    gram = reorder(jnp.where(dp_rank == OWNERS[1], late, early * coefficient), size, me)
    factor = newton_schulz_factor(gram, cond_all, corr, width)
    column_width = width // dp_size
    column_start = dp_rank * column_width
    factors = lax.all_to_all(
        factor.reshape(dp_size, column_width, width), "dp", 0, 0, tiled=True
    )

    weights_old = (w_ada, w_qkv, w_proj, w_up, w_down)
    sizes = [max(w.size // width * size, width) for w in weights_old]
    columns = [
        lax.dynamic_slice_in_dim(flat(w), column_start, column_width, 1) for w in weights_old
    ]
    new_weights = update_weights(starts, columns, factors, sizes)
    new_weights = [
        new.reshape(old.shape[:-1] + (column_width,))
        for new, old in zip(new_weights, weights_old)
    ]
    new_bias_first = BETA_ONE * bias_first + (1.0 - BETA_ONE) * grad_biases
    new_bias_second = BETA_TWO * bias_second + (1.0 - BETA_TWO) * grad_biases * grad_biases
    first_hat = new_bias_first / (1.0 - BETA_ONE**STEP)
    second_hat = new_bias_second / (1.0 - BETA_TWO**STEP)
    new_biases = biases - ADAM_RATE * first_hat / (jnp.sqrt(second_hat) + ADAM_EPS)
    return (
        output,
        grad_inputs,
        grad_condition,
        *new_weights,
        moments[0].reshape(momentum_ada.shape),
        moments[1].reshape(momentum_qkv.shape),
        moments[2],
        moments[3].reshape(momentum_up.shape),
        moments[4].reshape(momentum_down.shape),
        new_biases,
        new_bias_first,
        new_bias_second,
    )


def solution(mesh):
    placed = (
        P("dp", None, None),
        P("dp", None),
        P("dp", None, None),
        P(None, "tensor", None),
        P(None, "tensor", None),
        P("tensor", None),
        P(None, "tensor", None),
        P(None, "tensor", None),
        P(None, "tensor"),
        P(None, "tensor", None),
        P(None, "tensor", None),
        P("tensor", None),
        P(None, "tensor", None),
        P(None, "tensor", None),
        P(None, "tensor"),
        P(None, "tensor"),
    )
    return jax.shard_map(
        on_device,
        mesh=mesh,
        in_specs=placed,
        out_specs=(
            P("dp", None, None),
            P("dp", None, None),
            P("dp", None),
            P(None, "tensor", "dp"),
            P(None, "tensor", "dp"),
            P("tensor", "dp"),
            P(None, "tensor", "dp"),
            P(None, "tensor", "dp"),
            P(None, "tensor", None),
            P(None, "tensor", None),
            P("tensor", None),
            P(None, "tensor", None),
            P(None, "tensor", None),
            P(None, "tensor"),
            P(None, "tensor"),
            P(None, "tensor"),
        ),
        check_vma=False,
    )
```

```python
import functools
import math

import jax
import jax.numpy as jnp
from jax import lax
from jax.experimental import pallas as pl
from jax.experimental.pallas import tpu as pltpu
from jax.sharding import PartitionSpec as P

HEAD_DIM = 64
NS_ITERS = 5
STEP = 10


NS_A = 3.4445
NS_B = -4.775
NS_C = 2.0315
MUON_RATE = 0.16
MUON_DECAY = 0.01
MUON_MOMENTUM = 0.95
ADAM_RATE = 0.25
BETA_ONE = 0.9
BETA_TWO = 0.999
ADAM_EPS = 1e-08
NORM_EPS = 1e-06

BF = jnp.bfloat16
F32 = jnp.float32
TILE = 256
VMEM_LIMIT = 48 * 1024 * 1024
OWNERS = (0, 2, 1, 4, 6)


def dot(a, b):
    return jnp.dot(a, b, preferred_element_type=F32)


def dot_t(a, b):
    return lax.dot_general(a, b, (((1,), (1,)), ((), ())), preferred_element_type=F32)


def t_dot(a, b):
    return lax.dot_general(a, b, (((0,), (0,)), ((), ())), preferred_element_type=F32)


def parts(value):
    high = value.astype(BF)
    return high, (value - high.astype(F32)).astype(BF)


def blocks_of(count):
    return [(i, j) for i in range(count) for j in range(i, count)]


def gram_kernel(rows_ref, out_ref):
    count = rows_ref.shape[1] // TILE
    low = rows_ref[...].astype(BF)
    for k, (i, j) in enumerate(blocks_of(count)):
        out_ref[k * TILE : (k + 1) * TILE, :] = t_dot(
            low[:, i * TILE : (i + 1) * TILE], low[:, j * TILE : (j + 1) * TILE]
        )


def gram_blocks(rows):
    depth, width = rows.shape
    count = len(blocks_of(width // TILE))
    return pl.pallas_call(
        gram_kernel,
        out_shape=jax.ShapeDtypeStruct((count * TILE, TILE), F32),
        compiler_params=pltpu.CompilerParams(vmem_limit_bytes=VMEM_LIMIT),
        cost_estimate=pl.CostEstimate(
            flops=2 * depth * width * width, bytes_accessed=depth * width * 6, transcendentals=0
        ),
    )(rows)


def newton_schulz_kernel(
    blocks_ref, cond_ref, corr_ref, out_ref, cur, high, rest, poly, mid_h, mid_l, f_h, f_l, g_h, g_l
):
    width = cur.shape[0]
    spans = [slice(i * TILE, (i + 1) * TILE) for i in range(width // TILE)]
    corr = corr_ref[...]
    corr_h, corr_l = parts(corr)
    cond = cond_ref[...]
    for k, (i, j) in enumerate(blocks_of(width // TILE)):
        block = (
            blocks_ref[k * TILE : (k + 1) * TILE, :]
            + t_dot(cond[:, spans[i]], corr_h[:, spans[j]])
            + t_dot(cond[:, spans[i]], corr_l[:, spans[j]])
            + t_dot(corr_h[:, spans[i]], cond[:, spans[j]])
            + t_dot(corr_l[:, spans[i]], cond[:, spans[j]])
        )
        cur[spans[i], spans[j]] = block
        if i != j:
            cur[spans[j], spans[i]] = block.T
    square_norm = jnp.zeros((1, 1), F32)
    row = lax.broadcasted_iota(jnp.int32, (TILE, TILE), 0)
    col = lax.broadcasted_iota(jnp.int32, (TILE, TILE), 1)
    for span in spans:
        square_norm += jnp.sum(jnp.where(row == col, cur[span, span], 0.0), keepdims=True)
    scale = 1.0 / (jnp.sqrt(square_norm) + 1e-07)
    for span in spans:
        cur[span, :] = cur[span, :] * (scale * scale)

    def make_poly():
        for span in spans:
            high[span, :], rest[span, :] = parts(cur[span, :])
        for span in spans:
            poly[span, :] = (NS_B * cur[span, :] + NS_C * dot(high[span, :], high[...])).astype(BF)

    def step_gram():
        for span in spans:
            half = (
                NS_A * cur[span, :] + dot(high[span, :], poly[...]) + dot(rest[span, :], poly[...])
            )
            mid_h[span, :], mid_l[span, :] = parts(half)
        for span in spans:
            half = mid_h[span, :].astype(F32) + mid_l[span, :].astype(F32)
            cur[span, :] = (
                NS_A * half + dot(poly[span, :], mid_h[...]) + dot(poly[span, :], mid_l[...])
            )

    def stepped_factor(span):
        before = f_h[span, :].astype(F32) + f_l[span, :].astype(F32)
        return NS_A * before + dot(poly[span, :], f_h[...]) + dot(poly[span, :], f_l[...])

    make_poly()
    wide_row = lax.broadcasted_iota(jnp.int32, (TILE, width), 0)
    wide_col = lax.broadcasted_iota(jnp.int32, (TILE, width), 1)
    for i, span in enumerate(spans):
        start = poly[span, :].astype(F32) + jnp.where(wide_row + i * TILE == wide_col, NS_A, 0.0)
        f_h[span, :], f_l[span, :] = parts(start)
    step_gram()

    def middle(_, carry):
        make_poly()
        for span in spans:
            g_h[span, :], g_l[span, :] = parts(stepped_factor(span))
        f_h[...] = g_h[...]
        f_l[...] = g_l[...]
        step_gram()
        return carry

    lax.fori_loop(0, NS_ITERS - 2, middle, 0)
    make_poly()
    for span in spans:
        out_ref[span, :] = (stepped_factor(span) * scale).astype(out_ref.dtype)


def newton_schulz_factor(blocks, cond, corr, width):
    whole = lambda kind: pltpu.VMEM((width, width), kind)
    return pl.pallas_call(
        newton_schulz_kernel,
        out_shape=jax.ShapeDtypeStruct((width, width), BF),
        scratch_shapes=[whole(F32)] + [whole(BF)] * 9,
        compiler_params=pltpu.CompilerParams(vmem_limit_bytes=VMEM_LIMIT),
        cost_estimate=pl.CostEstimate(
            flops=2 * 29 * width**3, bytes_accessed=width * width * 6, transcendentals=0
        ),
    )(blocks, cond, corr)


def update_kernel(sizes, *refs):
    count = len(sizes)
    rows, weights, factor, outs = refs[:count], refs[count : 2 * count], refs[2 * count], refs[2 * count + 1 :]
    for k, size in enumerate(sizes):
        ortho = dot_t(rows[k][...], factor[OWNERS[k]])
        outs[k][...] = (
            weights[k][...] * (1.0 - MUON_RATE * MUON_DECAY)
            - MUON_RATE * 0.2 * math.sqrt(size) * ortho
        )


def update_weights(rows, weights, factors, sizes):
    return pl.pallas_call(
        functools.partial(update_kernel, sizes),
        out_shape=[jax.ShapeDtypeStruct(w.shape, F32) for w in weights],
        compiler_params=pltpu.CompilerParams(vmem_limit_bytes=VMEM_LIMIT),
        cost_estimate=pl.CostEstimate(
            flops=sum(2 * r.size * w.shape[1] for r, w in zip(rows, weights)),
            bytes_accessed=sum(2 * r.size + 12 * w.size for r, w in zip(rows, weights)),
            transcendentals=0,
        ),
    )(*rows, *weights, factors)


def attention_kernel(
    x_ref, mod_ref, w_ref, proj_ref, bias_ref, partial_ref, hidden_ref, heads_ref, attended_ref
):
    quarter = proj_ref.shape[0]
    normed, _ = normed_of(x_ref[...].astype(F32))
    hidden = (normed * (1.0 + mod_ref[0, 1:2, :]) + mod_ref[0, 0:1, :]).astype(BF)
    hidden_ref[...] = hidden
    queries = (dot_t(hidden, w_ref[:quarter, :]) + bias_ref[0:1, :]).astype(BF)
    keys = dot_t(hidden, w_ref[quarter : 2 * quarter, :]).astype(BF)
    values = (dot_t(hidden, w_ref[2 * quarter :, :]) + bias_ref[1:2, :]).astype(BF)
    heads_ref[0] = queries
    heads_ref[1] = keys
    heads_ref[2] = values
    attended = []
    for start in range(0, quarter, HEAD_DIM):
        head = slice(start, start + HEAD_DIM)
        probs = softmax_of(queries[:, head], keys[:, head]).astype(BF)
        attended.append(dot(probs, values[:, head]))
    attended = jnp.concatenate(attended, axis=1).astype(BF)
    attended_ref[...] = attended
    partial_ref[...] = dot(attended, proj_ref[...]).astype(BF)


def softmax_of(queries, keys):
    scores = dot_t(queries, keys) * (1.0 / math.sqrt(HEAD_DIM))
    raised = jnp.exp(scores - jnp.max(scores, axis=-1, keepdims=True))
    return raised * (1.0 / jnp.sum(raised, axis=-1, keepdims=True))


def attention(tokens_in, modulation, qkv_low, proj_low, bias_rows, seq_length):
    tokens, width = tokens_in.shape
    quarter = proj_low.shape[0]
    rows = lambda last: pl.BlockSpec((seq_length, last), lambda i: (i, 0))
    whole = lambda shape: pl.BlockSpec(shape, lambda i: (0,) * len(shape))
    return pl.pallas_call(
        attention_kernel,
        grid=(tokens // seq_length,),
        in_specs=[
            rows(width),
            pl.BlockSpec((1, 6, width), lambda i: (i, 0, 0)),
            whole(qkv_low.shape),
            whole(proj_low.shape),
            whole(bias_rows.shape),
        ],
        out_specs=[
            rows(width),
            rows(width),
            pl.BlockSpec((3, seq_length, quarter), lambda i: (0, i, 0)),
            rows(quarter),
        ],
        out_shape=[
            jax.ShapeDtypeStruct((tokens, width), BF),
            jax.ShapeDtypeStruct((tokens, width), BF),
            jax.ShapeDtypeStruct((3, tokens, quarter), BF),
            jax.ShapeDtypeStruct((tokens, quarter), BF),
        ],
        compiler_params=pltpu.CompilerParams(vmem_limit_bytes=VMEM_LIMIT),
        cost_estimate=pl.CostEstimate(
            flops=8 * tokens * width * quarter + 4 * tokens * seq_length * quarter,
            bytes_accessed=tokens * width * 8 + qkv_low.size * 3,
            transcendentals=tokens * seq_length * quarter // HEAD_DIM,
        ),
    )(tokens_in, modulation, qkv_low, proj_low, bias_rows)


def attention_back_kernel(grad_ref, heads_ref, w_ref, proj_ref, d_heads_ref, part_ref, sums_ref):
    quarter = proj_ref.shape[0]
    scale = 1.0 / math.sqrt(HEAD_DIM)
    d_attended = dot_t(grad_ref[...], proj_ref[...]).astype(BF)
    queries, keys, values = heads_ref[0], heads_ref[1], heads_ref[2]
    d_queries, d_keys, d_values = [], [], []
    for start in range(0, quarter, HEAD_DIM):
        head = slice(start, start + HEAD_DIM)
        probs = softmax_of(queries[:, head], keys[:, head])
        d_out = d_attended[:, head]
        d_values.append(t_dot(probs.astype(BF), d_out))
        d_probs = dot_t(d_out, values[:, head])
        d_scores = (
            probs * (d_probs - jnp.sum(probs * d_probs, axis=-1, keepdims=True))
        ).astype(BF)
        d_queries.append(dot(d_scores, keys[:, head]) * scale)
        d_keys.append(t_dot(d_scores, queries[:, head]) * scale)
    d_queries = jnp.concatenate(d_queries, axis=1)
    d_values = jnp.concatenate(d_values, axis=1)
    sums_ref[0, 0:1, :] = jnp.sum(d_queries, axis=0, keepdims=True)
    sums_ref[0, 1:2, :] = jnp.sum(d_values, axis=0, keepdims=True)
    d_queries = d_queries.astype(BF)
    d_keys = jnp.concatenate(d_keys, axis=1).astype(BF)
    d_values = d_values.astype(BF)
    d_heads_ref[0] = d_queries
    d_heads_ref[1] = d_keys
    d_heads_ref[2] = d_values
    part_ref[...] = (
        dot(d_queries, w_ref[:quarter, :])
        + dot(d_keys, w_ref[quarter : 2 * quarter, :])
        + dot(d_values, w_ref[2 * quarter :, :])
    ).astype(BF)


def attention_back(grad, heads, qkv_low, proj_low, seq_length):
    tokens, width = grad.shape
    quarter = proj_low.shape[0]
    rows = lambda last: pl.BlockSpec((seq_length, last), lambda i: (i, 0))
    whole = lambda shape: pl.BlockSpec(shape, lambda i: (0,) * len(shape))
    of_heads = pl.BlockSpec((3, seq_length, quarter), lambda i: (0, i, 0))
    return pl.pallas_call(
        attention_back_kernel,
        grid=(tokens // seq_length,),
        in_specs=[rows(width), of_heads, whole(qkv_low.shape), whole(proj_low.shape)],
        out_specs=[
            of_heads,
            rows(width),
            pl.BlockSpec((1, 2, quarter), lambda i: (i, 0, 0)),
        ],
        out_shape=[
            jax.ShapeDtypeStruct(heads.shape, BF),
            jax.ShapeDtypeStruct((tokens, width), BF),
            jax.ShapeDtypeStruct((tokens // seq_length, 2, quarter), F32),
        ],
        compiler_params=pltpu.CompilerParams(vmem_limit_bytes=VMEM_LIMIT),
        cost_estimate=pl.CostEstimate(
            flops=8 * tokens * width * quarter + 10 * tokens * seq_length * quarter,
            bytes_accessed=tokens * width * 8 + qkv_low.size * 3,
            transcendentals=tokens * seq_length * quarter // HEAD_DIM,
        ),
    )(grad, heads, qkv_low, proj_low)


def feed_forward_kernel(
    hidden_ref, grad_ref, up_ref, down_ref, bias_ref, act_ref, d_pre_ref, part_ref, sums_ref
):
    pre = dot_t(hidden_ref[...], up_ref[...]) + bias_ref[...]
    d_act = dot_t(grad_ref[...], down_ref[...])
    root = math.sqrt(2.0 / math.pi)
    square = pre * pre
    bent = jnp.tanh(root * pre * (1.0 + 0.044715 * square))
    half = 0.5 * (1.0 + bent)
    act_ref[...] = (pre * half).astype(BF)
    slope = half + 0.5 * pre * (1.0 - bent * bent) * (root * (1.0 + 0.134145 * square))
    d_pre = d_act * slope

    @pl.when(pl.program_id(0) == 0)
    def _():
        sums_ref[...] = jnp.zeros_like(sums_ref)

    sums_ref[...] += jnp.sum(d_pre, axis=0, keepdims=True)
    d_pre = d_pre.astype(BF)
    d_pre_ref[...] = d_pre
    part_ref[...] = dot(d_pre, up_ref[...]).astype(BF)


def feed_forward(hidden, grad, up_low, down_low, bias):
    tokens, width = hidden.shape
    units = up_low.shape[0]
    block = tokens // 2
    rows = lambda last: pl.BlockSpec((block, last), lambda i: (i, 0))
    whole = lambda shape: pl.BlockSpec(shape, lambda i: (0,) * len(shape))
    return pl.pallas_call(
        feed_forward_kernel,
        grid=(tokens // block,),
        in_specs=[
            rows(width),
            rows(width),
            whole(up_low.shape),
            whole(down_low.shape),
            whole((1, units)),
        ],
        out_specs=[rows(units), rows(units), rows(width), whole((1, units))],
        out_shape=[
            jax.ShapeDtypeStruct((tokens, units), BF),
            jax.ShapeDtypeStruct((tokens, units), BF),
            jax.ShapeDtypeStruct((tokens, width), BF),
            jax.ShapeDtypeStruct((1, units), F32),
        ],
        compiler_params=pltpu.CompilerParams(vmem_limit_bytes=VMEM_LIMIT),
        cost_estimate=pl.CostEstimate(
            flops=6 * tokens * width * units,
            bytes_accessed=tokens * width * 10 + up_low.size * 4,
            transcendentals=tokens * units,
        ),
    )(hidden, grad, up_low, down_low, bias)


def dp_swap(piece, mask):
    return lax.ppermute(piece, "dp", [(i, i ^ mask) for i in range(lax.axis_size("dp"))])


def dp_levels():
    size, step, levels = lax.axis_size("dp"), 2, []
    while step < size:
        radix = min(4, size // step)
        levels.append((step, radix))
        step *= radix
    return levels + [(1, 2)]


def dp_masks():
    masks = [0]
    for step, radix in dp_levels():
        masks = [j * step + mask for j in range(radix) for mask in masks]
    return masks


def dp_collect(piece):
    gathered = piece[None]
    for step, radix in dp_levels():
        gathered = jnp.concatenate(
            [gathered] + [dp_swap(gathered, j * step) for j in range(1, radix)], axis=0
        )
    return gathered


def dp_scatter_sum(value):
    for step, radix in reversed(dp_levels()):
        value = value.reshape((radix, -1) + value.shape[1:])
        total = value[0].astype(F32)
        for j in range(1, radix):
            total = total + dp_swap(value[j], j * step).astype(F32)
        value = total.astype(BF)
    return value[0]


def dp_sum(value):
    size, rank, masks = lax.axis_size("dp"), lax.axis_index("dp"), dp_masks()
    value = reorder(value, masks, rank)
    piece = dp_scatter_sum(value.reshape((size, -1) + value.shape[1:]))
    places = [masks.index(p) for p in range(size)]
    gathered = dp_collect(piece)
    table = jnp.asarray(places, jnp.int32)
    blocks = [
        lax.dynamic_index_in_dim(gathered, table[rank ^ p], 0, False) for p in range(size)
    ]
    return jnp.concatenate(blocks, axis=0)


def swap(piece, mask, ranks=None):
    size = lax.axis_size("tensor")
    if ranks is None:
        return lax.ppermute(piece, "tensor", [(i, i ^ mask) for i in range(size)])
    pairs = [(r * size + i, r * size + (i ^ mask)) for r in ranks for i in range(size)]
    return lax.ppermute(piece, ("dp", "tensor"), pairs)


def scatter_sum(value, ranks=None):
    size = lax.axis_size("tensor")
    rows = value.shape[0] // size
    total = value[:rows].astype(F32)
    for mask in range(1, size):
        total = total + swap(value[mask * rows : (mask + 1) * rows], mask, ranks).astype(F32)
    return total


def collect(piece, ranks=None):
    size = lax.axis_size("tensor")
    return jnp.concatenate([piece] + [swap(piece, mask, ranks) for mask in range(1, size)], axis=0)


def reorder(value, masks, index):
    masks = list(range(masks)) if isinstance(masks, int) else masks
    rows = value.shape[0] // len(masks)
    return jnp.concatenate(
        [lax.dynamic_slice_in_dim(value, (index ^ p) * rows, rows, 0) for p in masks], axis=0
    )


def normed_of(values):
    average = jnp.mean(values, axis=-1, keepdims=True)
    centered = values - average
    variance = jnp.mean(centered * centered, axis=-1, keepdims=True)
    inverse = lax.rsqrt(variance + NORM_EPS)
    return centered * inverse, inverse


def norm_back(normed, inverse, grad):
    return (
        grad
        - jnp.mean(grad, axis=-1, keepdims=True)
        - normed * jnp.mean(grad * normed, axis=-1, keepdims=True)
    ) * inverse


def on_device(
    inputs,
    condition,
    cotangent,
    w_ada,
    w_qkv,
    w_proj,
    w_up,
    w_down,
    biases,
    momentum_ada,
    momentum_qkv,
    momentum_proj,
    momentum_up,
    momentum_down,
    bias_first,
    bias_second,
):
    quarter = w_ada.shape[1]
    width = w_ada.shape[-1]
    latent_count = inputs.shape[0]
    seq_length = inputs.shape[1]
    tokens = latent_count * seq_length
    heads_here = quarter // HEAD_DIM
    size = lax.axis_size("tensor")
    me = lax.axis_index("tensor")
    dp_size = lax.axis_size("dp")
    dp_rank = lax.axis_index("dp")
    chunk = tokens // size
    my_latent = me // (size // latent_count)
    scale_factor = 1.0 / math.sqrt(HEAD_DIM)
    flat = lambda w: w.reshape(-1, width)
    ada_low = flat(w_ada).astype(BF)
    qkv_low = flat(w_qkv).astype(BF)
    proj_low = w_proj.astype(BF)
    up_low = flat(w_up).astype(BF)
    down_low = flat(w_down).astype(BF)
    up_bias = biases[9:13].reshape(-1)

    cond_act, silu_pull = jax.vjp(jax.nn.silu, condition.astype(F32))
    cond_low = cond_act.astype(BF)
    mod_part = dot_t(cond_low, ada_low).reshape(latent_count * 6, quarter) + jnp.tile(
        biases[0:6], (latent_count, 1)
    )
    mod_part = jnp.concatenate([mod_part, biases[8:9], biases[13:14]], axis=0)
    gathered = collect(mod_part[None])
    gathered = reorder(gathered, size, me)
    gathered = jnp.moveaxis(gathered, 0, 1).reshape(-1, width)
    modulation = reorder(gathered[: latent_count * 6], latent_count, my_latent).reshape(
        latent_count, 6, width
    )
    bias_proj = gathered[latent_count * 6]
    bias_down = gathered[latent_count * 6 + 1]
    shift_first, scale_first, gate_first = modulation[0, 0], modulation[0, 1], modulation[0, 2]
    shift_second, scale_second, gate_second = modulation[0, 3], modulation[0, 4], modulation[0, 5]

    tokens_in = reorder(inputs.reshape(tokens, width), size, me)
    tangent = reorder(cotangent.reshape(tokens, width), size, me)
    partial_first, first_low, heads, attended_low = attention(
        tokens_in, modulation, qkv_low, proj_low, biases[6:8], seq_length
    )
    own = tokens_in[:chunk].astype(F32)
    tangent_own = tangent[:chunk].astype(F32)

    branch_first = scatter_sum(partial_first) + bias_proj
    middle = own + gate_first * branch_first
    normed_second, inverse_second = normed_of(middle)
    second_low = collect((normed_second * (1.0 + scale_second) + shift_second).astype(BF))

    d_branch_second = (
        tangent.astype(F32).reshape(latent_count, seq_length, width)
        * modulation[:, 5][:, None, :]
    ).reshape(tokens, width)
    d_down_bias = jnp.sum(d_branch_second, axis=0)
    d_second_low = d_branch_second.astype(BF)
    act_low, d_pre_low, second_part, d_up_bias = feed_forward(
        second_low, d_second_low, up_low, down_low, up_bias[None]
    )
    d_up_bias = d_up_bias.reshape(-1, quarter)
    d_hidden_second = scatter_sum(second_part)

    grad_down = t_dot(act_low, d_second_low).astype(BF)
    grad_up = t_dot(d_pre_low, second_low).astype(BF)
    grad_up, grad_down = lax.psum((grad_up, grad_down), "dp")

    d_shift_second = jnp.sum(d_hidden_second, axis=0)
    d_scale_second = jnp.sum(d_hidden_second * normed_second, axis=0)
    d_middle = tangent_own + norm_back(
        normed_second, inverse_second, d_hidden_second * (1.0 + scale_second)
    )
    d_branch_first = gate_first * d_middle
    d_gate_first = jnp.sum(d_middle * branch_first, axis=0)
    d_proj_bias = jnp.sum(d_branch_first, axis=0)
    d_first_low = collect(d_branch_first.astype(BF))

    partial_second = dot(act_low, down_low).astype(BF)
    partial_second, d_first_low = lax.optimization_barrier((partial_second, d_first_low))
    branch_second = scatter_sum(partial_second) + bias_down
    output = collect((middle + gate_second * branch_second).astype(BF))
    output = reorder(output, size, me).reshape(inputs.shape)
    d_gate_second = jnp.sum(tangent_own * branch_second, axis=0)

    grad_proj = t_dot(attended_low, d_first_low).astype(BF)
    d_heads, first_part, d_head_sums = attention_back(
        d_first_low, heads, qkv_low, proj_low, seq_length
    )
    d_head_bias = jnp.sum(d_head_sums, axis=0)
    grad_qkv = jnp.concatenate([t_dot(d_heads[k], first_low) for k in range(3)], axis=0).astype(BF)
    late_grads = dp_sum(jnp.concatenate([grad_qkv, grad_proj], axis=0))
    grad_qkv, grad_proj = late_grads[: 3 * quarter], late_grads[3 * quarter :]
    d_hidden_first = scatter_sum(first_part)

    normed_own, inverse_own = normed_of(own)
    d_shift_first = jnp.sum(d_hidden_first, axis=0)
    d_scale_first = jnp.sum(d_hidden_first * normed_own, axis=0)
    grad_inputs = d_middle + norm_back(
        normed_own, inverse_own, d_hidden_first * (1.0 + scale_first)
    )
    grad_inputs = reorder(collect(grad_inputs.astype(BF)), size, me).reshape(inputs.shape)

    sums = jnp.stack(
        [
            d_shift_first,
            d_scale_first,
            d_gate_first,
            d_shift_second,
            d_scale_second,
            d_gate_second,
            d_proj_bias,
        ]
    )
    of_device = [
        lax.dynamic_slice_in_dim(sums, (me ^ mask) * quarter, quarter, 1) for mask in range(size)
    ]
    arrived = jnp.stack(
        [of_device[0]] + [swap(of_device[mask], mask) for mask in range(1, size)]
    )
    d_proj_own = jnp.sum(arrived[:, 6], axis=0)
    d_mod_own = jnp.sum(
        arrived[:, :6].reshape(latent_count, size // latent_count, 6, quarter), axis=1
    )
    d_mod_own = reorder(d_mod_own, latent_count, my_latent)
    d_cond_part = dot(d_mod_own.reshape(latent_count, -1).astype(BF), ada_low)
    d_down_own = lax.dynamic_slice_in_dim(d_down_bias, me * quarter, quarter, 0)
    small = jnp.concatenate(
        [
            d_mod_own.reshape(-1, quarter),
            d_head_bias,
            d_proj_own[None],
            d_up_bias,
            d_down_own[None],
        ],
        axis=0,
    )
    cond_all = dp_collect(cond_low).reshape(-1, width)
    small_all = dp_collect(small)
    d_mod_all = small_all[:, : 6 * latent_count].reshape(-1, 6, quarter)
    grad_biases = jnp.concatenate(
        [jnp.sum(d_mod_all, axis=0), jnp.sum(small_all[:, 6 * latent_count :], axis=0)], axis=0
    )
    d_mod_low = d_mod_all.reshape(d_mod_all.shape[0], -1).astype(BF)
    grad_ada = t_dot(d_mod_low, cond_all)

    cross = jnp.dot(
        d_mod_low.astype(F32), flat(momentum_ada), precision=lax.Precision.HIGHEST
    )
    summed = jnp.concatenate([d_cond_part, cross, dot_t(d_mod_low, d_mod_low) @ jnp.eye(d_mod_low.shape[0], width, dtype=F32)], axis=0)
    summed = sum([swap(summed, mask) for mask in range(1, size)], summed)
    d_cond_act, cross, square = (
        summed[:latent_count],
        summed[latent_count : latent_count + d_mod_low.shape[0]],
        summed[latent_count + d_mod_low.shape[0] :, : d_mod_low.shape[0]],
    )
    grad_condition = silu_pull(d_cond_act)[0]
    corr = MUON_MOMENTUM * cross + 0.5 * jnp.dot(
        square, cond_all.astype(F32), precision=lax.Precision.HIGHEST
    )
    corr = jnp.where(dp_rank == OWNERS[0], corr, 0.0)

    moments = (
        MUON_MOMENTUM * flat(momentum_ada) + grad_ada,
        MUON_MOMENTUM * flat(momentum_qkv) + grad_qkv.astype(F32),
        MUON_MOMENTUM * momentum_proj + grad_proj.astype(F32),
        MUON_MOMENTUM * flat(momentum_up) + grad_up.astype(F32),
        MUON_MOMENTUM * flat(momentum_down) + grad_down.astype(F32),
    )
    starts = tuple(m.astype(BF) for m in moments)

    block_rows = len(blocks_of(width // TILE)) * TILE
    none = jnp.zeros((block_rows, TILE), F32)
    turn = jnp.int32(0)
    for place, matrix_index in enumerate((0, 3, 4)):
        turn = jnp.where(dp_rank == OWNERS[matrix_index], place + 1, turn)
    early = lax.switch(
        turn,
        [lambda *rows: none] + [(lambda *rows, k=k: gram_blocks(rows[k])) for k in range(3)],
        flat(momentum_ada),
        starts[3],
        starts[4],
    )
    turn = jnp.where(dp_rank == OWNERS[1], 1, jnp.where(dp_rank == OWNERS[2], 2, 0))
    late = lax.switch(
        turn,
        [lambda *rows: none] + [(lambda *rows, k=k: gram_blocks(rows[k])) for k in range(2)],
        starts[1],
        starts[2],
    )
    early_ranks = [OWNERS[k] for k in (0, 3, 4)]
    late_ranks = [OWNERS[k] for k in (1, 2)]
    early = collect(scatter_sum(reorder(early, size, me), early_ranks), early_ranks)
    late = collect(scatter_sum(reorder(late, size, me), late_ranks), late_ranks)
    coefficient = jnp.where(dp_rank == OWNERS[0], MUON_MOMENTUM**2, 1.0)
    is_late = (dp_rank == OWNERS[1]) | (dp_rank == OWNERS[2])
    gram = reorder(jnp.where(is_late, late, early * coefficient), size, me)
    factor = newton_schulz_factor(gram, cond_all, corr, width)
    column_width = width // dp_size
    column_start = dp_rank * column_width
    factors = lax.all_to_all(
        factor.reshape(dp_size, column_width, width), "dp", 0, 0, tiled=True
    )

    weights_old = (w_ada, w_qkv, w_proj, w_up, w_down)
    sizes = [max(w.size // width * size, width) for w in weights_old]
    columns = [
        lax.dynamic_slice_in_dim(flat(w), column_start, column_width, 1) for w in weights_old
    ]
    new_weights = update_weights(starts, columns, factors, sizes)
    new_weights = [
        new.reshape(old.shape[:-1] + (column_width,))
        for new, old in zip(new_weights, weights_old)
    ]
    new_bias_first = BETA_ONE * bias_first + (1.0 - BETA_ONE) * grad_biases
    new_bias_second = BETA_TWO * bias_second + (1.0 - BETA_TWO) * grad_biases * grad_biases
    first_hat = new_bias_first / (1.0 - BETA_ONE**STEP)
    second_hat = new_bias_second / (1.0 - BETA_TWO**STEP)
    new_biases = biases - ADAM_RATE * first_hat / (jnp.sqrt(second_hat) + ADAM_EPS)
    return (
        output,
        grad_inputs,
        grad_condition,
        *new_weights,
        moments[0].reshape(momentum_ada.shape),
        moments[1].reshape(momentum_qkv.shape),
        moments[2],
        moments[3].reshape(momentum_up.shape),
        moments[4].reshape(momentum_down.shape),
        new_biases,
        new_bias_first,
        new_bias_second,
    )


def solution(mesh):
    placed = (
        P("dp", None, None),
        P("dp", None),
        P("dp", None, None),
        P(None, "tensor", None),
        P(None, "tensor", None),
        P("tensor", None),
        P(None, "tensor", None),
        P(None, "tensor", None),
        P(None, "tensor"),
        P(None, "tensor", None),
        P(None, "tensor", None),
        P("tensor", None),
        P(None, "tensor", None),
        P(None, "tensor", None),
        P(None, "tensor"),
        P(None, "tensor"),
    )
    return jax.shard_map(
        on_device,
        mesh=mesh,
        in_specs=placed,
        out_specs=(
            P("dp", None, None),
            P("dp", None, None),
            P("dp", None),
            P(None, "tensor", "dp"),
            P(None, "tensor", "dp"),
            P("tensor", "dp"),
            P(None, "tensor", "dp"),
            P(None, "tensor", "dp"),
            P(None, "tensor", None),
            P(None, "tensor", None),
            P("tensor", None),
            P(None, "tensor", None),
            P(None, "tensor", None),
            P(None, "tensor"),
            P(None, "tensor"),
            P(None, "tensor"),
        ),
        check_vma=False,
    )
```

```python
import functools
import math

import jax
import jax.numpy as jnp
from jax import lax
from jax.experimental import pallas as pl
from jax.experimental.pallas import tpu as pltpu
from jax.sharding import PartitionSpec as P

HEAD_DIM = 64
NS_ITERS = 5
STEP = 10


NS_A = 3.4445
NS_B = -4.775
NS_C = 2.0315
MUON_RATE = 0.16
MUON_DECAY = 0.01
MUON_MOMENTUM = 0.95
ADAM_RATE = 0.25
BETA_ONE = 0.9
BETA_TWO = 0.999
ADAM_EPS = 1e-08
NORM_EPS = 1e-06

BF = jnp.bfloat16
F32 = jnp.float32
TILE = 256
VMEM_LIMIT = 28 * 1024 * 1024
OWNERS = (0, 2, 1, 4, 6)


def dot(a, b):
    return jnp.dot(a, b, preferred_element_type=F32)


def dot_t(a, b):
    return lax.dot_general(a, b, (((1,), (1,)), ((), ())), preferred_element_type=F32)


def t_dot(a, b):
    return lax.dot_general(a, b, (((0,), (0,)), ((), ())), preferred_element_type=F32)


def parts(value):
    high = value.astype(BF)
    return high, (value - high.astype(F32)).astype(BF)


def blocks_of(count):
    return [(i, j) for i in range(count) for j in range(i, count)]


def gram_kernel(rows_ref, out_ref):
    count = rows_ref.shape[1] // TILE
    low = rows_ref[...].astype(BF)
    for k, (i, j) in enumerate(blocks_of(count)):
        out_ref[k * TILE : (k + 1) * TILE, :] = t_dot(
            low[:, i * TILE : (i + 1) * TILE], low[:, j * TILE : (j + 1) * TILE]
        )


def gram_blocks(rows):
    depth, width = rows.shape
    count = len(blocks_of(width // TILE))
    return pl.pallas_call(
        gram_kernel,
        out_shape=jax.ShapeDtypeStruct((count * TILE, TILE), F32),
        compiler_params=pltpu.CompilerParams(vmem_limit_bytes=VMEM_LIMIT),
        cost_estimate=pl.CostEstimate(
            flops=2 * depth * width * width, bytes_accessed=depth * width * 6, transcendentals=0
        ),
    )(rows)


def newton_schulz_kernel(
    blocks_ref, cond_ref, corr_ref, out_ref, cur, high, rest, poly, mid_h, mid_l, f_h, f_l, g_h, g_l
):
    width = cur.shape[0]
    spans = [slice(i * TILE, (i + 1) * TILE) for i in range(width // TILE)]
    corr = corr_ref[...]
    corr_h, corr_l = parts(corr)
    cond = cond_ref[...]
    for k, (i, j) in enumerate(blocks_of(width // TILE)):
        block = (
            blocks_ref[k * TILE : (k + 1) * TILE, :]
            + t_dot(cond[:, spans[i]], corr_h[:, spans[j]])
            + t_dot(cond[:, spans[i]], corr_l[:, spans[j]])
            + t_dot(corr_h[:, spans[i]], cond[:, spans[j]])
            + t_dot(corr_l[:, spans[i]], cond[:, spans[j]])
        )
        cur[spans[i], spans[j]] = block
        if i != j:
            cur[spans[j], spans[i]] = block.T
    square_norm = jnp.zeros((1, 1), F32)
    row = lax.broadcasted_iota(jnp.int32, (TILE, TILE), 0)
    col = lax.broadcasted_iota(jnp.int32, (TILE, TILE), 1)
    for span in spans:
        square_norm += jnp.sum(jnp.where(row == col, cur[span, span], 0.0), keepdims=True)
    scale = 1.0 / (jnp.sqrt(square_norm) + 1e-07)
    for span in spans:
        cur[span, :] = cur[span, :] * (scale * scale)

    def make_poly():
        for span in spans:
            high[span, :], rest[span, :] = parts(cur[span, :])
        for span in spans:
            poly[span, :] = (NS_B * cur[span, :] + NS_C * dot(high[span, :], high[...])).astype(BF)

    def step_gram():
        for span in spans:
            half = (
                NS_A * cur[span, :] + dot(high[span, :], poly[...]) + dot(rest[span, :], poly[...])
            )
            mid_h[span, :], mid_l[span, :] = parts(half)
        for span in spans:
            half = mid_h[span, :].astype(F32) + mid_l[span, :].astype(F32)
            cur[span, :] = (
                NS_A * half + dot(poly[span, :], mid_h[...]) + dot(poly[span, :], mid_l[...])
            )

    def stepped_factor(span):
        before = f_h[span, :].astype(F32) + f_l[span, :].astype(F32)
        return NS_A * before + dot(poly[span, :], f_h[...]) + dot(poly[span, :], f_l[...])

    make_poly()
    wide_row = lax.broadcasted_iota(jnp.int32, (TILE, width), 0)
    wide_col = lax.broadcasted_iota(jnp.int32, (TILE, width), 1)
    for i, span in enumerate(spans):
        start = poly[span, :].astype(F32) + jnp.where(wide_row + i * TILE == wide_col, NS_A, 0.0)
        f_h[span, :], f_l[span, :] = parts(start)
    step_gram()

    def middle(_, carry):
        make_poly()
        for span in spans:
            g_h[span, :], g_l[span, :] = parts(stepped_factor(span))
        f_h[...] = g_h[...]
        f_l[...] = g_l[...]
        step_gram()
        return carry

    lax.fori_loop(0, NS_ITERS - 2, middle, 0)
    make_poly()
    for span in spans:
        out_ref[span, :] = (stepped_factor(span) * scale).astype(out_ref.dtype)


def newton_schulz_factor(blocks, cond, corr, width):
    whole = lambda kind: pltpu.VMEM((width, width), kind)
    return pl.pallas_call(
        newton_schulz_kernel,
        out_shape=jax.ShapeDtypeStruct((width, width), BF),
        scratch_shapes=[whole(F32)] + [whole(BF)] * 9,
        compiler_params=pltpu.CompilerParams(vmem_limit_bytes=VMEM_LIMIT),
        cost_estimate=pl.CostEstimate(
            flops=2 * 29 * width**3, bytes_accessed=width * width * 6, transcendentals=0
        ),
    )(blocks, cond, corr)


def update_kernel(sizes, *refs):
    count = len(sizes)
    rows, weights, factor, outs = refs[:count], refs[count : 2 * count], refs[2 * count], refs[2 * count + 1 :]
    for k, size in enumerate(sizes):
        ortho = dot_t(rows[k][...], factor[OWNERS[k]])
        outs[k][...] = (
            weights[k][...] * (1.0 - MUON_RATE * MUON_DECAY)
            - MUON_RATE * 0.2 * math.sqrt(size) * ortho
        )


def update_weights(rows, weights, factors, sizes):
    return pl.pallas_call(
        functools.partial(update_kernel, sizes),
        out_shape=[jax.ShapeDtypeStruct(w.shape, F32) for w in weights],
        compiler_params=pltpu.CompilerParams(vmem_limit_bytes=VMEM_LIMIT),
        cost_estimate=pl.CostEstimate(
            flops=sum(2 * r.size * w.shape[1] for r, w in zip(rows, weights)),
            bytes_accessed=sum(2 * r.size + 12 * w.size for r, w in zip(rows, weights)),
            transcendentals=0,
        ),
    )(*rows, *weights, factors)


def attention_kernel(
    x_ref, mod_ref, w_ref, proj_ref, bias_ref, partial_ref, hidden_ref, heads_ref, attended_ref
):
    quarter = proj_ref.shape[0]
    normed, _ = normed_of(x_ref[...].astype(F32))
    hidden = (normed * (1.0 + mod_ref[0, 1:2, :]) + mod_ref[0, 0:1, :]).astype(BF)
    hidden_ref[...] = hidden
    queries = (dot_t(hidden, w_ref[:quarter, :]) + bias_ref[0:1, :]).astype(BF)
    keys = dot_t(hidden, w_ref[quarter : 2 * quarter, :]).astype(BF)
    values = (dot_t(hidden, w_ref[2 * quarter :, :]) + bias_ref[1:2, :]).astype(BF)
    heads_ref[0] = queries
    heads_ref[1] = keys
    heads_ref[2] = values
    attended = []
    for start in range(0, quarter, HEAD_DIM):
        head = slice(start, start + HEAD_DIM)
        probs = softmax_of(queries[:, head], keys[:, head]).astype(BF)
        attended.append(dot(probs, values[:, head]))
    attended = jnp.concatenate(attended, axis=1).astype(BF)
    attended_ref[...] = attended
    partial_ref[...] = dot(attended, proj_ref[...]).astype(BF)


def softmax_of(queries, keys):
    scores = dot_t(queries, keys) * (1.0 / math.sqrt(HEAD_DIM))
    raised = jnp.exp(scores - jnp.max(scores, axis=-1, keepdims=True))
    return raised * (1.0 / jnp.sum(raised, axis=-1, keepdims=True))


def attention(tokens_in, modulation, qkv_low, proj_low, bias_rows, seq_length):
    tokens, width = tokens_in.shape
    quarter = proj_low.shape[0]
    rows = lambda last: pl.BlockSpec((seq_length, last), lambda i: (i, 0))
    whole = lambda shape: pl.BlockSpec(shape, lambda i: (0,) * len(shape))
    return pl.pallas_call(
        attention_kernel,
        grid=(tokens // seq_length,),
        in_specs=[
            rows(width),
            pl.BlockSpec((1, 6, width), lambda i: (i, 0, 0)),
            whole(qkv_low.shape),
            whole(proj_low.shape),
            whole(bias_rows.shape),
        ],
        out_specs=[
            rows(width),
            rows(width),
            pl.BlockSpec((3, seq_length, quarter), lambda i: (0, i, 0)),
            rows(quarter),
        ],
        out_shape=[
            jax.ShapeDtypeStruct((tokens, width), BF),
            jax.ShapeDtypeStruct((tokens, width), BF),
            jax.ShapeDtypeStruct((3, tokens, quarter), BF),
            jax.ShapeDtypeStruct((tokens, quarter), BF),
        ],
        compiler_params=pltpu.CompilerParams(vmem_limit_bytes=VMEM_LIMIT),
        cost_estimate=pl.CostEstimate(
            flops=8 * tokens * width * quarter + 4 * tokens * seq_length * quarter,
            bytes_accessed=tokens * width * 8 + qkv_low.size * 3,
            transcendentals=tokens * seq_length * quarter // HEAD_DIM,
        ),
    )(tokens_in, modulation, qkv_low, proj_low, bias_rows)


def attention_back_kernel(grad_ref, heads_ref, w_ref, proj_ref, d_heads_ref, part_ref, sums_ref):
    quarter = proj_ref.shape[0]
    scale = 1.0 / math.sqrt(HEAD_DIM)
    d_attended = dot_t(grad_ref[...], proj_ref[...]).astype(BF)
    queries, keys, values = heads_ref[0], heads_ref[1], heads_ref[2]
    d_queries, d_keys, d_values = [], [], []
    for start in range(0, quarter, HEAD_DIM):
        head = slice(start, start + HEAD_DIM)
        probs = softmax_of(queries[:, head], keys[:, head])
        d_out = d_attended[:, head]
        d_values.append(t_dot(probs.astype(BF), d_out))
        d_probs = dot_t(d_out, values[:, head])
        d_scores = (
            probs * (d_probs - jnp.sum(probs * d_probs, axis=-1, keepdims=True))
        ).astype(BF)
        d_queries.append(dot(d_scores, keys[:, head]) * scale)
        d_keys.append(t_dot(d_scores, queries[:, head]) * scale)
    d_queries = jnp.concatenate(d_queries, axis=1)
    d_values = jnp.concatenate(d_values, axis=1)
    sums_ref[0, 0:1, :] = jnp.sum(d_queries, axis=0, keepdims=True)
    sums_ref[0, 1:2, :] = jnp.sum(d_values, axis=0, keepdims=True)
    d_queries = d_queries.astype(BF)
    d_keys = jnp.concatenate(d_keys, axis=1).astype(BF)
    d_values = d_values.astype(BF)
    d_heads_ref[0] = d_queries
    d_heads_ref[1] = d_keys
    d_heads_ref[2] = d_values
    part_ref[...] = (
        dot(d_queries, w_ref[:quarter, :])
        + dot(d_keys, w_ref[quarter : 2 * quarter, :])
        + dot(d_values, w_ref[2 * quarter :, :])
    ).astype(BF)


def attention_back(grad, heads, qkv_low, proj_low, seq_length):
    tokens, width = grad.shape
    quarter = proj_low.shape[0]
    rows = lambda last: pl.BlockSpec((seq_length, last), lambda i: (i, 0))
    whole = lambda shape: pl.BlockSpec(shape, lambda i: (0,) * len(shape))
    of_heads = pl.BlockSpec((3, seq_length, quarter), lambda i: (0, i, 0))
    return pl.pallas_call(
        attention_back_kernel,
        grid=(tokens // seq_length,),
        in_specs=[rows(width), of_heads, whole(qkv_low.shape), whole(proj_low.shape)],
        out_specs=[
            of_heads,
            rows(width),
            pl.BlockSpec((1, 2, quarter), lambda i: (i, 0, 0)),
        ],
        out_shape=[
            jax.ShapeDtypeStruct(heads.shape, BF),
            jax.ShapeDtypeStruct((tokens, width), BF),
            jax.ShapeDtypeStruct((tokens // seq_length, 2, quarter), F32),
        ],
        compiler_params=pltpu.CompilerParams(vmem_limit_bytes=VMEM_LIMIT),
        cost_estimate=pl.CostEstimate(
            flops=8 * tokens * width * quarter + 10 * tokens * seq_length * quarter,
            bytes_accessed=tokens * width * 8 + qkv_low.size * 3,
            transcendentals=tokens * seq_length * quarter // HEAD_DIM,
        ),
    )(grad, heads, qkv_low, proj_low)


def feed_forward_kernel(
    hidden_ref, grad_ref, up_ref, down_ref, bias_ref, act_ref, d_pre_ref, part_ref, sums_ref
):
    pre = dot_t(hidden_ref[...], up_ref[...]) + bias_ref[...]
    d_act = dot_t(grad_ref[...], down_ref[...])
    root = math.sqrt(2.0 / math.pi)
    square = pre * pre
    bent = jnp.tanh(root * pre * (1.0 + 0.044715 * square))
    half = 0.5 * (1.0 + bent)
    act_ref[...] = (pre * half).astype(BF)
    slope = half + 0.5 * pre * (1.0 - bent * bent) * (root * (1.0 + 0.134145 * square))
    d_pre = d_act * slope

    @pl.when(pl.program_id(0) == 0)
    def _():
        sums_ref[...] = jnp.zeros_like(sums_ref)

    sums_ref[...] += jnp.sum(d_pre, axis=0, keepdims=True)
    d_pre = d_pre.astype(BF)
    d_pre_ref[...] = d_pre
    part_ref[...] = dot(d_pre, up_ref[...]).astype(BF)


def feed_forward(hidden, grad, up_low, down_low, bias):
    tokens, width = hidden.shape
    units = up_low.shape[0]
    block = tokens // 2
    rows = lambda last: pl.BlockSpec((block, last), lambda i: (i, 0))
    whole = lambda shape: pl.BlockSpec(shape, lambda i: (0,) * len(shape))
    return pl.pallas_call(
        feed_forward_kernel,
        grid=(tokens // block,),
        in_specs=[
            rows(width),
            rows(width),
            whole(up_low.shape),
            whole(down_low.shape),
            whole((1, units)),
        ],
        out_specs=[rows(units), rows(units), rows(width), whole((1, units))],
        out_shape=[
            jax.ShapeDtypeStruct((tokens, units), BF),
            jax.ShapeDtypeStruct((tokens, units), BF),
            jax.ShapeDtypeStruct((tokens, width), BF),
            jax.ShapeDtypeStruct((1, units), F32),
        ],
        compiler_params=pltpu.CompilerParams(vmem_limit_bytes=VMEM_LIMIT),
        cost_estimate=pl.CostEstimate(
            flops=6 * tokens * width * units,
            bytes_accessed=tokens * width * 10 + up_low.size * 4,
            transcendentals=tokens * units,
        ),
    )(hidden, grad, up_low, down_low, bias)


def dp_swap(piece, mask):
    return lax.ppermute(piece, "dp", [(i, i ^ mask) for i in range(lax.axis_size("dp"))])


def dp_levels():
    size, step, levels = lax.axis_size("dp"), 2, []
    while step < size:
        radix = min(4, size // step)
        levels.append((step, radix))
        step *= radix
    return levels + [(1, 2)]


def dp_masks():
    masks = [0]
    for step, radix in dp_levels():
        masks = [j * step + mask for j in range(radix) for mask in masks]
    return masks


def dp_collect(piece):
    gathered = piece[None]
    for step, radix in dp_levels():
        gathered = jnp.concatenate(
            [gathered] + [dp_swap(gathered, j * step) for j in range(1, radix)], axis=0
        )
    return gathered


def dp_scatter_sum(value):
    for step, radix in reversed(dp_levels()):
        value = value.reshape((radix, -1) + value.shape[1:])
        total = value[0].astype(F32)
        for j in range(1, radix):
            total = total + dp_swap(value[j], j * step).astype(F32)
        value = total.astype(BF)
    return value[0]


def dp_reduce(value):
    size = lax.axis_size("dp")
    value = reorder(value, dp_masks(), lax.axis_index("dp"))
    return dp_scatter_sum(value.reshape((size, -1) + value.shape[1:]))


def dp_gather(piece):
    size, rank, masks = lax.axis_size("dp"), lax.axis_index("dp"), dp_masks()
    table = jnp.asarray([masks.index(p) for p in range(size)], jnp.int32)
    gathered = dp_collect(piece)
    blocks = [
        lax.dynamic_index_in_dim(gathered, table[rank ^ p], 0, False) for p in range(size)
    ]
    return jnp.concatenate(blocks, axis=0)


def swap(piece, mask, ranks=None):
    size = lax.axis_size("tensor")
    if ranks is None:
        return lax.ppermute(piece, "tensor", [(i, i ^ mask) for i in range(size)])
    pairs = [(r * size + i, r * size + (i ^ mask)) for r in ranks for i in range(size)]
    return lax.ppermute(piece, ("dp", "tensor"), pairs)


def scatter_sum(value, ranks=None):
    size = lax.axis_size("tensor")
    rows = value.shape[0] // size
    total = value[:rows].astype(F32)
    for mask in range(1, size):
        total = total + swap(value[mask * rows : (mask + 1) * rows], mask, ranks).astype(F32)
    return total


def collect(piece, ranks=None):
    size = lax.axis_size("tensor")
    return jnp.concatenate([piece] + [swap(piece, mask, ranks) for mask in range(1, size)], axis=0)


def reorder(value, masks, index):
    masks = list(range(masks)) if isinstance(masks, int) else masks
    rows = value.shape[0] // len(masks)
    return jnp.concatenate(
        [lax.dynamic_slice_in_dim(value, (index ^ p) * rows, rows, 0) for p in masks], axis=0
    )


def normed_of(values):
    average = jnp.mean(values, axis=-1, keepdims=True)
    centered = values - average
    variance = jnp.mean(centered * centered, axis=-1, keepdims=True)
    inverse = lax.rsqrt(variance + NORM_EPS)
    return centered * inverse, inverse


def norm_back(normed, inverse, grad):
    return (
        grad
        - jnp.mean(grad, axis=-1, keepdims=True)
        - normed * jnp.mean(grad * normed, axis=-1, keepdims=True)
    ) * inverse


def on_device(
    inputs,
    condition,
    cotangent,
    w_ada,
    w_qkv,
    w_proj,
    w_up,
    w_down,
    biases,
    momentum_ada,
    momentum_qkv,
    momentum_proj,
    momentum_up,
    momentum_down,
    bias_first,
    bias_second,
):
    quarter = w_ada.shape[1]
    width = w_ada.shape[-1]
    latent_count = inputs.shape[0]
    seq_length = inputs.shape[1]
    tokens = latent_count * seq_length
    heads_here = quarter // HEAD_DIM
    size = lax.axis_size("tensor")
    me = lax.axis_index("tensor")
    dp_size = lax.axis_size("dp")
    dp_rank = lax.axis_index("dp")
    chunk = tokens // size
    my_latent = me // (size // latent_count)
    scale_factor = 1.0 / math.sqrt(HEAD_DIM)
    flat = lambda w: w.reshape(-1, width)
    ada_low = flat(w_ada).astype(BF)
    qkv_low = flat(w_qkv).astype(BF)
    proj_low = w_proj.astype(BF)
    up_bias = biases[9:13].reshape(-1)

    cond_act, silu_pull = jax.vjp(jax.nn.silu, condition.astype(F32))
    cond_low = cond_act.astype(BF)
    mod_part = dot_t(cond_low, ada_low).reshape(latent_count * 6, quarter) + jnp.tile(
        biases[0:6], (latent_count, 1)
    )
    mod_part = jnp.concatenate([mod_part, biases[8:9], biases[13:14]], axis=0)
    gathered = collect(mod_part[None])
    gathered = reorder(gathered, size, me)
    gathered = jnp.moveaxis(gathered, 0, 1).reshape(-1, width)
    modulation = reorder(gathered[: latent_count * 6], latent_count, my_latent).reshape(
        latent_count, 6, width
    )
    bias_proj = gathered[latent_count * 6]
    bias_down = gathered[latent_count * 6 + 1]
    shift_first, scale_first, gate_first = modulation[0, 0], modulation[0, 1], modulation[0, 2]
    shift_second, scale_second, gate_second = modulation[0, 3], modulation[0, 4], modulation[0, 5]

    modulation, cond_low = lax.optimization_barrier((modulation, cond_low))
    cond_all = dp_collect(cond_low).reshape(-1, width)

    tokens_in = reorder(inputs.reshape(tokens, width), size, me)
    tangent = reorder(cotangent.reshape(tokens, width), size, me)
    partial_first, first_low, heads, attended_low = attention(
        tokens_in, modulation, qkv_low, proj_low, biases[6:8], seq_length
    )
    partial_first, w_up, w_down = lax.optimization_barrier((partial_first, w_up, w_down))
    up_low = flat(w_up).astype(BF)
    down_low = flat(w_down).astype(BF)
    own = tokens_in[:chunk].astype(F32)
    tangent_own = tangent[:chunk].astype(F32)

    branch_first = scatter_sum(partial_first) + bias_proj
    middle = own + gate_first * branch_first
    normed_second, inverse_second = normed_of(middle)
    second_low = collect((normed_second * (1.0 + scale_second) + shift_second).astype(BF))

    d_branch_second = (
        tangent.astype(F32).reshape(latent_count, seq_length, width)
        * modulation[:, 5][:, None, :]
    ).reshape(tokens, width)
    d_down_bias = jnp.sum(d_branch_second, axis=0)
    d_second_low = d_branch_second.astype(BF)
    act_low, d_pre_low, second_part, d_up_bias = feed_forward(
        second_low, d_second_low, up_low, down_low, up_bias[None]
    )
    d_up_bias = d_up_bias.reshape(-1, quarter)
    partial_second = dot(act_low, down_low)
    second_latents = partial_second.reshape(latent_count, seq_length, width)
    d_gate_second = jnp.sum(
        tangent.astype(F32).reshape(second_latents.shape) * second_latents, axis=1
    )
    d_gate_second = d_gate_second.at[0].add(bias_down * jnp.sum(tangent_own, axis=0))
    output_part = (second_latents * modulation[:, 5][:, None, :]).reshape(tokens, width)
    output_part = jnp.concatenate(
        [output_part[:chunk] + (middle + gate_second * bias_down), output_part[chunk:]], axis=0
    ).astype(BF)

    d_hidden_second = scatter_sum(second_part)
    (
        d_hidden_second,
        momentum_ada,
        momentum_qkv,
        momentum_proj,
        momentum_up,
        momentum_down,
        w_ada_old,
        w_qkv_old,
        w_proj_old,
        w_up_old,
        w_down_old,
    ) = lax.optimization_barrier(
        (
            d_hidden_second,
            momentum_ada,
            momentum_qkv,
            momentum_proj,
            momentum_up,
            momentum_down,
            w_ada,
            w_qkv,
            w_proj,
            w_up,
            w_down,
        )
    )

    grad_down = t_dot(act_low, d_second_low).astype(BF)
    grad_up = t_dot(d_pre_low, second_low).astype(BF)
    grad_up, grad_down = lax.psum((grad_up, grad_down), "dp")

    d_shift_second = jnp.sum(d_hidden_second, axis=0)
    d_scale_second = jnp.sum(d_hidden_second * normed_second, axis=0)
    d_middle = tangent_own + norm_back(
        normed_second, inverse_second, d_hidden_second * (1.0 + scale_second)
    )
    d_branch_first = gate_first * d_middle
    d_gate_first = jnp.sum(d_middle * branch_first, axis=0)
    d_proj_bias = jnp.sum(d_branch_first, axis=0)
    d_first_low = collect(d_branch_first.astype(BF))

    grad_proj = t_dot(attended_low, d_first_low).astype(BF)
    d_heads, first_part, d_head_sums = attention_back(
        d_first_low, heads, qkv_low, proj_low, seq_length
    )
    d_head_bias = jnp.sum(d_head_sums, axis=0)
    grad_qkv = jnp.concatenate([t_dot(d_heads[k], first_low) for k in range(3)], axis=0).astype(BF)
    late_grads = dp_reduce(jnp.concatenate([grad_qkv, grad_proj], axis=0))
    d_hidden_first = scatter_sum(first_part)
    late_grads, grad_up, grad_down = lax.optimization_barrier((late_grads, grad_up, grad_down))
    late_grads = dp_gather(late_grads)
    grad_qkv, grad_proj = late_grads[: 3 * quarter], late_grads[3 * quarter :]

    normed_own, inverse_own = normed_of(own)
    d_shift_first = jnp.sum(d_hidden_first, axis=0)
    d_scale_first = jnp.sum(d_hidden_first * normed_own, axis=0)
    grad_inputs = d_middle + norm_back(
        normed_own, inverse_own, d_hidden_first * (1.0 + scale_first)
    )
    grad_inputs = grad_inputs.astype(BF)

    sums = jnp.stack(
        [
            d_shift_first,
            d_scale_first,
            d_gate_first,
            d_shift_second,
            d_scale_second,
            d_proj_bias,
            *d_gate_second,
        ]
    )
    of_device = [
        lax.dynamic_slice_in_dim(sums, (me ^ mask) * quarter, quarter, 1) for mask in range(size)
    ]
    arrived = jnp.stack(
        [of_device[0]] + [swap(of_device[mask], mask) for mask in range(1, size)]
    )
    d_proj_own = jnp.sum(arrived[:, 5], axis=0)
    per_latent = size // latent_count
    d_gate_own = [
        sum(arrived[mask, 6 + (q ^ (mask // per_latent))] for mask in range(size))
        for q in range(latent_count)
    ]
    d_mod_own = jnp.sum(
        arrived[:, :5].reshape(latent_count, per_latent, 5, quarter), axis=1
    )
    d_mod_own = jnp.concatenate([d_mod_own, jnp.stack(d_gate_own)[:, None]], axis=1)
    d_mod_own = reorder(d_mod_own, latent_count, my_latent)
    d_cond_part = dot(d_mod_own.reshape(latent_count, -1).astype(BF), ada_low)
    d_down_own = lax.dynamic_slice_in_dim(d_down_bias, me * quarter, quarter, 0)
    small = jnp.concatenate(
        [
            d_mod_own.reshape(-1, quarter),
            d_head_bias,
            d_proj_own[None],
            d_up_bias,
            d_down_own[None],
        ],
        axis=0,
    )
    small_all = dp_collect(small)
    d_mod_all = small_all[:, : 6 * latent_count].reshape(-1, 6, quarter)
    grad_biases = jnp.concatenate(
        [jnp.sum(d_mod_all, axis=0), jnp.sum(small_all[:, 6 * latent_count :], axis=0)], axis=0
    )
    d_mod_low = d_mod_all.reshape(d_mod_all.shape[0], -1).astype(BF)
    grad_ada = t_dot(d_mod_low, cond_all)

    cross = jnp.dot(
        d_mod_low.astype(F32), flat(momentum_ada), precision=lax.Precision.HIGHEST
    )
    summed = jnp.concatenate([d_cond_part, cross, dot_t(d_mod_low, d_mod_low) @ jnp.eye(d_mod_low.shape[0], width, dtype=F32)], axis=0)
    summed = sum([swap(summed, mask) for mask in range(1, size)], summed)
    d_cond_act, cross, square = (
        summed[:latent_count],
        summed[latent_count : latent_count + d_mod_low.shape[0]],
        summed[latent_count + d_mod_low.shape[0] :, : d_mod_low.shape[0]],
    )
    grad_condition = silu_pull(d_cond_act)[0]
    corr = MUON_MOMENTUM * cross + 0.5 * jnp.dot(
        square, cond_all.astype(F32), precision=lax.Precision.HIGHEST
    )
    corr = jnp.where(dp_rank == OWNERS[0], corr, 0.0)

    moments = (
        MUON_MOMENTUM * flat(momentum_ada) + grad_ada,
        MUON_MOMENTUM * flat(momentum_qkv) + grad_qkv.astype(F32),
        MUON_MOMENTUM * momentum_proj + grad_proj.astype(F32),
        MUON_MOMENTUM * flat(momentum_up) + grad_up.astype(F32),
        MUON_MOMENTUM * flat(momentum_down) + grad_down.astype(F32),
    )
    starts = tuple(m.astype(BF) for m in moments)

    block_rows = len(blocks_of(width // TILE)) * TILE
    none = jnp.zeros((block_rows, TILE), F32)
    turn = jnp.int32(0)
    for place, matrix_index in enumerate((0, 3, 4)):
        turn = jnp.where(dp_rank == OWNERS[matrix_index], place + 1, turn)
    early = lax.switch(
        turn,
        [lambda *rows: none] + [(lambda *rows, k=k: gram_blocks(rows[k])) for k in range(3)],
        flat(momentum_ada),
        starts[3],
        starts[4],
    )
    early_ranks = [OWNERS[k] for k in (0, 3, 4)]
    early = collect(scatter_sum(reorder(early, size, me), early_ranks), early_ranks)
    late = lax.cond(dp_rank == OWNERS[1], gram_blocks, lambda rows: none, starts[1])
    late = collect(scatter_sum(reorder(late, size, me), OWNERS[1:2]), OWNERS[1:2])
    proj_rows = collect(starts[2], OWNERS[2:3])
    proj_gram = lax.cond(dp_rank == OWNERS[2], gram_blocks, lambda rows: none, proj_rows)
    coefficient = jnp.where(dp_rank == OWNERS[0], MUON_MOMENTUM**2, 1.0)
    gram = reorder(jnp.where(dp_rank == OWNERS[1], late, early * coefficient), size, me)
    gram = jnp.where(dp_rank == OWNERS[2], proj_gram, gram)
    gram, output_part, grad_inputs = lax.optimization_barrier((gram, output_part, grad_inputs))
    output = lax.psum(reorder(output_part, size, me), "tensor").reshape(inputs.shape)
    grad_inputs = reorder(collect(grad_inputs), size, me).reshape(inputs.shape)
    factor = newton_schulz_factor(gram, cond_all, corr, width)
    column_width = width // dp_size
    column_start = dp_rank * column_width
    factors = lax.all_to_all(
        factor.reshape(dp_size, column_width, width), "dp", 0, 0, tiled=True
    )

    weights_old = (w_ada_old, w_qkv_old, w_proj_old, w_up_old, w_down_old)
    sizes = [max(w.size // width * size, width) for w in weights_old]
    columns = [
        lax.dynamic_slice_in_dim(flat(w), column_start, column_width, 1) for w in weights_old
    ]
    new_weights = update_weights(starts, columns, factors, sizes)
    new_weights = [
        new.reshape(old.shape[:-1] + (column_width,))
        for new, old in zip(new_weights, weights_old)
    ]
    new_bias_first = BETA_ONE * bias_first + (1.0 - BETA_ONE) * grad_biases
    new_bias_second = BETA_TWO * bias_second + (1.0 - BETA_TWO) * grad_biases * grad_biases
    first_hat = new_bias_first / (1.0 - BETA_ONE**STEP)
    second_hat = new_bias_second / (1.0 - BETA_TWO**STEP)
    new_biases = biases - ADAM_RATE * first_hat / (jnp.sqrt(second_hat) + ADAM_EPS)
    return (
        output,
        grad_inputs,
        grad_condition,
        *new_weights,
        moments[0].reshape(momentum_ada.shape),
        moments[1].reshape(momentum_qkv.shape),
        moments[2],
        moments[3].reshape(momentum_up.shape),
        moments[4].reshape(momentum_down.shape),
        new_biases,
        new_bias_first,
        new_bias_second,
    )


def solution(mesh):
    placed = (
        P("dp", None, None),
        P("dp", None),
        P("dp", None, None),
        P(None, "tensor", None),
        P(None, "tensor", None),
        P("tensor", None),
        P(None, "tensor", None),
        P(None, "tensor", None),
        P(None, "tensor"),
        P(None, "tensor", None),
        P(None, "tensor", None),
        P("tensor", None),
        P(None, "tensor", None),
        P(None, "tensor", None),
        P(None, "tensor"),
        P(None, "tensor"),
    )
    return jax.shard_map(
        on_device,
        mesh=mesh,
        in_specs=placed,
        out_specs=(
            P("dp", None, None),
            P("dp", None, None),
            P("dp", None),
            P(None, "tensor", "dp"),
            P(None, "tensor", "dp"),
            P("tensor", "dp"),
            P(None, "tensor", "dp"),
            P(None, "tensor", "dp"),
            P(None, "tensor", None),
            P(None, "tensor", None),
            P("tensor", None),
            P(None, "tensor", None),
            P(None, "tensor", None),
            P(None, "tensor"),
            P(None, "tensor"),
            P(None, "tensor"),
        ),
        check_vma=False,
    )
```

```python
import functools
import math

import jax
import jax.numpy as jnp
from jax import lax
from jax.experimental import pallas as pl
from jax.experimental.pallas import tpu as pltpu
from jax.sharding import PartitionSpec as P

HEAD_DIM = 64
NS_ITERS = 5
STEP = 10


NS_A = 3.4445
NS_B = -4.775
NS_C = 2.0315
MUON_RATE = 0.16
MUON_DECAY = 0.01
MUON_MOMENTUM = 0.95
ADAM_RATE = 0.25
BETA_ONE = 0.9
BETA_TWO = 0.999
ADAM_EPS = 1e-08
NORM_EPS = 1e-06

BF = jnp.bfloat16
F32 = jnp.float32
TILE = 256
VMEM_LIMIT = 28 * 1024 * 1024
OWNERS = (0, 2, 1, 4, 6)


def dot(a, b):
    return jnp.dot(a, b, preferred_element_type=F32)


def dot_t(a, b):
    return lax.dot_general(a, b, (((1,), (1,)), ((), ())), preferred_element_type=F32)


def t_dot(a, b):
    return lax.dot_general(a, b, (((0,), (0,)), ((), ())), preferred_element_type=F32)


def parts(value):
    high = value.astype(BF)
    return high, (value - high.astype(F32)).astype(BF)


def blocks_of(count):
    return [(i, j) for i in range(count) for j in range(i, count)]


def gram_kernel(rows_ref, out_ref):
    count = rows_ref.shape[1] // TILE
    low = rows_ref[...].astype(BF)
    for k, (i, j) in enumerate(blocks_of(count)):
        out_ref[k * TILE : (k + 1) * TILE, :] = t_dot(
            low[:, i * TILE : (i + 1) * TILE], low[:, j * TILE : (j + 1) * TILE]
        )


def gram_blocks(rows):
    depth, width = rows.shape
    count = len(blocks_of(width // TILE))
    return pl.pallas_call(
        gram_kernel,
        out_shape=jax.ShapeDtypeStruct((count * TILE, TILE), F32),
        compiler_params=pltpu.CompilerParams(vmem_limit_bytes=VMEM_LIMIT),
        cost_estimate=pl.CostEstimate(
            flops=2 * depth * width * width, bytes_accessed=depth * width * 6, transcendentals=0
        ),
    )(rows)


def newton_schulz_kernel(
    blocks_ref, cond_ref, corr_ref, out_ref, cur, high, rest, poly, mid_h, mid_l, f_h, f_l, g_h, g_l
):
    width = cur.shape[0]
    spans = [slice(i * TILE, (i + 1) * TILE) for i in range(width // TILE)]
    corr = corr_ref[...]
    corr_h, corr_l = parts(corr)
    cond = cond_ref[...]
    for k, (i, j) in enumerate(blocks_of(width // TILE)):
        block = (
            blocks_ref[k * TILE : (k + 1) * TILE, :]
            + t_dot(cond[:, spans[i]], corr_h[:, spans[j]])
            + t_dot(cond[:, spans[i]], corr_l[:, spans[j]])
            + t_dot(corr_h[:, spans[i]], cond[:, spans[j]])
            + t_dot(corr_l[:, spans[i]], cond[:, spans[j]])
        )
        cur[spans[i], spans[j]] = block
        if i != j:
            cur[spans[j], spans[i]] = block.T
    square_norm = jnp.zeros((1, 1), F32)
    row = lax.broadcasted_iota(jnp.int32, (TILE, TILE), 0)
    col = lax.broadcasted_iota(jnp.int32, (TILE, TILE), 1)
    for span in spans:
        square_norm += jnp.sum(jnp.where(row == col, cur[span, span], 0.0), keepdims=True)
    scale = 1.0 / (jnp.sqrt(square_norm) + 1e-07)
    for span in spans:
        cur[span, :] = cur[span, :] * (scale * scale)

    def make_poly():
        for span in spans:
            high[span, :], rest[span, :] = parts(cur[span, :])
        for span in spans:
            poly[span, :] = (NS_B * cur[span, :] + NS_C * dot(high[span, :], high[...])).astype(BF)

    def step_gram():
        for span in spans:
            half = (
                NS_A * cur[span, :] + dot(high[span, :], poly[...]) + dot(rest[span, :], poly[...])
            )
            mid_h[span, :], mid_l[span, :] = parts(half)
        for span in spans:
            half = mid_h[span, :].astype(F32) + mid_l[span, :].astype(F32)
            cur[span, :] = (
                NS_A * half + dot(poly[span, :], mid_h[...]) + dot(poly[span, :], mid_l[...])
            )

    def stepped_factor(span):
        before = f_h[span, :].astype(F32) + f_l[span, :].astype(F32)
        return NS_A * before + dot(poly[span, :], f_h[...]) + dot(poly[span, :], f_l[...])

    make_poly()
    wide_row = lax.broadcasted_iota(jnp.int32, (TILE, width), 0)
    wide_col = lax.broadcasted_iota(jnp.int32, (TILE, width), 1)
    for i, span in enumerate(spans):
        start = poly[span, :].astype(F32) + jnp.where(wide_row + i * TILE == wide_col, NS_A, 0.0)
        f_h[span, :], f_l[span, :] = parts(start)
    step_gram()

    def middle(_, carry):
        make_poly()
        for span in spans:
            g_h[span, :], g_l[span, :] = parts(stepped_factor(span))
        f_h[...] = g_h[...]
        f_l[...] = g_l[...]
        step_gram()
        return carry

    lax.fori_loop(0, NS_ITERS - 2, middle, 0)
    make_poly()
    for span in spans:
        out_ref[span, :] = (stepped_factor(span) * scale).astype(out_ref.dtype)


def newton_schulz_factor(blocks, cond, corr, width):
    whole = lambda kind: pltpu.VMEM((width, width), kind)
    return pl.pallas_call(
        newton_schulz_kernel,
        out_shape=jax.ShapeDtypeStruct((width, width), BF),
        scratch_shapes=[whole(F32)] + [whole(BF)] * 9,
        compiler_params=pltpu.CompilerParams(vmem_limit_bytes=VMEM_LIMIT),
        cost_estimate=pl.CostEstimate(
            flops=2 * 29 * width**3, bytes_accessed=width * width * 6, transcendentals=0
        ),
    )(blocks, cond, corr)


def update_kernel(sizes, *refs):
    count = len(sizes)
    rows, weights, factor, outs = refs[:count], refs[count : 2 * count], refs[2 * count], refs[2 * count + 1 :]
    for k, size in enumerate(sizes):
        ortho = dot_t(rows[k][...], factor[OWNERS[k]])
        outs[k][...] = (
            weights[k][...] * (1.0 - MUON_RATE * MUON_DECAY)
            - MUON_RATE * 0.2 * math.sqrt(size) * ortho
        )


def update_weights(rows, weights, factors, sizes):
    return pl.pallas_call(
        functools.partial(update_kernel, sizes),
        out_shape=[jax.ShapeDtypeStruct(w.shape, F32) for w in weights],
        compiler_params=pltpu.CompilerParams(vmem_limit_bytes=VMEM_LIMIT),
        cost_estimate=pl.CostEstimate(
            flops=sum(2 * r.size * w.shape[1] for r, w in zip(rows, weights)),
            bytes_accessed=sum(2 * r.size + 12 * w.size for r, w in zip(rows, weights)),
            transcendentals=0,
        ),
    )(*rows, *weights, factors)


def attention_kernel(
    x_ref, mod_ref, w_ref, proj_ref, bias_ref, partial_ref, hidden_ref, heads_ref, attended_ref
):
    quarter = proj_ref.shape[0]
    normed, _ = normed_of(x_ref[...].astype(F32))
    hidden = (normed * (1.0 + mod_ref[0, 1:2, :]) + mod_ref[0, 0:1, :]).astype(BF)
    hidden_ref[...] = hidden
    queries = (dot_t(hidden, w_ref[:quarter, :]) + bias_ref[0:1, :]).astype(BF)
    keys = dot_t(hidden, w_ref[quarter : 2 * quarter, :]).astype(BF)
    values = (dot_t(hidden, w_ref[2 * quarter :, :]) + bias_ref[1:2, :]).astype(BF)
    heads_ref[0] = queries
    heads_ref[1] = keys
    heads_ref[2] = values
    attended = []
    for start in range(0, quarter, HEAD_DIM):
        head = slice(start, start + HEAD_DIM)
        probs = softmax_of(queries[:, head], keys[:, head]).astype(BF)
        attended.append(dot(probs, values[:, head]))
    attended = jnp.concatenate(attended, axis=1).astype(BF)
    attended_ref[...] = attended
    partial_ref[...] = dot(attended, proj_ref[...]).astype(BF)


def softmax_of(queries, keys):
    scores = dot_t(queries, keys) * (1.0 / math.sqrt(HEAD_DIM))
    raised = jnp.exp(scores - jnp.max(scores, axis=-1, keepdims=True))
    return raised * (1.0 / jnp.sum(raised, axis=-1, keepdims=True))


def attention(tokens_in, modulation, qkv_low, proj_low, bias_rows, seq_length):
    tokens, width = tokens_in.shape
    quarter = proj_low.shape[0]
    rows = lambda last: pl.BlockSpec((seq_length, last), lambda i: (i, 0))
    whole = lambda shape: pl.BlockSpec(shape, lambda i: (0,) * len(shape))
    return pl.pallas_call(
        attention_kernel,
        grid=(tokens // seq_length,),
        in_specs=[
            rows(width),
            pl.BlockSpec((1, 6, width), lambda i: (i, 0, 0)),
            whole(qkv_low.shape),
            whole(proj_low.shape),
            whole(bias_rows.shape),
        ],
        out_specs=[
            rows(width),
            rows(width),
            pl.BlockSpec((3, seq_length, quarter), lambda i: (0, i, 0)),
            rows(quarter),
        ],
        out_shape=[
            jax.ShapeDtypeStruct((tokens, width), BF),
            jax.ShapeDtypeStruct((tokens, width), BF),
            jax.ShapeDtypeStruct((3, tokens, quarter), BF),
            jax.ShapeDtypeStruct((tokens, quarter), BF),
        ],
        compiler_params=pltpu.CompilerParams(vmem_limit_bytes=VMEM_LIMIT),
        cost_estimate=pl.CostEstimate(
            flops=8 * tokens * width * quarter + 4 * tokens * seq_length * quarter,
            bytes_accessed=tokens * width * 8 + qkv_low.size * 3,
            transcendentals=tokens * seq_length * quarter // HEAD_DIM,
        ),
    )(tokens_in, modulation, qkv_low, proj_low, bias_rows)


def attention_back_kernel(grad_ref, heads_ref, w_ref, proj_ref, d_heads_ref, part_ref, sums_ref):
    quarter = proj_ref.shape[0]
    scale = 1.0 / math.sqrt(HEAD_DIM)
    d_attended = dot_t(grad_ref[...], proj_ref[...]).astype(BF)
    queries, keys, values = heads_ref[0], heads_ref[1], heads_ref[2]
    d_queries, d_keys, d_values = [], [], []
    for start in range(0, quarter, HEAD_DIM):
        head = slice(start, start + HEAD_DIM)
        probs = softmax_of(queries[:, head], keys[:, head])
        d_out = d_attended[:, head]
        d_values.append(t_dot(probs.astype(BF), d_out))
        d_probs = dot_t(d_out, values[:, head])
        d_scores = (
            probs * (d_probs - jnp.sum(probs * d_probs, axis=-1, keepdims=True))
        ).astype(BF)
        d_queries.append(dot(d_scores, keys[:, head]) * scale)
        d_keys.append(t_dot(d_scores, queries[:, head]) * scale)
    d_queries = jnp.concatenate(d_queries, axis=1)
    d_values = jnp.concatenate(d_values, axis=1)
    sums_ref[0, 0:1, :] = jnp.sum(d_queries, axis=0, keepdims=True)
    sums_ref[0, 1:2, :] = jnp.sum(d_values, axis=0, keepdims=True)
    d_queries = d_queries.astype(BF)
    d_keys = jnp.concatenate(d_keys, axis=1).astype(BF)
    d_values = d_values.astype(BF)
    d_heads_ref[0] = d_queries
    d_heads_ref[1] = d_keys
    d_heads_ref[2] = d_values
    part_ref[...] = (
        dot(d_queries, w_ref[:quarter, :])
        + dot(d_keys, w_ref[quarter : 2 * quarter, :])
        + dot(d_values, w_ref[2 * quarter :, :])
    ).astype(BF)


def attention_back(grad, heads, qkv_low, proj_low, seq_length):
    tokens, width = grad.shape
    quarter = proj_low.shape[0]
    rows = lambda last: pl.BlockSpec((seq_length, last), lambda i: (i, 0))
    whole = lambda shape: pl.BlockSpec(shape, lambda i: (0,) * len(shape))
    of_heads = pl.BlockSpec((3, seq_length, quarter), lambda i: (0, i, 0))
    return pl.pallas_call(
        attention_back_kernel,
        grid=(tokens // seq_length,),
        in_specs=[rows(width), of_heads, whole(qkv_low.shape), whole(proj_low.shape)],
        out_specs=[
            of_heads,
            rows(width),
            pl.BlockSpec((1, 2, quarter), lambda i: (i, 0, 0)),
        ],
        out_shape=[
            jax.ShapeDtypeStruct(heads.shape, BF),
            jax.ShapeDtypeStruct((tokens, width), BF),
            jax.ShapeDtypeStruct((tokens // seq_length, 2, quarter), F32),
        ],
        compiler_params=pltpu.CompilerParams(vmem_limit_bytes=VMEM_LIMIT),
        cost_estimate=pl.CostEstimate(
            flops=8 * tokens * width * quarter + 10 * tokens * seq_length * quarter,
            bytes_accessed=tokens * width * 8 + qkv_low.size * 3,
            transcendentals=tokens * seq_length * quarter // HEAD_DIM,
        ),
    )(grad, heads, qkv_low, proj_low)


def feed_forward_kernel(
    hidden_ref, grad_ref, up_ref, down_ref, bias_ref, act_ref, d_pre_ref, part_ref, sums_ref
):
    pre = dot_t(hidden_ref[...], up_ref[...]) + bias_ref[...]
    d_act = dot_t(grad_ref[...], down_ref[...])
    root = math.sqrt(2.0 / math.pi)
    square = pre * pre
    bent = jnp.tanh(root * pre * (1.0 + 0.044715 * square))
    half = 0.5 * (1.0 + bent)
    act_ref[...] = (pre * half).astype(BF)
    slope = half + 0.5 * pre * (1.0 - bent * bent) * (root * (1.0 + 0.134145 * square))
    d_pre = d_act * slope

    @pl.when(pl.program_id(0) == 0)
    def _():
        sums_ref[...] = jnp.zeros_like(sums_ref)

    sums_ref[...] += jnp.sum(d_pre, axis=0, keepdims=True)
    d_pre = d_pre.astype(BF)
    d_pre_ref[...] = d_pre
    part_ref[...] = dot(d_pre, up_ref[...]).astype(BF)


def feed_forward(hidden, grad, up_low, down_low, bias):
    tokens, width = hidden.shape
    units = up_low.shape[0]
    block = tokens // 2
    rows = lambda last: pl.BlockSpec((block, last), lambda i: (i, 0))
    whole = lambda shape: pl.BlockSpec(shape, lambda i: (0,) * len(shape))
    return pl.pallas_call(
        feed_forward_kernel,
        grid=(tokens // block,),
        in_specs=[
            rows(width),
            rows(width),
            whole(up_low.shape),
            whole(down_low.shape),
            whole((1, units)),
        ],
        out_specs=[rows(units), rows(units), rows(width), whole((1, units))],
        out_shape=[
            jax.ShapeDtypeStruct((tokens, units), BF),
            jax.ShapeDtypeStruct((tokens, units), BF),
            jax.ShapeDtypeStruct((tokens, width), BF),
            jax.ShapeDtypeStruct((1, units), F32),
        ],
        compiler_params=pltpu.CompilerParams(vmem_limit_bytes=VMEM_LIMIT),
        cost_estimate=pl.CostEstimate(
            flops=6 * tokens * width * units,
            bytes_accessed=tokens * width * 10 + up_low.size * 4,
            transcendentals=tokens * units,
        ),
    )(hidden, grad, up_low, down_low, bias)


def dp_swap(piece, mask):
    return lax.ppermute(piece, "dp", [(i, i ^ mask) for i in range(lax.axis_size("dp"))])


def dp_levels():
    size, step, levels = lax.axis_size("dp"), 2, []
    while step < size:
        radix = min(4, size // step)
        levels.append((step, radix))
        step *= radix
    return levels + [(1, 2)]


def dp_masks():
    masks = [0]
    for step, radix in dp_levels():
        masks = [j * step + mask for j in range(radix) for mask in masks]
    return masks


def dp_collect(piece):
    gathered = piece[None]
    for step, radix in dp_levels():
        gathered = jnp.concatenate(
            [gathered] + [dp_swap(gathered, j * step) for j in range(1, radix)], axis=0
        )
    return gathered


def dp_scatter_sum(value):
    for step, radix in reversed(dp_levels()):
        value = value.reshape((radix, -1) + value.shape[1:])
        total = value[0].astype(F32)
        for j in range(1, radix):
            total = total + dp_swap(value[j], j * step).astype(F32)
        value = total.astype(BF)
    return value[0]


def dp_reduce(value):
    size = lax.axis_size("dp")
    value = reorder(value, dp_masks(), place_of("dp"))
    return dp_scatter_sum(value.reshape((size, -1) + value.shape[1:]))


def dp_gather(piece):
    rank, place, bit = place_of("dp"), jnp.uint32(0), 0
    masks = dp_masks()
    while 1 << bit < len(masks):
        place = place | (((rank >> bit) & 1) * masks.index(1 << bit))
        bit += 1
    gathered = dp_collect(piece)
    return reorder(
        gathered.reshape((-1,) + piece.shape[1:]), [masks.index(p) for p in range(len(masks))], place
    )


def place_of(axis):
    return lax.axis_index(axis).astype(jnp.uint32)


def swap(piece, mask, ranks=None):
    size = lax.axis_size("tensor")
    if ranks is None:
        return lax.ppermute(piece, "tensor", [(i, i ^ mask) for i in range(size)])
    pairs = [(r * size + i, r * size + (i ^ mask)) for r in ranks for i in range(size)]
    return lax.ppermute(piece, ("dp", "tensor"), pairs)


def scatter(value, ranks=None):
    size = lax.axis_size("tensor")
    rows = value.shape[0] // size
    return [value[:rows]] + [
        swap(value[mask * rows : (mask + 1) * rows], mask, ranks) for mask in range(1, size)
    ]


def total(pieces):
    return sum([piece.astype(F32) for piece in pieces[1:]], pieces[0].astype(F32))


def scatter_sum(value, ranks=None):
    return total(scatter(value, ranks))


def collect(piece, ranks=None):
    size = lax.axis_size("tensor")
    return jnp.concatenate([piece] + [swap(piece, mask, ranks) for mask in range(1, size)], axis=0)


def reorder(value, masks, index):
    masks = list(range(masks)) if isinstance(masks, int) else masks
    rows = value.shape[0] // len(masks)
    return jnp.concatenate(
        [lax.dynamic_slice_in_dim(value, (index ^ p) * rows, rows, 0) for p in masks], axis=0
    )


def normed_of(values):
    average = jnp.mean(values, axis=-1, keepdims=True)
    centered = values - average
    variance = jnp.mean(centered * centered, axis=-1, keepdims=True)
    inverse = lax.rsqrt(variance + NORM_EPS)
    return centered * inverse, inverse


def norm_back(normed, inverse, grad):
    return (
        grad
        - jnp.mean(grad, axis=-1, keepdims=True)
        - normed * jnp.mean(grad * normed, axis=-1, keepdims=True)
    ) * inverse


def on_device(
    inputs,
    condition,
    cotangent,
    w_ada,
    w_qkv,
    w_proj,
    w_up,
    w_down,
    biases,
    momentum_ada,
    momentum_qkv,
    momentum_proj,
    momentum_up,
    momentum_down,
    bias_first,
    bias_second,
):
    quarter = w_ada.shape[1]
    width = w_ada.shape[-1]
    latent_count = inputs.shape[0]
    seq_length = inputs.shape[1]
    tokens = latent_count * seq_length
    heads_here = quarter // HEAD_DIM
    size = lax.axis_size("tensor")
    me = place_of("tensor")
    dp_size = lax.axis_size("dp")
    dp_rank = place_of("dp")
    chunk = tokens // size
    my_latent = me // (size // latent_count)
    scale_factor = 1.0 / math.sqrt(HEAD_DIM)
    flat = lambda w: w.reshape(-1, width)
    ada_low = flat(w_ada).astype(BF)
    qkv_low = flat(w_qkv).astype(BF)
    proj_low = w_proj.astype(BF)
    up_bias = biases[9:13].reshape(-1)

    cond_act, silu_pull = jax.vjp(jax.nn.silu, condition.astype(F32))
    cond_low = cond_act.astype(BF)
    mod_part = dot_t(cond_low, ada_low).reshape(latent_count * 6, quarter) + jnp.tile(
        biases[0:6], (latent_count, 1)
    )
    mod_part = jnp.concatenate([mod_part, biases[8:9], biases[13:14]], axis=0)
    gathered = collect(mod_part[None])
    gathered = reorder(gathered, size, me)
    gathered = jnp.moveaxis(gathered, 0, 1).reshape(-1, width)
    modulation = reorder(gathered[: latent_count * 6], latent_count, my_latent).reshape(
        latent_count, 6, width
    )
    bias_proj = gathered[latent_count * 6]
    bias_down = gathered[latent_count * 6 + 1]
    shift_first, scale_first, gate_first = modulation[0, 0], modulation[0, 1], modulation[0, 2]
    shift_second, scale_second, gate_second = modulation[0, 3], modulation[0, 4], modulation[0, 5]

    tokens_in = reorder(inputs.reshape(tokens, width), size, me)
    tangent = reorder(cotangent.reshape(tokens, width), size, me)
    partial_first, first_low, heads, attended_low = attention(
        tokens_in, modulation, qkv_low, proj_low, biases[6:8], seq_length
    )
    partial_first, w_up, w_down, cond_low = lax.optimization_barrier(
        (partial_first, w_up, w_down, cond_low)
    )
    cond_all = dp_collect(cond_low).reshape(-1, width)
    up_low = flat(w_up).astype(BF)
    down_low = flat(w_down).astype(BF)
    own = tokens_in[:chunk].astype(F32)
    tangent_own = tangent[:chunk].astype(F32)

    branch_first = scatter_sum(partial_first) + bias_proj
    middle = own + gate_first * branch_first
    normed_second, inverse_second = normed_of(middle)
    second_low = collect((normed_second * (1.0 + scale_second) + shift_second).astype(BF))

    d_branch_second = (
        tangent.astype(F32).reshape(latent_count, seq_length, width)
        * modulation[:, 5][:, None, :]
    ).reshape(tokens, width)
    d_down_bias = jnp.sum(d_branch_second, axis=0)
    d_second_low = d_branch_second.astype(BF)
    act_low, d_pre_low, second_part, d_up_bias = feed_forward(
        second_low, d_second_low, up_low, down_low, up_bias[None]
    )
    d_up_bias = d_up_bias.reshape(-1, quarter)
    partial_second = dot(act_low, down_low)
    second_latents = partial_second.reshape(latent_count, seq_length, width)
    d_gate_second = jnp.sum(
        tangent.astype(F32).reshape(second_latents.shape) * second_latents, axis=1
    )
    d_gate_second = d_gate_second.at[0].add(bias_down * jnp.sum(tangent_own, axis=0))
    output_part = (second_latents * modulation[:, 5][:, None, :]).reshape(tokens, width)
    output_part = jnp.concatenate(
        [output_part[:chunk] + (middle + gate_second * bias_down), output_part[chunk:]], axis=0
    ).astype(BF)

    d_hidden_second = scatter_sum(second_part)
    (
        d_hidden_second,
        momentum_ada,
        momentum_qkv,
        momentum_proj,
        momentum_up,
        momentum_down,
        w_ada_old,
        w_qkv_old,
        w_proj_old,
        w_up_old,
        w_down_old,
    ) = lax.optimization_barrier(
        (
            d_hidden_second,
            momentum_ada,
            momentum_qkv,
            momentum_proj,
            momentum_up,
            momentum_down,
            w_ada,
            w_qkv,
            w_proj,
            w_up,
            w_down,
        )
    )

    grad_down = t_dot(act_low, d_second_low).astype(BF)
    grad_up = t_dot(d_pre_low, second_low).astype(BF)
    grad_up, grad_down = lax.psum((grad_up, grad_down), "dp")

    d_shift_second = jnp.sum(d_hidden_second, axis=0)
    d_scale_second = jnp.sum(d_hidden_second * normed_second, axis=0)
    d_middle = tangent_own + norm_back(
        normed_second, inverse_second, d_hidden_second * (1.0 + scale_second)
    )
    d_branch_first = gate_first * d_middle
    d_gate_first = jnp.sum(d_middle * branch_first, axis=0)
    d_proj_bias = jnp.sum(d_branch_first, axis=0)
    d_first_low = collect(d_branch_first.astype(BF))

    grad_proj = t_dot(attended_low, d_first_low).astype(BF)
    d_heads, first_part, d_head_sums = attention_back(
        d_first_low, heads, qkv_low, proj_low, seq_length
    )
    d_head_bias = jnp.sum(d_head_sums, axis=0)
    grad_qkv = jnp.concatenate([t_dot(d_heads[k], first_low) for k in range(3)], axis=0).astype(BF)
    first_pieces = scatter(first_part)
    late_grads = dp_gather(dp_reduce(jnp.concatenate([grad_qkv, grad_proj], axis=0)))
    grad_qkv, grad_proj = late_grads[: 3 * quarter], late_grads[3 * quarter :]

    block_rows = len(blocks_of(width // TILE)) * TILE
    none = jnp.zeros((block_rows, TILE), F32)
    moment_qkv = MUON_MOMENTUM * flat(momentum_qkv) + grad_qkv.astype(F32)
    start_qkv = moment_qkv.astype(BF)
    late = lax.cond(dp_rank == OWNERS[1], gram_blocks, lambda rows: none, start_qkv)
    late, grad_up, grad_down = lax.optimization_barrier((late, grad_up, grad_down))
    late = scatter(reorder(late, size, me), OWNERS[1:2])
    moment_up = MUON_MOMENTUM * flat(momentum_up) + grad_up.astype(F32)
    moment_down = MUON_MOMENTUM * flat(momentum_down) + grad_down.astype(F32)
    start_up, start_down = moment_up.astype(BF), moment_down.astype(BF)
    turn = jnp.int32(0)
    for place, matrix_index in enumerate((0, 3, 4)):
        turn = jnp.where(dp_rank == OWNERS[matrix_index], place + 1, turn)
    early = lax.switch(
        turn,
        [lambda *rows: none] + [(lambda *rows, k=k: gram_blocks(rows[k])) for k in range(3)],
        flat(momentum_ada),
        start_up,
        start_down,
    )
    early, first_pieces, grad_proj = lax.optimization_barrier((early, first_pieces, grad_proj))
    early_ranks = [OWNERS[k] for k in (0, 3, 4)]
    early = scatter(reorder(early, size, me), early_ranks)
    moment_proj = MUON_MOMENTUM * momentum_proj + grad_proj.astype(F32)
    start_proj = moment_proj.astype(BF)
    proj_rows = collect(start_proj, OWNERS[2:3])
    d_hidden_first = total(first_pieces)

    normed_own, inverse_own = normed_of(own)
    d_shift_first = jnp.sum(d_hidden_first, axis=0)
    d_scale_first = jnp.sum(d_hidden_first * normed_own, axis=0)
    grad_inputs = d_middle + norm_back(
        normed_own, inverse_own, d_hidden_first * (1.0 + scale_first)
    )
    grad_inputs = grad_inputs.astype(BF)

    sums = jnp.stack(
        [
            d_shift_first,
            d_scale_first,
            d_gate_first,
            d_shift_second,
            d_scale_second,
            d_proj_bias,
            *d_gate_second,
        ]
    )
    of_device = [
        lax.dynamic_slice_in_dim(sums, (me ^ mask) * quarter, quarter, 1) for mask in range(size)
    ]
    arrived = jnp.stack(
        [of_device[0]] + [swap(of_device[mask], mask) for mask in range(1, size)]
    )
    d_proj_own = jnp.sum(arrived[:, 5], axis=0)
    per_latent = size // latent_count
    d_gate_own = [
        sum(arrived[mask, 6 + (q ^ (mask // per_latent))] for mask in range(size))
        for q in range(latent_count)
    ]
    d_mod_own = jnp.sum(
        arrived[:, :5].reshape(latent_count, per_latent, 5, quarter), axis=1
    )
    d_mod_own = jnp.concatenate([d_mod_own, jnp.stack(d_gate_own)[:, None]], axis=1)
    d_mod_own = reorder(d_mod_own, latent_count, my_latent)
    d_cond_part = dot(
        d_mod_own.reshape(latent_count, -1).astype(BF), flat(w_ada_old).astype(BF)
    )
    d_down_own = lax.dynamic_slice_in_dim(d_down_bias, me * quarter, quarter, 0)
    small = jnp.concatenate(
        [
            d_mod_own.reshape(-1, quarter),
            d_head_bias,
            d_proj_own[None],
            d_up_bias,
            d_down_own[None],
        ],
        axis=0,
    )
    small_all = dp_collect(small)
    d_mod_all = small_all[:, : 6 * latent_count].reshape(-1, 6, quarter)
    grad_biases = jnp.concatenate(
        [jnp.sum(d_mod_all, axis=0), jnp.sum(small_all[:, 6 * latent_count :], axis=0)], axis=0
    )
    d_mod_low = d_mod_all.reshape(d_mod_all.shape[0], -1).astype(BF)
    grad_ada = t_dot(d_mod_low, cond_all)

    cross = jnp.dot(
        d_mod_low.astype(F32), flat(momentum_ada), precision=lax.Precision.HIGHEST
    )
    summed = jnp.concatenate([d_cond_part, cross, dot_t(d_mod_low, d_mod_low) @ jnp.eye(d_mod_low.shape[0], width, dtype=F32)], axis=0)
    summed = sum([swap(summed, mask) for mask in range(1, size)], summed)
    d_cond_act, cross, square = (
        summed[:latent_count],
        summed[latent_count : latent_count + d_mod_low.shape[0]],
        summed[latent_count + d_mod_low.shape[0] :, : d_mod_low.shape[0]],
    )
    grad_condition = silu_pull(d_cond_act)[0]
    corr = MUON_MOMENTUM * cross + 0.5 * jnp.dot(
        square, cond_all.astype(F32), precision=lax.Precision.HIGHEST
    )
    corr = jnp.where(dp_rank == OWNERS[0], corr, 0.0)

    moment_ada = MUON_MOMENTUM * flat(momentum_ada) + grad_ada
    moments = (moment_ada, moment_qkv, moment_proj, moment_up, moment_down)
    starts = (moment_ada.astype(BF), start_qkv, start_proj, start_up, start_down)

    late = collect(total(late), OWNERS[1:2])
    early = collect(total(early), early_ranks)
    proj_gram = lax.cond(dp_rank == OWNERS[2], gram_blocks, lambda rows: none, proj_rows)
    coefficient = jnp.where(dp_rank == OWNERS[0], MUON_MOMENTUM**2, 1.0)
    gram = reorder(jnp.where(dp_rank == OWNERS[1], late, early * coefficient), size, me)
    gram = jnp.where(dp_rank == OWNERS[2], proj_gram, gram)
    gram, output_part, grad_inputs = lax.optimization_barrier((gram, output_part, grad_inputs))
    output = scatter_sum(output_part).astype(BF)
    grad_inputs = collect(grad_inputs)
    factor = newton_schulz_factor(gram, cond_all, corr, width)
    factor, output, grad_inputs = lax.optimization_barrier((factor, output, grad_inputs))
    output = reorder(collect(output), size, me).reshape(inputs.shape)
    grad_inputs = reorder(grad_inputs, size, me).reshape(inputs.shape)
    column_width = width // dp_size
    column_start = dp_rank * column_width
    factors = lax.all_to_all(
        factor.reshape(dp_size, column_width, width), "dp", 0, 0, tiled=True
    )

    weights_old = (w_ada_old, w_qkv_old, w_proj_old, w_up_old, w_down_old)
    sizes = [max(w.size // width * size, width) for w in weights_old]
    columns = [
        lax.dynamic_slice_in_dim(flat(w), column_start, column_width, 1) for w in weights_old
    ]
    new_weights = update_weights(starts, columns, factors, sizes)
    new_weights = [
        new.reshape(old.shape[:-1] + (column_width,))
        for new, old in zip(new_weights, weights_old)
    ]
    new_bias_first = BETA_ONE * bias_first + (1.0 - BETA_ONE) * grad_biases
    new_bias_second = BETA_TWO * bias_second + (1.0 - BETA_TWO) * grad_biases * grad_biases
    first_hat = new_bias_first / (1.0 - BETA_ONE**STEP)
    second_hat = new_bias_second / (1.0 - BETA_TWO**STEP)
    new_biases = biases - ADAM_RATE * first_hat / (jnp.sqrt(second_hat) + ADAM_EPS)
    return (
        output,
        grad_inputs,
        grad_condition,
        *new_weights,
        moments[0].reshape(momentum_ada.shape),
        moments[1].reshape(momentum_qkv.shape),
        moments[2],
        moments[3].reshape(momentum_up.shape),
        moments[4].reshape(momentum_down.shape),
        new_biases,
        new_bias_first,
        new_bias_second,
    )


def solution(mesh):
    placed = (
        P("dp", None, None),
        P("dp", None),
        P("dp", None, None),
        P(None, "tensor", None),
        P(None, "tensor", None),
        P("tensor", None),
        P(None, "tensor", None),
        P(None, "tensor", None),
        P(None, "tensor"),
        P(None, "tensor", None),
        P(None, "tensor", None),
        P("tensor", None),
        P(None, "tensor", None),
        P(None, "tensor", None),
        P(None, "tensor"),
        P(None, "tensor"),
    )
    return jax.shard_map(
        on_device,
        mesh=mesh,
        in_specs=placed,
        out_specs=(
            P("dp", None, None),
            P("dp", None, None),
            P("dp", None),
            P(None, "tensor", "dp"),
            P(None, "tensor", "dp"),
            P("tensor", "dp"),
            P(None, "tensor", "dp"),
            P(None, "tensor", "dp"),
            P(None, "tensor", None),
            P(None, "tensor", None),
            P("tensor", None),
            P(None, "tensor", None),
            P(None, "tensor", None),
            P(None, "tensor"),
            P(None, "tensor"),
            P(None, "tensor"),
        ),
        check_vma=False,
    )
```

```python
import functools
import math

import jax
import jax.numpy as jnp
from jax import lax
from jax.experimental import pallas as pl
from jax.experimental.pallas import tpu as pltpu
from jax.sharding import PartitionSpec as P

HEAD_DIM = 64
NS_ITERS = 5
STEP = 10


NS_A = 3.4445
NS_B = -4.775
NS_C = 2.0315
MUON_RATE = 0.16
MUON_DECAY = 0.01
MUON_MOMENTUM = 0.95
ADAM_RATE = 0.25
BETA_ONE = 0.9
BETA_TWO = 0.999
ADAM_EPS = 1e-08
NORM_EPS = 1e-06

BF = jnp.bfloat16
F32 = jnp.float32
TILE = 256
HALF = 128
VMEM_LIMIT = 28 * 1024 * 1024
OWNERS = (0, 2, 5, 4, 6)


def dot(a, b):
    return jnp.dot(a, b, preferred_element_type=F32)


def dot_t(a, b):
    return lax.dot_general(a, b, (((1,), (1,)), ((), ())), preferred_element_type=F32)


def t_dot(a, b):
    return lax.dot_general(a, b, (((0,), (0,)), ((), ())), preferred_element_type=F32)


def parts(value):
    high = value.astype(BF)
    return high, (value - high.astype(F32)).astype(BF)


def blocks_of(count):
    return [(i, j) for i in range(count) for j in range(i, count)]


def half_blocks(count):
    return [(i, j, half) for i, j in blocks_of(count) for half in range(2)]


def half_rows(index, total, me_ref, size):
    per_chunk = total // size
    place = (index // per_chunk) ^ me_ref[0]
    return pl.ds(pl.multiple_of(place * (per_chunk * HALF) + index % per_chunk * HALF, HALF), HALF)


def gram_kernel(size, me_ref, *refs):
    out_ref = refs[-1]
    count = refs[0].shape[1] // TILE
    halves = half_blocks(count)
    for index, (i, j, half) in enumerate(halves):
        left = slice(i * TILE + half * HALF, i * TILE + (half + 1) * HALF)
        right = slice(j * TILE, (j + 1) * TILE)
        block = sum(
            t_dot(ref[:, left].astype(BF), ref[:, right].astype(BF)) for ref in refs[:-1]
        )
        out_ref[half_rows(index, len(halves), me_ref, size), :] = block


def gram_blocks(me, *rows):
    width = rows[0].shape[1]
    depth = sum(r.shape[0] for r in rows)
    count = len(half_blocks(width // TILE))
    return pl.pallas_call(
        functools.partial(gram_kernel, lax.axis_size("tensor")),
        in_specs=[pl.BlockSpec(memory_space=pltpu.SMEM)]
        + [pl.BlockSpec(memory_space=pltpu.VMEM)] * len(rows),
        out_shape=jax.ShapeDtypeStruct((count * HALF, TILE), F32),
        compiler_params=pltpu.CompilerParams(vmem_limit_bytes=VMEM_LIMIT),
        cost_estimate=pl.CostEstimate(
            flops=2 * depth * width * width, bytes_accessed=depth * width * 6, transcendentals=0
        ),
    )(me, *rows)


def newton_schulz_kernel(
    size, me_ref, blocks_ref, out_ref, cur, high, rest, poly, mid_h, mid_l, f_h, f_l, g_h, g_l
):
    width = cur.shape[0]
    spans = [slice(i * TILE, (i + 1) * TILE) for i in range(width // TILE)]
    halves = half_blocks(width // TILE)
    for index, (i, j, half) in enumerate(halves):
        block = blocks_ref[half_rows(index, len(halves), me_ref, size), :]
        left = slice(i * TILE + half * HALF, i * TILE + (half + 1) * HALF)
        cur[left, spans[j]] = block
        if i != j:
            cur[spans[j], left] = block.T
    square_norm = jnp.zeros((1, 1), F32)
    row = lax.broadcasted_iota(jnp.int32, (TILE, TILE), 0)
    col = lax.broadcasted_iota(jnp.int32, (TILE, TILE), 1)
    for span in spans:
        square_norm += jnp.sum(jnp.where(row == col, cur[span, span], 0.0), keepdims=True)
    scale = 1.0 / (jnp.sqrt(square_norm) + 1e-07)
    for span in spans:
        cur[span, :] = cur[span, :] * (scale * scale)

    def make_poly():
        for span in spans:
            high[span, :], rest[span, :] = parts(cur[span, :])
        for span in spans:
            poly[span, :] = (NS_B * cur[span, :] + NS_C * dot(high[span, :], high[...])).astype(BF)

    def step_gram():
        for span in spans:
            half = (
                NS_A * cur[span, :] + dot(high[span, :], poly[...]) + dot(rest[span, :], poly[...])
            )
            mid_h[span, :], mid_l[span, :] = parts(half)
        for span in spans:
            half = mid_h[span, :].astype(F32) + mid_l[span, :].astype(F32)
            cur[span, :] = (
                NS_A * half + dot(poly[span, :], mid_h[...]) + dot(poly[span, :], mid_l[...])
            )

    def stepped_factor(span):
        before = f_h[span, :].astype(F32) + f_l[span, :].astype(F32)
        return NS_A * before + dot(poly[span, :], f_h[...]) + dot(poly[span, :], f_l[...])

    make_poly()
    wide_row = lax.broadcasted_iota(jnp.int32, (TILE, width), 0)
    wide_col = lax.broadcasted_iota(jnp.int32, (TILE, width), 1)
    for i, span in enumerate(spans):
        start = poly[span, :].astype(F32) + jnp.where(wide_row + i * TILE == wide_col, NS_A, 0.0)
        f_h[span, :], f_l[span, :] = parts(start)
    step_gram()

    def middle(_, carry):
        make_poly()
        for span in spans:
            g_h[span, :], g_l[span, :] = parts(stepped_factor(span))
        f_h[...] = g_h[...]
        f_l[...] = g_l[...]
        step_gram()
        return carry

    lax.fori_loop(0, NS_ITERS - 2, middle, 0)
    make_poly()
    for span in spans:
        out_ref[span, :] = (stepped_factor(span) * scale).astype(out_ref.dtype)


def newton_schulz_factor(me, blocks, width):
    whole = lambda kind: pltpu.VMEM((width, width), kind)
    return pl.pallas_call(
        functools.partial(newton_schulz_kernel, lax.axis_size("tensor")),
        in_specs=[
            pl.BlockSpec(memory_space=pltpu.SMEM),
            pl.BlockSpec(memory_space=pltpu.VMEM),
        ],
        out_shape=jax.ShapeDtypeStruct((width, width), BF),
        scratch_shapes=[whole(F32)] + [whole(BF)] * 9,
        compiler_params=pltpu.CompilerParams(vmem_limit_bytes=VMEM_LIMIT),
        cost_estimate=pl.CostEstimate(
            flops=2 * 29 * width**3, bytes_accessed=width * width * 6, transcendentals=0
        ),
    )(me, blocks)


def update_kernel(sizes, *refs):
    count = len(sizes)
    rows, weights, factor, outs = refs[:count], refs[count : 2 * count], refs[2 * count], refs[2 * count + 1 :]
    for k, size in enumerate(sizes):
        ortho = dot_t(rows[k][...], factor[OWNERS[k]])
        outs[k][...] = (
            weights[k][...] * (1.0 - MUON_RATE * MUON_DECAY)
            - MUON_RATE * 0.2 * math.sqrt(size) * ortho
        )


def update_weights(rows, weights, factors, sizes):
    return pl.pallas_call(
        functools.partial(update_kernel, sizes),
        out_shape=[jax.ShapeDtypeStruct(w.shape, F32) for w in weights],
        compiler_params=pltpu.CompilerParams(vmem_limit_bytes=VMEM_LIMIT),
        cost_estimate=pl.CostEstimate(
            flops=sum(2 * r.size * w.shape[1] for r, w in zip(rows, weights)),
            bytes_accessed=sum(2 * r.size + 12 * w.size for r, w in zip(rows, weights)),
            transcendentals=0,
        ),
    )(*rows, *weights, factors)


def put_pieces(refs, value):
    step, steps = pl.program_id(0), pl.num_programs(0)
    rows = refs[0].shape[0]
    per_step = value.shape[0] // rows
    for index, ref in enumerate(refs):
        k = index % per_step

        @pl.when(step == index // per_step)
        def _(ref=ref, k=k):
            ref[...] = value[k * rows : (k + 1) * rows, :]


def take_pieces(refs, scratch):
    step = pl.program_id(0)
    rows = refs[0].shape[0]
    per_step = scratch.shape[0] // rows
    for index, ref in enumerate(refs):
        k = index % per_step

        @pl.when(step == index // per_step)
        def _(ref=ref, k=k):
            scratch[k * rows : (k + 1) * rows, :] = ref[...]


def attention_kernel(
    count, x_ref, mod_ref, w_ref, proj_ref, bias_ref, hidden_ref, heads_ref, attended_ref, *partial_refs
):
    quarter = proj_ref.shape[0]
    normed, _ = normed_of(x_ref[...].astype(F32))
    hidden = (normed * (1.0 + mod_ref[0, 1:2, :]) + mod_ref[0, 0:1, :]).astype(BF)
    hidden_ref[...] = hidden
    queries = (dot_t(hidden, w_ref[:quarter, :]) + bias_ref[0:1, :]).astype(BF)
    keys = dot_t(hidden, w_ref[quarter : 2 * quarter, :]).astype(BF)
    values = (dot_t(hidden, w_ref[2 * quarter :, :]) + bias_ref[1:2, :]).astype(BF)
    heads_ref[0] = queries
    heads_ref[1] = keys
    heads_ref[2] = values
    attended = []
    for start in range(0, quarter, HEAD_DIM):
        head = slice(start, start + HEAD_DIM)
        probs = softmax_of(queries[:, head], keys[:, head]).astype(BF)
        attended.append(dot(probs, values[:, head]))
    attended = jnp.concatenate(attended, axis=1).astype(BF)
    attended_ref[...] = attended
    put_pieces(partial_refs, dot(attended, proj_ref[...]).astype(BF))


def softmax_of(queries, keys):
    scores = dot_t(queries, keys) * (1.0 / math.sqrt(HEAD_DIM))
    raised = jnp.exp(scores - jnp.max(scores, axis=-1, keepdims=True))
    return raised * (1.0 / jnp.sum(raised, axis=-1, keepdims=True))


def attention(tokens_in, modulation, qkv_low, proj_low, bias_rows, seq_length, count):
    tokens, width = tokens_in.shape
    quarter = proj_low.shape[0]
    rows = lambda last: pl.BlockSpec((seq_length, last), lambda i: (i, 0))
    whole = lambda shape: pl.BlockSpec(shape, lambda i: (0,) * len(shape))
    piece = (tokens // count, width)
    out = pl.pallas_call(
        functools.partial(attention_kernel, count),
        grid=(tokens // seq_length,),
        in_specs=[
            rows(width),
            pl.BlockSpec((1, 6, width), lambda i: (i, 0, 0)),
            whole(qkv_low.shape),
            whole(proj_low.shape),
            whole(bias_rows.shape),
        ],
        out_specs=[
            rows(width),
            pl.BlockSpec((3, seq_length, quarter), lambda i: (0, i, 0)),
            rows(quarter),
        ]
        + [whole(piece)] * count,
        out_shape=[
            jax.ShapeDtypeStruct((tokens, width), BF),
            jax.ShapeDtypeStruct((3, tokens, quarter), BF),
            jax.ShapeDtypeStruct((tokens, quarter), BF),
        ]
        + [jax.ShapeDtypeStruct(piece, BF)] * count,
        compiler_params=pltpu.CompilerParams(vmem_limit_bytes=VMEM_LIMIT),
        cost_estimate=pl.CostEstimate(
            flops=8 * tokens * width * quarter + 4 * tokens * seq_length * quarter,
            bytes_accessed=tokens * width * 8 + qkv_low.size * 3,
            transcendentals=tokens * seq_length * quarter // HEAD_DIM,
        ),
    )(tokens_in, modulation, qkv_low, proj_low, bias_rows)
    return out[0], out[1], out[2], out[3:]


def attention_back_kernel(count, heads_ref, w_ref, proj_ref, *refs):
    grad_refs, (d_heads_ref, sums_ref) = refs[:count], refs[count : count + 2]
    part_refs, grad = refs[count + 2 : -1], refs[-1]
    take_pieces(grad_refs, grad)
    quarter = proj_ref.shape[0]
    scale = 1.0 / math.sqrt(HEAD_DIM)
    d_attended = dot_t(grad[...], proj_ref[...]).astype(BF)
    queries, keys, values = heads_ref[0], heads_ref[1], heads_ref[2]
    d_queries, d_keys, d_values = [], [], []
    for start in range(0, quarter, HEAD_DIM):
        head = slice(start, start + HEAD_DIM)
        probs = softmax_of(queries[:, head], keys[:, head])
        d_out = d_attended[:, head]
        d_values.append(t_dot(probs.astype(BF), d_out))
        d_probs = dot_t(d_out, values[:, head])
        d_scores = (
            probs * (d_probs - jnp.sum(probs * d_probs, axis=-1, keepdims=True))
        ).astype(BF)
        d_queries.append(dot(d_scores, keys[:, head]) * scale)
        d_keys.append(t_dot(d_scores, queries[:, head]) * scale)
    d_queries = jnp.concatenate(d_queries, axis=1)
    d_values = jnp.concatenate(d_values, axis=1)
    sums_ref[0, 0:1, :] = jnp.sum(d_queries, axis=0, keepdims=True)
    sums_ref[0, 1:2, :] = jnp.sum(d_values, axis=0, keepdims=True)
    d_queries = d_queries.astype(BF)
    d_keys = jnp.concatenate(d_keys, axis=1).astype(BF)
    d_values = d_values.astype(BF)
    d_heads_ref[0] = d_queries
    d_heads_ref[1] = d_keys
    d_heads_ref[2] = d_values
    part = (
        dot(d_queries, w_ref[:quarter, :])
        + dot(d_keys, w_ref[quarter : 2 * quarter, :])
        + dot(d_values, w_ref[2 * quarter :, :])
    )
    put_pieces(part_refs, part.astype(BF))


def attention_back(grads, heads, qkv_low, proj_low, seq_length):
    count = len(grads)
    rows, width = grads[0].shape
    tokens = rows * count
    quarter = proj_low.shape[0]
    whole = lambda shape: pl.BlockSpec(shape, lambda i: (0,) * len(shape))
    of_heads = pl.BlockSpec((3, seq_length, quarter), lambda i: (0, i, 0))
    out = pl.pallas_call(
        functools.partial(attention_back_kernel, count),
        grid=(tokens // seq_length,),
        in_specs=[of_heads, whole(qkv_low.shape), whole(proj_low.shape)]
        + [whole(grads[0].shape)] * count,
        out_specs=[of_heads, pl.BlockSpec((1, 2, quarter), lambda i: (i, 0, 0))]
        + [whole(grads[0].shape)] * count,
        out_shape=[
            jax.ShapeDtypeStruct(heads.shape, BF),
            jax.ShapeDtypeStruct((tokens // seq_length, 2, quarter), F32),
        ]
        + [jax.ShapeDtypeStruct(grads[0].shape, BF)] * count,
        scratch_shapes=[pltpu.VMEM((seq_length, width), BF)],
        compiler_params=pltpu.CompilerParams(vmem_limit_bytes=VMEM_LIMIT),
        cost_estimate=pl.CostEstimate(
            flops=8 * tokens * width * quarter + 10 * tokens * seq_length * quarter,
            bytes_accessed=tokens * width * 8 + qkv_low.size * 3,
            transcendentals=tokens * seq_length * quarter // HEAD_DIM,
        ),
    )(heads, qkv_low, proj_low, *grads)
    return out[0], out[1], out[2:]


def feed_forward_kernel(count, grad_ref, up_ref, down_ref, bias_ref, *refs):
    hidden_refs, (act_ref, d_pre_ref, sums_ref) = refs[:count], refs[count : count + 3]
    part_refs, hidden = refs[count + 3 : -1], refs[-1]
    take_pieces(hidden_refs, hidden)
    pre = dot_t(hidden[...], up_ref[...]) + bias_ref[...]
    d_act = dot_t(grad_ref[...], down_ref[...])
    root = math.sqrt(2.0 / math.pi)
    square = pre * pre
    bent = jnp.tanh(root * pre * (1.0 + 0.044715 * square))
    half = 0.5 * (1.0 + bent)
    act_ref[...] = (pre * half).astype(BF)
    slope = half + 0.5 * pre * (1.0 - bent * bent) * (root * (1.0 + 0.134145 * square))
    d_pre = d_act * slope

    @pl.when(pl.program_id(0) == 0)
    def _():
        sums_ref[...] = jnp.zeros_like(sums_ref)

    sums_ref[...] += jnp.sum(d_pre, axis=0, keepdims=True)
    d_pre = d_pre.astype(BF)
    d_pre_ref[...] = d_pre
    put_pieces(part_refs, dot(d_pre, up_ref[...]).astype(BF))


def feed_forward(hidden, grad, up_low, down_low, bias):
    count = len(hidden)
    tokens, width = grad.shape
    units = up_low.shape[0]
    block = tokens // 2
    rows = lambda last: pl.BlockSpec((block, last), lambda i: (i, 0))
    whole = lambda shape: pl.BlockSpec(shape, lambda i: (0,) * len(shape))
    out = pl.pallas_call(
        functools.partial(feed_forward_kernel, count),
        grid=(tokens // block,),
        in_specs=[rows(width), whole(up_low.shape), whole(down_low.shape), whole((1, units))]
        + [whole(hidden[0].shape)] * count,
        out_specs=[rows(units), rows(units), whole((1, units))]
        + [whole(hidden[0].shape)] * count,
        out_shape=[
            jax.ShapeDtypeStruct((tokens, units), BF),
            jax.ShapeDtypeStruct((tokens, units), BF),
            jax.ShapeDtypeStruct((1, units), F32),
        ]
        + [jax.ShapeDtypeStruct(hidden[0].shape, BF)] * count,
        scratch_shapes=[pltpu.VMEM((block, width), BF)],
        compiler_params=pltpu.CompilerParams(vmem_limit_bytes=VMEM_LIMIT),
        cost_estimate=pl.CostEstimate(
            flops=6 * tokens * width * units,
            bytes_accessed=tokens * width * 10 + up_low.size * 4,
            transcendentals=tokens * units,
        ),
    )(grad, up_low, down_low, bias, *hidden)
    return out[0], out[1], out[2], out[3:]


def dp_swap(piece, mask):
    return lax.ppermute(piece, "dp", [(i, i ^ mask) for i in range(lax.axis_size("dp"))])


def dp_levels():
    size, step, levels = lax.axis_size("dp"), 2, []
    while step < size:
        radix = min(4, size // step)
        levels.append((step, radix))
        step *= radix
    return levels + [(1, 2)]


def dp_masks():
    masks = [0]
    for step, radix in dp_levels():
        masks = [j * step + mask for j in range(radix) for mask in masks]
    return masks


def dp_collect(piece, levels=None):
    gathered = piece[None]
    for step, radix in dp_levels() if levels is None else levels:
        gathered = jnp.concatenate(
            [gathered] + [dp_swap(gathered, j * step) for j in range(1, radix)], axis=0
        )
    return gathered


def dp_scatter_sum(value):
    for step, radix in reversed(dp_levels()):
        value = value.reshape((radix, -1) + value.shape[1:])
        total = value[0].astype(F32)
        for j in range(1, radix):
            total = total + dp_swap(value[j], j * step).astype(F32)
        value = total.astype(BF)
    return value[0]


def dp_reduce(value):
    size = lax.axis_size("dp")
    value = reorder(value, dp_masks(), place_of("dp"))
    return dp_scatter_sum(value.reshape((size, -1) + value.shape[1:]))


def dp_places():
    masks, rank = dp_masks(), place_of("dp")
    place, bit = jnp.uint32(0), 0
    while 1 << bit < len(masks):
        place = place | (((rank >> bit) & 1) * masks.index(1 << bit))
        bit += 1
    return [masks.index(p) for p in range(len(masks))], place


def place_of(axis):
    return lax.axis_index(axis).astype(jnp.uint32)


def swap(piece, mask, ranks=None):
    size = lax.axis_size("tensor")
    if ranks is None:
        return lax.ppermute(piece, "tensor", [(i, i ^ mask) for i in range(size)])
    pairs = [(r * size + i, r * size + (i ^ mask)) for r in ranks for i in range(size)]
    return lax.ppermute(piece, ("dp", "tensor"), pairs)


def split(value, count):
    rows = value.shape[0] // count
    return [value[k * rows : (k + 1) * rows] for k in range(count)]


def scatter(pieces, ranks=None):
    return [pieces[0]] + [swap(pieces[mask], mask, ranks) for mask in range(1, len(pieces))]


def total(pieces):
    return sum([piece.astype(F32) for piece in pieces[1:]], pieces[0].astype(F32))


def collect(piece, ranks=None):
    size = lax.axis_size("tensor")
    return [piece] + [swap(piece, mask, ranks) for mask in range(1, size)]


def reorder(value, masks, index):
    masks = list(range(masks)) if isinstance(masks, int) else masks
    rows = value.shape[0] // len(masks)
    return jnp.concatenate(
        [lax.dynamic_slice_in_dim(value, (index ^ p) * rows, rows, 0) for p in masks], axis=0
    )


def normed_of(values):
    average = jnp.mean(values, axis=-1, keepdims=True)
    centered = values - average
    variance = jnp.mean(centered * centered, axis=-1, keepdims=True)
    inverse = lax.rsqrt(variance + NORM_EPS)
    return centered * inverse, inverse


def norm_back(normed, inverse, grad):
    return (
        grad
        - jnp.mean(grad, axis=-1, keepdims=True)
        - normed * jnp.mean(grad * normed, axis=-1, keepdims=True)
    ) * inverse


def on_device(
    inputs,
    condition,
    cotangent,
    w_ada,
    w_qkv,
    w_proj,
    w_up,
    w_down,
    biases,
    momentum_ada,
    momentum_qkv,
    momentum_proj,
    momentum_up,
    momentum_down,
    bias_first,
    bias_second,
):
    quarter = w_ada.shape[1]
    width = w_ada.shape[-1]
    latent_count = inputs.shape[0]
    seq_length = inputs.shape[1]
    tokens = latent_count * seq_length
    heads_here = quarter // HEAD_DIM
    size = lax.axis_size("tensor")
    me = place_of("tensor")
    dp_size = lax.axis_size("dp")
    dp_rank = place_of("dp")
    chunk = tokens // size
    my_latent = me // (size // latent_count)
    scale_factor = 1.0 / math.sqrt(HEAD_DIM)
    flat = lambda w: w.reshape(-1, width)
    ada_low = flat(w_ada).astype(BF)
    qkv_low = flat(w_qkv).astype(BF)
    proj_low = w_proj.astype(BF)
    up_bias = biases[9:13].reshape(-1)

    cond_act, silu_pull = jax.vjp(jax.nn.silu, condition.astype(F32))
    cond_low = cond_act.astype(BF)
    mod_part = dot_t(cond_low, ada_low).reshape(latent_count * 6, quarter) + jnp.tile(
        biases[0:6], (latent_count, 1)
    )
    mod_part = jnp.concatenate([mod_part, biases[8:9], biases[13:14]], axis=0)
    gathered = jnp.concatenate(collect(mod_part[None]), axis=0)
    gathered = reorder(gathered, size, me)
    gathered = jnp.moveaxis(gathered, 0, 1).reshape(-1, width)
    modulation = reorder(gathered[: latent_count * 6], latent_count, my_latent).reshape(
        latent_count, 6, width
    )
    bias_proj = gathered[latent_count * 6]
    bias_down = gathered[latent_count * 6 + 1]
    shift_first, scale_first, gate_first = modulation[0, 0], modulation[0, 1], modulation[0, 2]
    shift_second, scale_second, gate_second = modulation[0, 3], modulation[0, 4], modulation[0, 5]

    tokens_in = reorder(inputs.reshape(tokens, width), size, me)
    tangent = reorder(cotangent.reshape(tokens, width), size, me)
    first_low, heads, attended_low, partial_first = attention(
        tokens_in, modulation, qkv_low, proj_low, biases[6:8], seq_length, size
    )
    partial_first, w_up, w_down = lax.optimization_barrier((partial_first, w_up, w_down))
    up_low = flat(w_up).astype(BF)
    down_low = flat(w_down).astype(BF)
    own = tokens_in[:chunk].astype(F32)
    tangent_own = tangent[:chunk].astype(F32)

    branch_first = total(scatter(partial_first)) + bias_proj
    middle = own + gate_first * branch_first
    normed_second, inverse_second = normed_of(middle)
    second_pieces = collect((normed_second * (1.0 + scale_second) + shift_second).astype(BF))

    d_branch_second = (
        tangent.astype(F32).reshape(latent_count, seq_length, width)
        * modulation[:, 5][:, None, :]
    ).reshape(tokens, width)
    d_down_bias = jnp.sum(d_branch_second, axis=0)
    d_second_low = d_branch_second.astype(BF)
    act_low, d_pre_low, d_up_bias, second_part = feed_forward(
        second_pieces, d_second_low, up_low, down_low, up_bias[None]
    )
    second_low = jnp.concatenate(second_pieces, axis=0)
    d_up_bias = d_up_bias.reshape(-1, quarter)
    partial_second = dot(act_low, down_low)
    second_latents = partial_second.reshape(latent_count, seq_length, width)
    d_gate_second = jnp.sum(
        tangent.astype(F32).reshape(second_latents.shape) * second_latents, axis=1
    )
    d_gate_second = d_gate_second.at[0].add(bias_down * jnp.sum(tangent_own, axis=0))
    output_part = (second_latents * modulation[:, 5][:, None, :]).reshape(tokens, width)
    output_part = jnp.concatenate(
        [output_part[:chunk] + (middle + gate_second * bias_down), output_part[chunk:]], axis=0
    ).astype(BF)

    d_hidden_second = total(scatter(second_part))
    (
        d_hidden_second,
        cond_low,
        momentum_ada,
        momentum_qkv,
        momentum_proj,
        momentum_up,
        momentum_down,
        w_ada_old,
        w_qkv_old,
        w_proj_old,
        w_up_old,
        w_down_old,
    ) = lax.optimization_barrier(
        (
            d_hidden_second,
            cond_low,
            momentum_ada,
            momentum_qkv,
            momentum_proj,
            momentum_up,
            momentum_down,
            w_ada,
            w_qkv,
            w_proj,
            w_up,
            w_down,
        )
    )

    grad_down = t_dot(act_low, d_second_low).astype(BF)
    grad_up = t_dot(d_pre_low, second_low).astype(BF)
    grad_up, grad_down = lax.psum((grad_up, grad_down), "dp")

    d_shift_second = jnp.sum(d_hidden_second, axis=0)
    d_scale_second = jnp.sum(d_hidden_second * normed_second, axis=0)
    d_middle = tangent_own + norm_back(
        normed_second, inverse_second, d_hidden_second * (1.0 + scale_second)
    )
    d_branch_first = gate_first * d_middle
    d_gate_first = jnp.sum(d_middle * branch_first, axis=0)
    d_proj_bias = jnp.sum(d_branch_first, axis=0)
    d_first_pieces = collect(d_branch_first.astype(BF))

    d_heads, d_head_sums, first_part = attention_back(
        d_first_pieces, heads, qkv_low, proj_low, seq_length
    )
    d_first_low = jnp.concatenate(d_first_pieces, axis=0)
    grad_proj = t_dot(attended_low, d_first_low).astype(BF)
    d_head_bias = jnp.sum(d_head_sums, axis=0)
    grad_qkv = jnp.concatenate([t_dot(d_heads[k], first_low) for k in range(3)], axis=0).astype(BF)
    cond_all = dp_collect(cond_low).reshape(-1, width)
    first_pieces = scatter(first_part)
    late_rows = 3 * quarter + proj_low.shape[0]
    masks, levels = dp_masks(), dp_levels()
    late_momentum = reorder(
        jnp.concatenate([flat(momentum_qkv), momentum_proj], axis=0), masks, dp_rank
    )
    late_grads = reorder(jnp.concatenate([grad_qkv, grad_proj], axis=0), masks, dp_rank)
    late_grads = dp_scatter_sum(late_grads.reshape(dp_size, -1, width))
    late_grads, first_pieces = lax.optimization_barrier((late_grads, first_pieces))
    late_grads = dp_collect(late_grads, levels[:-1])
    d_hidden_first = total(first_pieces)

    me_index = me.astype(jnp.int32).reshape(1)
    none = jnp.zeros((len(half_blocks(width // TILE)) * HALF, TILE), F32)
    moment_up = MUON_MOMENTUM * flat(momentum_up) + grad_up.astype(F32)
    moment_down = MUON_MOMENTUM * flat(momentum_down) + grad_down.astype(F32)
    start_up, start_down = moment_up.astype(BF), moment_down.astype(BF)
    turn = jnp.where(dp_rank == OWNERS[3], 1, jnp.where(dp_rank == OWNERS[4], 2, 0))
    early = lax.switch(
        turn,
        [
            lambda *rows: none,
            lambda *rows: gram_blocks(rows[0], rows[1]),
            lambda *rows: gram_blocks(rows[0], rows[2]),
        ],
        me_index,
        start_up,
        start_down,
    )
    early, late_grads = lax.optimization_barrier((early, late_grads))
    early_ranks = OWNERS[3:5]
    early = scatter(split(early, size), early_ranks)
    late_grads = [late_grads, dp_swap(late_grads, levels[-1][0])]
    late_moments = [
        MUON_MOMENTUM * momentum + grads.reshape(-1, width).astype(F32)
        for momentum, grads in zip(split(late_momentum, 2), late_grads)
    ]
    of_qkv = (jnp.asarray(masks, jnp.uint32) ^ dp_rank) * (late_rows // dp_size) < 3 * quarter
    of_qkv = jnp.repeat(of_qkv, late_rows // dp_size).reshape(2, -1, 1)
    qkv_rows = [
        jnp.where(of_qkv[k], late_moments[k], 0.0).astype(BF) for k in range(2)
    ]

    normed_own, inverse_own = normed_of(own)
    d_shift_first = jnp.sum(d_hidden_first, axis=0)
    d_scale_first = jnp.sum(d_hidden_first * normed_own, axis=0)
    grad_inputs = d_middle + norm_back(
        normed_own, inverse_own, d_hidden_first * (1.0 + scale_first)
    )
    grad_inputs = grad_inputs.astype(BF)

    sums = jnp.stack(
        [
            d_shift_first,
            d_scale_first,
            d_gate_first,
            d_shift_second,
            d_scale_second,
            d_proj_bias,
            *d_gate_second,
        ]
    )
    of_device = [
        lax.dynamic_slice_in_dim(sums, (me ^ mask) * quarter, quarter, 1) for mask in range(size)
    ]
    arrived = jnp.stack(
        [of_device[0]] + [swap(of_device[mask], mask) for mask in range(1, size)]
    )
    d_proj_own = jnp.sum(arrived[:, 5], axis=0)
    per_latent = size // latent_count
    d_gate_own = [
        sum(arrived[mask, 6 + (q ^ (mask // per_latent))] for mask in range(size))
        for q in range(latent_count)
    ]
    d_mod_own = jnp.sum(
        arrived[:, :5].reshape(latent_count, per_latent, 5, quarter), axis=1
    )
    d_mod_own = jnp.concatenate([d_mod_own, jnp.stack(d_gate_own)[:, None]], axis=1)
    d_mod_own = reorder(d_mod_own, latent_count, my_latent)
    d_cond_part = dot(
        d_mod_own.reshape(latent_count, -1).astype(BF), flat(w_ada_old).astype(BF)
    )
    d_down_own = lax.dynamic_slice_in_dim(d_down_bias, me * quarter, quarter, 0)
    small = jnp.concatenate(
        [
            d_mod_own.reshape(-1, quarter),
            d_head_bias,
            d_proj_own[None],
            d_up_bias,
            d_down_own[None],
        ],
        axis=0,
    )
    small_all = dp_collect(small)
    d_mod_all = small_all[:, : 6 * latent_count].reshape(-1, 6, quarter)
    grad_biases = jnp.concatenate(
        [jnp.sum(d_mod_all, axis=0), jnp.sum(small_all[:, 6 * latent_count :], axis=0)], axis=0
    )
    d_mod_low = d_mod_all.reshape(d_mod_all.shape[0], -1).astype(BF)
    grad_ada = t_dot(d_mod_low, cond_all)

    moment_ada = MUON_MOMENTUM * flat(momentum_ada) + grad_ada
    start_ada = moment_ada.astype(BF)
    turn = jnp.where(dp_rank == OWNERS[0], 1, jnp.where(dp_rank == OWNERS[1], 2, 0))
    late = lax.switch(
        turn,
        [
            lambda *rows: none,
            lambda *rows: gram_blocks(rows[0], rows[1]),
            lambda *rows: gram_blocks(rows[0], *rows[2:]),
        ],
        me_index,
        start_ada,
        *qkv_rows,
    )
    late_ranks = OWNERS[:2]
    late, late_moments = lax.optimization_barrier((late, late_moments))
    late = scatter(split(late, size), late_ranks)
    places, place = dp_places()
    late_moments = reorder(jnp.concatenate(late_moments, axis=0), places, place)
    moment_qkv, moment_proj = late_moments[: 3 * quarter], late_moments[3 * quarter :]
    start_qkv, start_proj = moment_qkv.astype(BF), moment_proj.astype(BF)
    proj_rows = collect(start_proj, OWNERS[2:3])
    moments = (moment_ada, moment_qkv, moment_proj, moment_up, moment_down)
    starts = (start_ada, start_qkv, start_proj, start_up, start_down)

    early = jnp.concatenate(collect(total(early), early_ranks), axis=0)
    early, output_part, grad_inputs, d_cond_part = lax.optimization_barrier(
        (early, output_part, grad_inputs, d_cond_part)
    )
    output = total(scatter(split(output_part, size))).astype(BF)
    grad_inputs = collect(grad_inputs)
    late = jnp.concatenate(collect(total(late), late_ranks), axis=0)
    proj_gram = lax.cond(
        dp_rank == OWNERS[2], gram_blocks, lambda *rows: none, me_index, *proj_rows
    )
    is_late = (dp_rank == OWNERS[0]) | (dp_rank == OWNERS[1])
    gram = jnp.where(dp_rank == OWNERS[2], proj_gram, jnp.where(is_late, late, early))
    factor = newton_schulz_factor(me_index, gram, width)
    factor, output, grad_inputs = lax.optimization_barrier((factor, output, grad_inputs))
    output = jnp.concatenate(collect(output), axis=0)
    output = reorder(output, size, me).reshape(inputs.shape)
    grad_inputs = jnp.concatenate(grad_inputs, axis=0)
    grad_inputs = reorder(grad_inputs, size, me).reshape(inputs.shape)
    d_cond_act = total(collect(d_cond_part))
    grad_condition = silu_pull(d_cond_act)[0]
    column_width = width // dp_size
    column_start = dp_rank * column_width
    factors = lax.all_to_all(
        factor.reshape(dp_size, column_width, width), "dp", 0, 0, tiled=True
    )

    weights_old = (w_ada_old, w_qkv_old, w_proj_old, w_up_old, w_down_old)
    sizes = [max(w.size // width * size, width) for w in weights_old]
    columns = [
        lax.dynamic_slice_in_dim(flat(w), column_start, column_width, 1) for w in weights_old
    ]
    new_weights = update_weights(starts, columns, factors, sizes)
    new_weights = [
        new.reshape(old.shape[:-1] + (column_width,))
        for new, old in zip(new_weights, weights_old)
    ]
    new_bias_first = BETA_ONE * bias_first + (1.0 - BETA_ONE) * grad_biases
    new_bias_second = BETA_TWO * bias_second + (1.0 - BETA_TWO) * grad_biases * grad_biases
    first_hat = new_bias_first / (1.0 - BETA_ONE**STEP)
    second_hat = new_bias_second / (1.0 - BETA_TWO**STEP)
    new_biases = biases - ADAM_RATE * first_hat / (jnp.sqrt(second_hat) + ADAM_EPS)
    return (
        output,
        grad_inputs,
        grad_condition,
        *new_weights,
        moments[0].reshape(momentum_ada.shape),
        moments[1].reshape(momentum_qkv.shape),
        moments[2],
        moments[3].reshape(momentum_up.shape),
        moments[4].reshape(momentum_down.shape),
        new_biases,
        new_bias_first,
        new_bias_second,
    )


def solution(mesh):
    placed = (
        P("dp", None, None),
        P("dp", None),
        P("dp", None, None),
        P(None, "tensor", None),
        P(None, "tensor", None),
        P("tensor", None),
        P(None, "tensor", None),
        P(None, "tensor", None),
        P(None, "tensor"),
        P(None, "tensor", None),
        P(None, "tensor", None),
        P("tensor", None),
        P(None, "tensor", None),
        P(None, "tensor", None),
        P(None, "tensor"),
        P(None, "tensor"),
    )
    return jax.shard_map(
        on_device,
        mesh=mesh,
        in_specs=placed,
        out_specs=(
            P("dp", None, None),
            P("dp", None, None),
            P("dp", None),
            P(None, "tensor", "dp"),
            P(None, "tensor", "dp"),
            P("tensor", "dp"),
            P(None, "tensor", "dp"),
            P(None, "tensor", "dp"),
            P(None, "tensor", None),
            P(None, "tensor", None),
            P("tensor", None),
            P(None, "tensor", None),
            P(None, "tensor", None),
            P(None, "tensor"),
            P(None, "tensor"),
            P(None, "tensor"),
        ),
        check_vma=False,
    )
```

```python
import functools
import math

import jax
import jax.numpy as jnp
from jax import lax
from jax.experimental import pallas as pl
from jax.experimental.pallas import tpu as pltpu
from jax.sharding import PartitionSpec as P

HEAD_DIM = 64
NS_ITERS = 5
STEP = 10


NS_A = 3.4445
NS_B = -4.775
NS_C = 2.0315
MUON_RATE = 0.16
MUON_DECAY = 0.01
MUON_MOMENTUM = 0.95
ADAM_RATE = 0.25
BETA_ONE = 0.9
BETA_TWO = 0.999
ADAM_EPS = 1e-08
NORM_EPS = 1e-06

BF = jnp.bfloat16
F32 = jnp.float32
TILE = 256
HALF = 128
VMEM_LIMIT = 28 * 1024 * 1024
OWNERS = (0, 2, 5, 4, 6)


def dot(a, b):
    return jnp.dot(a, b, preferred_element_type=F32)


def dot_t(a, b):
    return lax.dot_general(a, b, (((1,), (1,)), ((), ())), preferred_element_type=F32)


def t_dot(a, b):
    return lax.dot_general(a, b, (((0,), (0,)), ((), ())), preferred_element_type=F32)


def parts(value):
    high = value.astype(BF)
    return high, (value - high.astype(F32)).astype(BF)


def blocks_of(count):
    return [(i, j) for i in range(count) for j in range(i, count)]


def half_blocks(count):
    return [(i, j, half) for i, j in blocks_of(count) for half in range(2)]


def half_rows(index, total, me_ref, size):
    per_chunk = total // size
    place = (index // per_chunk) ^ me_ref[0]
    return pl.ds(pl.multiple_of(place * (per_chunk * HALF) + index % per_chunk * HALF, HALF), HALF)


def gram_kernel(size, kinds, me_ref, *refs):
    out_ref, rows_ref = refs[-2:]
    refs, first = list(refs[:-2]), 0
    for kind in kinds:
        rows = refs.pop(0)[...]
        if kind != "plain":
            grad = refs.pop(0)[...]
            if kind == "outer":
                grad = t_dot(grad, refs.pop(0)[...])
            rows = MUON_MOMENTUM * rows + grad.astype(F32)
            if kind == "masked":
                rows = jnp.where(refs.pop(0)[...] > 0.0, rows, 0.0)
        last = first + rows.shape[0]
        rows_ref[first:last, :] = rows.astype(BF)
        first = last
    halves = half_blocks(rows_ref.shape[1] // TILE)
    for index, (i, j, half) in enumerate(halves):
        left = slice(i * TILE + half * HALF, i * TILE + (half + 1) * HALF)
        right = slice(j * TILE, (j + 1) * TILE)
        out_ref[half_rows(index, len(halves), me_ref, size), :] = t_dot(
            rows_ref[:, left], rows_ref[:, right]
        )


def gram_blocks(me, kinds, *operands):
    taken = {"plain": 1, "grad": 2, "masked": 3, "outer": 3}
    depth, place = 0, 0
    for kind in kinds:
        depth += operands[place].shape[0]
        place += taken[kind]
    width = operands[0].shape[1]
    count = len(half_blocks(width // TILE))
    return pl.pallas_call(
        functools.partial(gram_kernel, lax.axis_size("tensor"), kinds),
        in_specs=[pl.BlockSpec(memory_space=pltpu.SMEM)]
        + [pl.BlockSpec(memory_space=pltpu.VMEM)] * len(operands),
        out_shape=jax.ShapeDtypeStruct((count * HALF, TILE), F32),
        scratch_shapes=[pltpu.VMEM((depth, width), BF)],
        compiler_params=pltpu.CompilerParams(vmem_limit_bytes=VMEM_LIMIT),
        cost_estimate=pl.CostEstimate(
            flops=2 * depth * width * width, bytes_accessed=depth * width * 6, transcendentals=0
        ),
    )(me, *operands)


def newton_schulz_kernel(
    size, me_ref, blocks_ref, out_ref, cur, high, rest, poly, mid_h, mid_l, f_h, f_l, g_h, g_l
):
    width = cur.shape[0]
    spans = [slice(i * TILE, (i + 1) * TILE) for i in range(width // TILE)]
    halves = half_blocks(width // TILE)
    for index, (i, j, half) in enumerate(halves):
        block = blocks_ref[half_rows(index, len(halves), me_ref, size), :]
        left = slice(i * TILE + half * HALF, i * TILE + (half + 1) * HALF)
        cur[left, spans[j]] = block
        if i != j:
            cur[spans[j], left] = block.T
    square_norm = jnp.zeros((1, 1), F32)
    row = lax.broadcasted_iota(jnp.int32, (TILE, TILE), 0)
    col = lax.broadcasted_iota(jnp.int32, (TILE, TILE), 1)
    for span in spans:
        square_norm += jnp.sum(jnp.where(row == col, cur[span, span], 0.0), keepdims=True)
    scale = 1.0 / (jnp.sqrt(square_norm) + 1e-07)
    for span in spans:
        cur[span, :] = cur[span, :] * (scale * scale)

    def make_poly():
        for span in spans:
            high[span, :], rest[span, :] = parts(cur[span, :])
        for span in spans:
            poly[span, :] = (NS_B * cur[span, :] + NS_C * dot(high[span, :], high[...])).astype(BF)

    def step_gram():
        for span in spans:
            half = (
                NS_A * cur[span, :] + dot(high[span, :], poly[...]) + dot(rest[span, :], poly[...])
            )
            mid_h[span, :], mid_l[span, :] = parts(half)
        for span in spans:
            half = mid_h[span, :].astype(F32) + mid_l[span, :].astype(F32)
            cur[span, :] = (
                NS_A * half + dot(poly[span, :], mid_h[...]) + dot(poly[span, :], mid_l[...])
            )

    def stepped_factor(span):
        before = f_h[span, :].astype(F32) + f_l[span, :].astype(F32)
        return NS_A * before + dot(poly[span, :], f_h[...]) + dot(poly[span, :], f_l[...])

    make_poly()
    wide_row = lax.broadcasted_iota(jnp.int32, (TILE, width), 0)
    wide_col = lax.broadcasted_iota(jnp.int32, (TILE, width), 1)
    for i, span in enumerate(spans):
        start = poly[span, :].astype(F32) + jnp.where(wide_row + i * TILE == wide_col, NS_A, 0.0)
        f_h[span, :], f_l[span, :] = parts(start)
    step_gram()

    def middle(_, carry):
        make_poly()
        for span in spans:
            g_h[span, :], g_l[span, :] = parts(stepped_factor(span))
        f_h[...] = g_h[...]
        f_l[...] = g_l[...]
        step_gram()
        return carry

    lax.fori_loop(0, NS_ITERS - 2, middle, 0)
    make_poly()
    for span in spans:
        out_ref[span, :] = (stepped_factor(span) * scale).astype(out_ref.dtype)


def newton_schulz_factor(me, blocks, width):
    whole = lambda kind: pltpu.VMEM((width, width), kind)
    return pl.pallas_call(
        functools.partial(newton_schulz_kernel, lax.axis_size("tensor")),
        in_specs=[
            pl.BlockSpec(memory_space=pltpu.SMEM),
            pl.BlockSpec(memory_space=pltpu.VMEM),
        ],
        out_shape=jax.ShapeDtypeStruct((width, width), BF),
        scratch_shapes=[whole(F32)] + [whole(BF)] * 9,
        compiler_params=pltpu.CompilerParams(vmem_limit_bytes=VMEM_LIMIT),
        cost_estimate=pl.CostEstimate(
            flops=2 * 29 * width**3, bytes_accessed=width * width * 6, transcendentals=0
        ),
    )(me, blocks)


def update_kernel(sizes, place_ref, *refs):
    count = len(sizes)
    rows, weights, factor, outs = refs[:count], refs[count : 2 * count], refs[2 * count], refs[2 * count + 1 :]
    for k, size in enumerate(sizes):
        ortho = dot_t(rows[k][...], factor[place_ref[k]])
        outs[k][...] = (
            weights[k][...] * (1.0 - MUON_RATE * MUON_DECAY)
            - MUON_RATE * 0.2 * math.sqrt(size) * ortho
        )


def update_weights(places, rows, weights, factors, sizes):
    return pl.pallas_call(
        functools.partial(update_kernel, sizes),
        in_specs=[pl.BlockSpec(memory_space=pltpu.SMEM)]
        + [pl.BlockSpec(memory_space=pltpu.VMEM)] * (2 * len(sizes) + 1),
        out_shape=[jax.ShapeDtypeStruct(w.shape, F32) for w in weights],
        compiler_params=pltpu.CompilerParams(vmem_limit_bytes=VMEM_LIMIT),
        cost_estimate=pl.CostEstimate(
            flops=sum(2 * r.size * w.shape[1] for r, w in zip(rows, weights)),
            bytes_accessed=sum(2 * r.size + 12 * w.size for r, w in zip(rows, weights)),
            transcendentals=0,
        ),
    )(places, *rows, *weights, factors)


def put_pieces(refs, scratch):
    step = pl.program_id(0)
    rows = refs[0].shape[0]
    per_step = scratch.shape[0] // rows
    for index, ref in enumerate(refs):
        k = index % per_step

        @pl.when(step == index // per_step)
        def _(ref=ref, k=k):
            ref[...] = scratch[k * rows : (k + 1) * rows, :]


def take_pieces(refs, scratch):
    step = pl.program_id(0)
    rows = refs[0].shape[0]
    per_step = scratch.shape[0] // rows
    for index, ref in enumerate(refs):
        k = index % per_step

        @pl.when(step == index // per_step)
        def _(ref=ref, k=k):
            scratch[k * rows : (k + 1) * rows, :] = ref[...]


def attention_kernel(
    count, x_ref, mod_ref, w_ref, proj_ref, bias_ref, hidden_ref, heads_ref, attended_ref, *refs
):
    quarter = proj_ref.shape[0]
    normed, _ = normed_of(x_ref[...].astype(F32))
    hidden = (normed * (1.0 + mod_ref[0, 1:2, :]) + mod_ref[0, 0:1, :]).astype(BF)
    hidden_ref[...] = hidden
    queries = (dot_t(hidden, w_ref[:quarter, :]) + bias_ref[0:1, :]).astype(BF)
    keys = dot_t(hidden, w_ref[quarter : 2 * quarter, :]).astype(BF)
    values = (dot_t(hidden, w_ref[2 * quarter :, :]) + bias_ref[1:2, :]).astype(BF)
    heads_ref[0] = queries
    heads_ref[1] = keys
    heads_ref[2] = values
    attended = []
    for start in range(0, quarter, HEAD_DIM):
        head = slice(start, start + HEAD_DIM)
        probs = softmax_of(queries[:, head], keys[:, head]).astype(BF)
        attended.append(dot(probs, values[:, head]))
    attended = jnp.concatenate(attended, axis=1).astype(BF)
    attended_ref[...] = attended
    part = refs[-1]
    part[...] = dot(attended, proj_ref[...]).astype(BF)
    put_pieces(refs[:-1], part)


def softmax_of(queries, keys):
    scores = dot_t(queries, keys) * (1.0 / math.sqrt(HEAD_DIM))
    raised = jnp.exp(scores - jnp.max(scores, axis=-1, keepdims=True))
    return raised * (1.0 / jnp.sum(raised, axis=-1, keepdims=True))


def attention(tokens_in, modulation, qkv_low, proj_low, bias_rows, seq_length, count):
    tokens, width = tokens_in.shape
    quarter = proj_low.shape[0]
    rows = lambda last: pl.BlockSpec((seq_length, last), lambda i: (i, 0))
    whole = lambda shape: pl.BlockSpec(shape, lambda i: (0,) * len(shape))
    piece = (tokens // count, width)
    out = pl.pallas_call(
        functools.partial(attention_kernel, count),
        grid=(tokens // seq_length,),
        in_specs=[
            rows(width),
            pl.BlockSpec((1, 6, width), lambda i: (i, 0, 0)),
            whole(qkv_low.shape),
            whole(proj_low.shape),
            whole(bias_rows.shape),
        ],
        out_specs=[
            rows(width),
            pl.BlockSpec((3, seq_length, quarter), lambda i: (0, i, 0)),
            rows(quarter),
        ]
        + [whole(piece)] * count,
        out_shape=[
            jax.ShapeDtypeStruct((tokens, width), BF),
            jax.ShapeDtypeStruct((3, tokens, quarter), BF),
            jax.ShapeDtypeStruct((tokens, quarter), BF),
        ]
        + [jax.ShapeDtypeStruct(piece, BF)] * count,
        scratch_shapes=[pltpu.VMEM((seq_length, width), BF)],
        compiler_params=pltpu.CompilerParams(vmem_limit_bytes=VMEM_LIMIT),
        cost_estimate=pl.CostEstimate(
            flops=8 * tokens * width * quarter + 4 * tokens * seq_length * quarter,
            bytes_accessed=tokens * width * 8 + qkv_low.size * 3,
            transcendentals=tokens * seq_length * quarter // HEAD_DIM,
        ),
    )(tokens_in, modulation, qkv_low, proj_low, bias_rows)
    return out[0], out[1], out[2], out[3:]


def attention_back_kernel(count, heads_ref, w_ref, proj_ref, *refs):
    grad_refs, (d_heads_ref, sums_ref) = refs[:count], refs[count : count + 2]
    part_refs, grad = refs[count + 2 : -1], refs[-1]
    take_pieces(grad_refs, grad)
    quarter = proj_ref.shape[0]
    scale = 1.0 / math.sqrt(HEAD_DIM)
    d_attended = dot_t(grad[...], proj_ref[...]).astype(BF)
    queries, keys, values = heads_ref[0], heads_ref[1], heads_ref[2]
    d_queries, d_keys, d_values = [], [], []
    for start in range(0, quarter, HEAD_DIM):
        head = slice(start, start + HEAD_DIM)
        probs = softmax_of(queries[:, head], keys[:, head])
        d_out = d_attended[:, head]
        d_values.append(t_dot(probs.astype(BF), d_out))
        d_probs = dot_t(d_out, values[:, head])
        d_scores = (
            probs * (d_probs - jnp.sum(probs * d_probs, axis=-1, keepdims=True))
        ).astype(BF)
        d_queries.append(dot(d_scores, keys[:, head]) * scale)
        d_keys.append(t_dot(d_scores, queries[:, head]) * scale)
    d_queries = jnp.concatenate(d_queries, axis=1)
    d_values = jnp.concatenate(d_values, axis=1)
    sums_ref[0, 0:1, :] = jnp.sum(d_queries, axis=0, keepdims=True)
    sums_ref[0, 1:2, :] = jnp.sum(d_values, axis=0, keepdims=True)
    d_queries = d_queries.astype(BF)
    d_keys = jnp.concatenate(d_keys, axis=1).astype(BF)
    d_values = d_values.astype(BF)
    d_heads_ref[0] = d_queries
    d_heads_ref[1] = d_keys
    d_heads_ref[2] = d_values
    part = (
        dot(d_queries, w_ref[:quarter, :])
        + dot(d_keys, w_ref[quarter : 2 * quarter, :])
        + dot(d_values, w_ref[2 * quarter :, :])
    )
    grad[...] = part.astype(BF)
    put_pieces(part_refs, grad)


def attention_back(grads, heads, qkv_low, proj_low, seq_length):
    count = len(grads)
    rows, width = grads[0].shape
    tokens = rows * count
    quarter = proj_low.shape[0]
    whole = lambda shape: pl.BlockSpec(shape, lambda i: (0,) * len(shape))
    of_heads = pl.BlockSpec((3, seq_length, quarter), lambda i: (0, i, 0))
    out = pl.pallas_call(
        functools.partial(attention_back_kernel, count),
        grid=(tokens // seq_length,),
        in_specs=[of_heads, whole(qkv_low.shape), whole(proj_low.shape)]
        + [whole(grads[0].shape)] * count,
        out_specs=[of_heads, pl.BlockSpec((1, 2, quarter), lambda i: (i, 0, 0))]
        + [whole(grads[0].shape)] * count,
        out_shape=[
            jax.ShapeDtypeStruct(heads.shape, BF),
            jax.ShapeDtypeStruct((tokens // seq_length, 2, quarter), F32),
        ]
        + [jax.ShapeDtypeStruct(grads[0].shape, BF)] * count,
        scratch_shapes=[pltpu.VMEM((seq_length, width), BF)],
        compiler_params=pltpu.CompilerParams(vmem_limit_bytes=VMEM_LIMIT),
        cost_estimate=pl.CostEstimate(
            flops=8 * tokens * width * quarter + 10 * tokens * seq_length * quarter,
            bytes_accessed=tokens * width * 8 + qkv_low.size * 3,
            transcendentals=tokens * seq_length * quarter // HEAD_DIM,
        ),
    )(heads, qkv_low, proj_low, *grads)
    return out[0], out[1], out[2:]


def feed_forward_kernel(count, grad_ref, up_ref, down_ref, bias_ref, *refs):
    hidden_refs, (act_ref, d_pre_ref, sums_ref) = refs[:count], refs[count : count + 3]
    part_refs, hidden = refs[count + 3 : -1], refs[-1]
    take_pieces(hidden_refs, hidden)
    pre = dot_t(hidden[...], up_ref[...]) + bias_ref[...]
    d_act = dot_t(grad_ref[...], down_ref[...])
    root = math.sqrt(2.0 / math.pi)
    square = pre * pre
    bent = jnp.tanh(root * pre * (1.0 + 0.044715 * square))
    half = 0.5 * (1.0 + bent)
    act_ref[...] = (pre * half).astype(BF)
    slope = half + 0.5 * pre * (1.0 - bent * bent) * (root * (1.0 + 0.134145 * square))
    d_pre = d_act * slope

    @pl.when(pl.program_id(0) == 0)
    def _():
        sums_ref[...] = jnp.zeros_like(sums_ref)

    sums_ref[...] += jnp.sum(d_pre, axis=0, keepdims=True)
    d_pre = d_pre.astype(BF)
    d_pre_ref[...] = d_pre
    hidden[...] = dot(d_pre, up_ref[...]).astype(BF)
    put_pieces(part_refs, hidden)


def feed_forward(hidden, grad, up_low, down_low, bias):
    count = len(hidden)
    tokens, width = grad.shape
    units = up_low.shape[0]
    block = tokens // 2
    rows = lambda last: pl.BlockSpec((block, last), lambda i: (i, 0))
    whole = lambda shape: pl.BlockSpec(shape, lambda i: (0,) * len(shape))
    out = pl.pallas_call(
        functools.partial(feed_forward_kernel, count),
        grid=(tokens // block,),
        in_specs=[rows(width), whole(up_low.shape), whole(down_low.shape), whole((1, units))]
        + [whole(hidden[0].shape)] * count,
        out_specs=[rows(units), rows(units), whole((1, units))]
        + [whole(hidden[0].shape)] * count,
        out_shape=[
            jax.ShapeDtypeStruct((tokens, units), BF),
            jax.ShapeDtypeStruct((tokens, units), BF),
            jax.ShapeDtypeStruct((1, units), F32),
        ]
        + [jax.ShapeDtypeStruct(hidden[0].shape, BF)] * count,
        scratch_shapes=[pltpu.VMEM((block, width), BF)],
        compiler_params=pltpu.CompilerParams(vmem_limit_bytes=VMEM_LIMIT),
        cost_estimate=pl.CostEstimate(
            flops=6 * tokens * width * units,
            bytes_accessed=tokens * width * 10 + up_low.size * 4,
            transcendentals=tokens * units,
        ),
    )(grad, up_low, down_low, bias, *hidden)
    return out[0], out[1], out[2], out[3:]


def dp_swap(piece, mask, ranks=None):
    ranks = range(lax.axis_size("dp")) if ranks is None else ranks
    return lax.ppermute(piece, "dp", [(i, i ^ mask) for i in ranks])


def dp_all_to_all(value, ranks):
    shape = value.shape
    for step, radix in dp_levels():
        lower = dp_masks().index(step)
        value = value.reshape((-1, radix, lower) + shape[1:])
        value = jnp.stack(
            [value[:, 0]] + [dp_swap(value[:, j], j * step, ranks) for j in range(1, radix)], axis=1
        )
        ranks = None
    return value.reshape(shape)


def dp_levels():
    size, step, levels = lax.axis_size("dp"), 2, []
    while step < size:
        radix = min(4, size // step)
        levels.append((step, radix))
        step *= radix
    return levels + [(1, 2)]


def dp_masks():
    masks = [0]
    for step, radix in dp_levels():
        masks = [j * step + mask for j in range(radix) for mask in masks]
    return masks


def dp_collect(piece, levels=None):
    gathered = piece[None]
    for step, radix in dp_levels() if levels is None else levels:
        gathered = jnp.concatenate(
            [gathered] + [dp_swap(gathered, j * step) for j in range(1, radix)], axis=0
        )
    return gathered


def dp_scatter_sum(value):
    for step, radix in reversed(dp_levels()):
        value = value.reshape((radix, -1) + value.shape[1:])
        total = value[0].astype(F32)
        for j in range(1, radix):
            total = total + dp_swap(value[j], j * step).astype(F32)
        value = total.astype(BF)
    return value[0]


def dp_reduce(value):
    size = lax.axis_size("dp")
    value = reorder(value, dp_masks(), place_of("dp"))
    return dp_scatter_sum(value.reshape((size, -1) + value.shape[1:]))


def dp_places():
    masks, rank = dp_masks(), place_of("dp")
    place, bit = jnp.uint32(0), 0
    while 1 << bit < len(masks):
        place = place | (((rank >> bit) & 1) * masks.index(1 << bit))
        bit += 1
    return [masks.index(p) for p in range(len(masks))], place


def place_of(axis):
    return lax.axis_index(axis).astype(jnp.uint32)


def swap(piece, mask, ranks=None):
    size = lax.axis_size("tensor")
    if ranks is None:
        return lax.ppermute(piece, "tensor", [(i, i ^ mask) for i in range(size)])
    pairs = [(r * size + i, r * size + (i ^ mask)) for r in ranks for i in range(size)]
    return lax.ppermute(piece, ("dp", "tensor"), pairs)


def split(value, count):
    rows = value.shape[0] // count
    return [value[k * rows : (k + 1) * rows] for k in range(count)]


def scatter(pieces, ranks=None):
    return [pieces[0]] + [swap(pieces[mask], mask, ranks) for mask in range(1, len(pieces))]


def total(pieces):
    return sum([piece.astype(F32) for piece in pieces[1:]], pieces[0].astype(F32))


def scatter_halving(pieces, ranks=None):
    sent = [jnp.concatenate(pieces[1::2], axis=0), None]
    sent[1] = swap(sent[0], 1, ranks)
    rows = pieces[0].shape[0]
    kept = [
        total([piece, sent[1][k * rows : (k + 1) * rows]]) for k, piece in enumerate(pieces[::2])
    ]
    return total([kept[0], swap(kept[1].astype(pieces[0].dtype), 2, ranks)])


def collect_doubling(piece, ranks=None):
    pair = jnp.stack([piece, swap(piece, 2, ranks)])
    pairs = jnp.stack([pair, swap(pair, 1, ranks)], axis=1)
    return pairs.reshape((-1,) + piece.shape[1:])


def collect(piece, ranks=None):
    size = lax.axis_size("tensor")
    return [piece] + [swap(piece, mask, ranks) for mask in range(1, size)]


def reorder(value, masks, index):
    masks = list(range(masks)) if isinstance(masks, int) else masks
    rows = value.shape[0] // len(masks)
    return jnp.concatenate(
        [lax.dynamic_slice_in_dim(value, (index ^ p) * rows, rows, 0) for p in masks], axis=0
    )


def normed_of(values):
    average = jnp.mean(values, axis=-1, keepdims=True)
    centered = values - average
    variance = jnp.mean(centered * centered, axis=-1, keepdims=True)
    inverse = lax.rsqrt(variance + NORM_EPS)
    return centered * inverse, inverse


def norm_back(normed, inverse, grad):
    return (
        grad
        - jnp.mean(grad, axis=-1, keepdims=True)
        - normed * jnp.mean(grad * normed, axis=-1, keepdims=True)
    ) * inverse


def on_device(
    inputs,
    condition,
    cotangent,
    w_ada,
    w_qkv,
    w_proj,
    w_up,
    w_down,
    biases,
    momentum_ada,
    momentum_qkv,
    momentum_proj,
    momentum_up,
    momentum_down,
    bias_first,
    bias_second,
):
    quarter = w_ada.shape[1]
    width = w_ada.shape[-1]
    latent_count = inputs.shape[0]
    seq_length = inputs.shape[1]
    tokens = latent_count * seq_length
    heads_here = quarter // HEAD_DIM
    size = lax.axis_size("tensor")
    me = place_of("tensor")
    dp_size = lax.axis_size("dp")
    dp_rank = place_of("dp")
    chunk = tokens // size
    my_latent = me // (size // latent_count)
    scale_factor = 1.0 / math.sqrt(HEAD_DIM)
    flat = lambda w: w.reshape(-1, width)
    ada_low = flat(w_ada).astype(BF)
    qkv_low = flat(w_qkv).astype(BF)
    proj_low = w_proj.astype(BF)
    up_bias = biases[9:13].reshape(-1)

    cond_act, silu_pull = jax.vjp(jax.nn.silu, condition.astype(F32))
    cond_low = cond_act.astype(BF)
    mod_part = dot_t(cond_low, ada_low).reshape(latent_count * 6, quarter) + jnp.tile(
        biases[0:6], (latent_count, 1)
    )
    mod_part = jnp.concatenate([mod_part, biases[8:9], biases[13:14]], axis=0)
    gathered = jnp.concatenate(collect(mod_part[None]), axis=0)
    gathered = reorder(gathered, size, me)
    gathered = jnp.moveaxis(gathered, 0, 1).reshape(-1, width)
    modulation = reorder(gathered[: latent_count * 6], latent_count, my_latent).reshape(
        latent_count, 6, width
    )
    bias_proj = gathered[latent_count * 6]
    bias_down = gathered[latent_count * 6 + 1]
    shift_first, scale_first, gate_first = modulation[0, 0], modulation[0, 1], modulation[0, 2]
    shift_second, scale_second, gate_second = modulation[0, 3], modulation[0, 4], modulation[0, 5]

    tokens_in = reorder(inputs.reshape(tokens, width), size, me)
    tangent = reorder(cotangent.reshape(tokens, width), size, me)
    first_low, heads, attended_low, partial_first = attention(
        tokens_in, modulation, qkv_low, proj_low, biases[6:8], seq_length, size
    )
    partial_first, w_up, w_down = lax.optimization_barrier((partial_first, w_up, w_down))
    up_low = flat(w_up).astype(BF)
    down_low = flat(w_down).astype(BF)
    own = tokens_in[:chunk].astype(F32)
    tangent_own = tangent[:chunk].astype(F32)

    branch_first = total(scatter(partial_first)) + bias_proj
    middle = own + gate_first * branch_first
    normed_second, inverse_second = normed_of(middle)
    second_pieces = collect((normed_second * (1.0 + scale_second) + shift_second).astype(BF))

    d_branch_second = (
        tangent.astype(F32).reshape(latent_count, seq_length, width)
        * modulation[:, 5][:, None, :]
    ).reshape(tokens, width)
    d_down_bias = jnp.sum(d_branch_second, axis=0)
    d_second_low = d_branch_second.astype(BF)
    act_low, d_pre_low, d_up_bias, second_part = feed_forward(
        second_pieces, d_second_low, up_low, down_low, up_bias[None]
    )
    second_low = jnp.concatenate(second_pieces, axis=0)
    d_up_bias = d_up_bias.reshape(-1, quarter)
    partial_second = dot(act_low, down_low)
    second_latents = partial_second.reshape(latent_count, seq_length, width)
    d_gate_second = jnp.sum(
        tangent.astype(F32).reshape(second_latents.shape) * second_latents, axis=1
    )
    d_gate_second = d_gate_second.at[0].add(bias_down * jnp.sum(tangent_own, axis=0))
    output_part = (second_latents * modulation[:, 5][:, None, :]).reshape(tokens, width)
    output_part = jnp.concatenate(
        [output_part[:chunk] + (middle + gate_second * bias_down), output_part[chunk:]], axis=0
    ).astype(BF)

    d_hidden_second = total(scatter(second_part))
    (
        d_hidden_second,
        cond_low,
        momentum_ada,
        momentum_qkv,
        momentum_proj,
        momentum_up,
        momentum_down,
        w_ada_old,
        w_qkv_old,
        w_proj_old,
        w_up_old,
        w_down_old,
    ) = lax.optimization_barrier(
        (
            d_hidden_second,
            cond_low,
            momentum_ada,
            momentum_qkv,
            momentum_proj,
            momentum_up,
            momentum_down,
            w_ada,
            w_qkv,
            w_proj,
            w_up,
            w_down,
        )
    )

    grad_down = t_dot(act_low, d_second_low).astype(BF)
    grad_up = t_dot(d_pre_low, second_low).astype(BF)
    grad_up, grad_down = lax.psum((grad_up, grad_down), "dp")

    d_shift_second = jnp.sum(d_hidden_second, axis=0)
    d_scale_second = jnp.sum(d_hidden_second * normed_second, axis=0)
    d_middle = tangent_own + norm_back(
        normed_second, inverse_second, d_hidden_second * (1.0 + scale_second)
    )
    d_branch_first = gate_first * d_middle
    d_gate_first = jnp.sum(d_middle * branch_first, axis=0)
    d_proj_bias = jnp.sum(d_branch_first, axis=0)
    d_first_pieces = collect(d_branch_first.astype(BF))

    d_heads, d_head_sums, first_part = attention_back(
        d_first_pieces, heads, qkv_low, proj_low, seq_length
    )
    d_first_low = jnp.concatenate(d_first_pieces, axis=0)
    grad_proj = t_dot(attended_low, d_first_low).astype(BF)
    d_head_bias = jnp.sum(d_head_sums, axis=0)
    grad_qkv = jnp.concatenate([t_dot(d_heads[k], first_low) for k in range(3)], axis=0).astype(BF)
    output_part, first_part = lax.optimization_barrier((output_part, first_part))
    output = lax.psum(reorder(output_part, size, me), "tensor").reshape(inputs.shape)
    late_rows = 3 * quarter + proj_low.shape[0]
    masks, levels = dp_masks(), dp_levels()
    late_momentum = split(
        reorder(jnp.concatenate([flat(momentum_qkv), momentum_proj], axis=0), masks, dp_rank), 2
    )
    of_qkv = (jnp.asarray(masks, jnp.uint32) ^ dp_rank) * (late_rows // dp_size) < 3 * quarter
    of_qkv = jnp.repeat(of_qkv.astype(F32), late_rows // dp_size).reshape(2, -1, 1)
    late_grads = reorder(jnp.concatenate([grad_qkv, grad_proj], axis=0), masks, dp_rank)
    late_grads = dp_scatter_sum(late_grads.reshape(dp_size, -1, width))
    late_grads = dp_collect(late_grads, levels[:-1])
    d_hidden_first = scatter_halving(first_part)
    cond_all = dp_collect(cond_low).reshape(-1, width)

    me_index = me.astype(jnp.int32).reshape(1)
    none = jnp.zeros((len(half_blocks(width // TILE)) * HALF, TILE), F32)
    turn = jnp.where(dp_rank == OWNERS[3], 1, jnp.where(dp_rank == OWNERS[4], 2, 0))
    early = lax.switch(
        turn,
        [
            lambda *rows: none,
            lambda *rows: gram_blocks(rows[0], ["grad"], *rows[1:3]),
            lambda *rows: gram_blocks(rows[0], ["grad"], *rows[3:5]),
        ],
        me_index,
        flat(momentum_up),
        grad_up,
        flat(momentum_down),
        grad_down,
    )
    early, late_grads = lax.optimization_barrier((early, late_grads))
    early_ranks = OWNERS[3:5]
    early = scatter_halving(split(early, size), early_ranks)
    late_grads = [
        grads.reshape(-1, width) for grads in (late_grads, dp_swap(late_grads, levels[-1][0]))
    ]

    normed_own, inverse_own = normed_of(own)
    d_shift_first = jnp.sum(d_hidden_first, axis=0)
    d_scale_first = jnp.sum(d_hidden_first * normed_own, axis=0)
    grad_inputs = d_middle + norm_back(
        normed_own, inverse_own, d_hidden_first * (1.0 + scale_first)
    )
    grad_inputs = lax.all_gather(grad_inputs.astype(BF), "tensor", axis=0, tiled=True)

    sums = jnp.stack(
        [
            d_shift_first,
            d_scale_first,
            d_gate_first,
            d_shift_second,
            d_scale_second,
            d_proj_bias,
            *d_gate_second,
        ]
    )
    of_device = [
        lax.dynamic_slice_in_dim(sums, (me ^ mask) * quarter, quarter, 1) for mask in range(size)
    ]
    arrived = jnp.stack(
        [of_device[0]] + [swap(of_device[mask], mask) for mask in range(1, size)]
    )
    d_proj_own = jnp.sum(arrived[:, 5], axis=0)
    per_latent = size // latent_count
    d_gate_own = [
        sum(arrived[mask, 6 + (q ^ (mask // per_latent))] for mask in range(size))
        for q in range(latent_count)
    ]
    d_mod_own = jnp.sum(
        arrived[:, :5].reshape(latent_count, per_latent, 5, quarter), axis=1
    )
    d_mod_own = jnp.concatenate([d_mod_own, jnp.stack(d_gate_own)[:, None]], axis=1)
    d_mod_own = reorder(d_mod_own, latent_count, my_latent)
    d_cond_part = dot(
        d_mod_own.reshape(latent_count, -1).astype(BF), flat(w_ada_old).astype(BF)
    )
    d_down_own = lax.dynamic_slice_in_dim(d_down_bias, me * quarter, quarter, 0)
    small = jnp.concatenate(
        [
            d_mod_own.reshape(-1, quarter),
            d_head_bias,
            d_proj_own[None],
            d_up_bias,
            d_down_own[None],
        ],
        axis=0,
    )
    small_all = dp_collect(small)
    d_mod_all = small_all[:, : 6 * latent_count].reshape(-1, 6, quarter)
    grad_biases = jnp.concatenate(
        [jnp.sum(d_mod_all, axis=0), jnp.sum(small_all[:, 6 * latent_count :], axis=0)], axis=0
    )
    d_mod_low = d_mod_all.reshape(d_mod_all.shape[0], -1).astype(BF)

    turn = jnp.where(dp_rank == OWNERS[0], 1, jnp.where(dp_rank == OWNERS[1], 2, 0))
    late = lax.switch(
        turn,
        [
            lambda *rows: none,
            lambda *rows: gram_blocks(rows[0], ["outer"], *rows[1:4]),
            lambda *rows: gram_blocks(rows[0], ["masked"] * 2, *rows[4:]),
        ],
        me_index,
        flat(momentum_ada),
        d_mod_low,
        cond_all,
        late_momentum[0],
        late_grads[0],
        of_qkv[0],
        late_momentum[1],
        late_grads[1],
        of_qkv[1],
    )
    late_ranks = OWNERS[:2]
    late, late_grads, grad_up, grad_down, grad_ada = lax.optimization_barrier(
        (late, late_grads, grad_up, grad_down, (d_mod_low, cond_all))
    )
    late = scatter(split(late, size), late_ranks)
    places, place = dp_places()
    late_moments = reorder(
        jnp.concatenate(
            [
                MUON_MOMENTUM * momentum + grads.astype(F32)
                for momentum, grads in zip(late_momentum, late_grads)
            ],
            axis=0,
        ),
        places,
        place,
    )
    moment_qkv, moment_proj = late_moments[: 3 * quarter], late_moments[3 * quarter :]
    proj_rows = collect(moment_proj.astype(BF), OWNERS[2:3])
    moments = (
        MUON_MOMENTUM * flat(momentum_ada) + t_dot(*grad_ada),
        moment_qkv,
        moment_proj,
        MUON_MOMENTUM * flat(momentum_up) + grad_up.astype(F32),
        MUON_MOMENTUM * flat(momentum_down) + grad_down.astype(F32),
    )
    starts = [moment.astype(BF) for moment in moments]

    early = collect_doubling(early, early_ranks)
    late = jnp.concatenate(collect(total(late), late_ranks), axis=0)
    proj_gram = lax.cond(
        dp_rank == OWNERS[2],
        lambda *rows: gram_blocks(rows[0], ["plain"] * size, *rows[1:]),
        lambda *rows: none,
        me_index,
        *proj_rows,
    )
    is_late = (dp_rank == OWNERS[0]) | (dp_rank == OWNERS[1])
    gram = jnp.where(dp_rank == OWNERS[2], proj_gram, jnp.where(is_late, late, early))
    gram, output = lax.optimization_barrier((gram, output))
    factor = newton_schulz_factor(me_index, gram, width)
    factor, grad_inputs, d_cond_part = lax.optimization_barrier(
        (factor, grad_inputs, d_cond_part)
    )
    grad_inputs = grad_inputs.reshape(inputs.shape)
    pair_sum = d_cond_part + swap(d_cond_part, 1)
    d_cond_act = pair_sum + swap(pair_sum, 2)
    grad_condition = silu_pull(d_cond_act)[0]
    column_width = width // dp_size
    column_start = dp_rank * column_width
    factors = reorder(factor, masks, dp_rank).reshape(dp_size, column_width, width)
    factors = dp_all_to_all(factors, OWNERS)
    owner_places = jnp.stack(
        [(place ^ places[owner]).astype(jnp.int32) for owner in OWNERS]
    )

    weights_old = (w_ada_old, w_qkv_old, w_proj_old, w_up_old, w_down_old)
    sizes = [max(w.size // width * size, width) for w in weights_old]
    columns = [
        lax.dynamic_slice_in_dim(flat(w), column_start, column_width, 1) for w in weights_old
    ]
    new_weights = update_weights(owner_places, starts, columns, factors, sizes)
    new_weights = [
        new.reshape(old.shape[:-1] + (column_width,))
        for new, old in zip(new_weights, weights_old)
    ]
    new_bias_first = BETA_ONE * bias_first + (1.0 - BETA_ONE) * grad_biases
    new_bias_second = BETA_TWO * bias_second + (1.0 - BETA_TWO) * grad_biases * grad_biases
    first_hat = new_bias_first / (1.0 - BETA_ONE**STEP)
    second_hat = new_bias_second / (1.0 - BETA_TWO**STEP)
    new_biases = biases - ADAM_RATE * first_hat / (jnp.sqrt(second_hat) + ADAM_EPS)
    return (
        output,
        grad_inputs,
        grad_condition,
        *new_weights,
        moments[0].reshape(momentum_ada.shape),
        moments[1].reshape(momentum_qkv.shape),
        moments[2],
        moments[3].reshape(momentum_up.shape),
        moments[4].reshape(momentum_down.shape),
        new_biases,
        new_bias_first,
        new_bias_second,
    )


def solution(mesh):
    placed = (
        P("dp", None, None),
        P("dp", None),
        P("dp", None, None),
        P(None, "tensor", None),
        P(None, "tensor", None),
        P("tensor", None),
        P(None, "tensor", None),
        P(None, "tensor", None),
        P(None, "tensor"),
        P(None, "tensor", None),
        P(None, "tensor", None),
        P("tensor", None),
        P(None, "tensor", None),
        P(None, "tensor", None),
        P(None, "tensor"),
        P(None, "tensor"),
    )
    return jax.shard_map(
        on_device,
        mesh=mesh,
        in_specs=placed,
        out_specs=(
            P("dp", None, None),
            P("dp", None, None),
            P("dp", None),
            P(None, "tensor", "dp"),
            P(None, "tensor", "dp"),
            P("tensor", "dp"),
            P(None, "tensor", "dp"),
            P(None, "tensor", "dp"),
            P(None, "tensor", None),
            P(None, "tensor", None),
            P("tensor", None),
            P(None, "tensor", None),
            P(None, "tensor", None),
            P(None, "tensor"),
            P(None, "tensor"),
            P(None, "tensor"),
        ),
        check_vma=False,
    )
```

```python
import functools
import math

import jax
import jax.numpy as jnp
from jax import lax
from jax.experimental import pallas as pl
from jax.experimental.pallas import tpu as pltpu
from jax.sharding import PartitionSpec as P

HEAD_DIM = 64
NS_ITERS = 5
STEP = 10


NS_A = 3.4445
NS_B = -4.775
NS_C = 2.0315
MUON_RATE = 0.16
MUON_DECAY = 0.01
MUON_MOMENTUM = 0.95
ADAM_RATE = 0.25
BETA_ONE = 0.9
BETA_TWO = 0.999
ADAM_EPS = 1e-08
NORM_EPS = 1e-06

BF = jnp.bfloat16
F32 = jnp.float32
TILE = 256
HALF = 128
VMEM_LIMIT = 28 * 1024 * 1024
OWNERS = (0, 2, 5, 4, 6)


def dot(a, b):
    return jnp.dot(a, b, preferred_element_type=F32)


def dot_t(a, b):
    return lax.dot_general(a, b, (((1,), (1,)), ((), ())), preferred_element_type=F32)


def t_dot(a, b):
    return lax.dot_general(a, b, (((0,), (0,)), ((), ())), preferred_element_type=F32)


def parts(value):
    high = value.astype(BF)
    return high, (value - high.astype(F32)).astype(BF)


def blocks_of(count):
    return [(i, j) for i in range(count) for j in range(i, count)]


def half_blocks(count):
    return [(i, j, half) for i, j in blocks_of(count) for half in range(2)]


def half_rows(index, total, me_ref, size):
    per_chunk = total // size
    place = (index // per_chunk) ^ me_ref[0]
    return pl.ds(pl.multiple_of(place * (per_chunk * HALF) + index % per_chunk * HALF, HALF), HALF)


def gram_kernel(size, kinds, me_ref, *refs):
    out_ref, rows_ref = refs[-2:]
    refs, first = list(refs[:-2]), 0
    for kind in kinds:
        rows = refs.pop(0)[...]
        if kind != "plain":
            grad = refs.pop(0)[...]
            if kind == "outer":
                grad = t_dot(grad, refs.pop(0)[...])
            rows = MUON_MOMENTUM * rows + grad.astype(F32)
            if kind == "masked":
                rows = jnp.where(refs.pop(0)[...] > 0.0, rows, 0.0)
        last = first + rows.shape[0]
        rows_ref[first:last, :] = rows.astype(BF)
        first = last
    halves = half_blocks(rows_ref.shape[1] // TILE)
    for index, (i, j, half) in enumerate(halves):
        left = slice(i * TILE + half * HALF, i * TILE + (half + 1) * HALF)
        right = slice(j * TILE, (j + 1) * TILE)
        out_ref[half_rows(index, len(halves), me_ref, size), :] = t_dot(
            rows_ref[:, left], rows_ref[:, right]
        )


def gram_blocks(me, kinds, *operands):
    taken = {"plain": 1, "grad": 2, "masked": 3, "outer": 3}
    depth, place = 0, 0
    for kind in kinds:
        depth += operands[place].shape[0]
        place += taken[kind]
    width = operands[0].shape[1]
    count = len(half_blocks(width // TILE))
    return pl.pallas_call(
        functools.partial(gram_kernel, lax.axis_size("tensor"), kinds),
        in_specs=[pl.BlockSpec(memory_space=pltpu.SMEM)]
        + [pl.BlockSpec(memory_space=pltpu.VMEM)] * len(operands),
        out_shape=jax.ShapeDtypeStruct((count * HALF, TILE), F32),
        scratch_shapes=[pltpu.VMEM((depth, width), BF)],
        compiler_params=pltpu.CompilerParams(vmem_limit_bytes=VMEM_LIMIT),
        cost_estimate=pl.CostEstimate(
            flops=2 * depth * width * width, bytes_accessed=depth * width * 6, transcendentals=0
        ),
    )(me, *operands)


def newton_schulz_kernel(
    size, me_ref, blocks_ref, out_ref, cur, high, rest, poly, mid_h, mid_l, f_h, f_l, g_h, g_l
):
    width = cur.shape[0]
    spans = [slice(i * TILE, (i + 1) * TILE) for i in range(width // TILE)]
    halves = half_blocks(width // TILE)
    for index, (i, j, half) in enumerate(halves):
        block = blocks_ref[half_rows(index, len(halves), me_ref, size), :]
        left = slice(i * TILE + half * HALF, i * TILE + (half + 1) * HALF)
        cur[left, spans[j]] = block
        if i != j:
            cur[spans[j], left] = block.T
    square_norm = jnp.zeros((1, 1), F32)
    row = lax.broadcasted_iota(jnp.int32, (TILE, TILE), 0)
    col = lax.broadcasted_iota(jnp.int32, (TILE, TILE), 1)
    for span in spans:
        square_norm += jnp.sum(jnp.where(row == col, cur[span, span], 0.0), keepdims=True)
    scale = 1.0 / (jnp.sqrt(square_norm) + 1e-07)
    for span in spans:
        cur[span, :] = cur[span, :] * (scale * scale)

    def make_poly():
        for span in spans:
            high[span, :], rest[span, :] = parts(cur[span, :])
        for span in spans:
            poly[span, :] = (NS_B * cur[span, :] + NS_C * dot(high[span, :], high[...])).astype(BF)

    def step_gram():
        for span in spans:
            half = (
                NS_A * cur[span, :] + dot(high[span, :], poly[...]) + dot(rest[span, :], poly[...])
            )
            mid_h[span, :], mid_l[span, :] = parts(half)
        for span in spans:
            half = mid_h[span, :].astype(F32) + mid_l[span, :].astype(F32)
            cur[span, :] = (
                NS_A * half + dot(poly[span, :], mid_h[...]) + dot(poly[span, :], mid_l[...])
            )

    def stepped_factor(span):
        before = f_h[span, :].astype(F32) + f_l[span, :].astype(F32)
        return NS_A * before + dot(poly[span, :], f_h[...]) + dot(poly[span, :], f_l[...])

    make_poly()
    wide_row = lax.broadcasted_iota(jnp.int32, (TILE, width), 0)
    wide_col = lax.broadcasted_iota(jnp.int32, (TILE, width), 1)
    for i, span in enumerate(spans):
        start = poly[span, :].astype(F32) + jnp.where(wide_row + i * TILE == wide_col, NS_A, 0.0)
        f_h[span, :], f_l[span, :] = parts(start)
    step_gram()

    def middle(_, carry):
        make_poly()
        for span in spans:
            g_h[span, :], g_l[span, :] = parts(stepped_factor(span))
        f_h[...] = g_h[...]
        f_l[...] = g_l[...]
        step_gram()
        return carry

    lax.fori_loop(0, NS_ITERS - 2, middle, 0)
    make_poly()
    for span in spans:
        out_ref[span, :] = (stepped_factor(span) * scale).astype(out_ref.dtype)


def newton_schulz_factor(me, blocks, width):
    whole = lambda kind: pltpu.VMEM((width, width), kind)
    return pl.pallas_call(
        functools.partial(newton_schulz_kernel, lax.axis_size("tensor")),
        in_specs=[
            pl.BlockSpec(memory_space=pltpu.SMEM),
            pl.BlockSpec(memory_space=pltpu.VMEM),
        ],
        out_shape=jax.ShapeDtypeStruct((width, width), BF),
        scratch_shapes=[whole(F32)] + [whole(BF)] * 9,
        compiler_params=pltpu.CompilerParams(vmem_limit_bytes=VMEM_LIMIT),
        cost_estimate=pl.CostEstimate(
            flops=2 * 29 * width**3, bytes_accessed=width * width * 6, transcendentals=0
        ),
    )(me, blocks)


def update_kernel(sizes, place_ref, *refs):
    count = len(sizes)
    rows, weights, factor, outs = refs[:count], refs[count : 2 * count], refs[2 * count], refs[2 * count + 1 :]
    for k, size in enumerate(sizes):
        ortho = dot_t(rows[k][...], factor[place_ref[k]])
        outs[k][...] = (
            weights[k][...] * (1.0 - MUON_RATE * MUON_DECAY)
            - MUON_RATE * 0.2 * math.sqrt(size) * ortho
        )


def update_weights(places, rows, weights, factors, sizes):
    return pl.pallas_call(
        functools.partial(update_kernel, sizes),
        in_specs=[pl.BlockSpec(memory_space=pltpu.SMEM)]
        + [pl.BlockSpec(memory_space=pltpu.VMEM)] * (2 * len(sizes) + 1),
        out_shape=[jax.ShapeDtypeStruct(w.shape, F32) for w in weights],
        compiler_params=pltpu.CompilerParams(vmem_limit_bytes=VMEM_LIMIT),
        cost_estimate=pl.CostEstimate(
            flops=sum(2 * r.size * w.shape[1] for r, w in zip(rows, weights)),
            bytes_accessed=sum(2 * r.size + 12 * w.size for r, w in zip(rows, weights)),
            transcendentals=0,
        ),
    )(places, *rows, *weights, factors)


def put_pieces(refs, scratch):
    step = pl.program_id(0)
    rows = refs[0].shape[0]
    per_step = scratch.shape[0] // rows
    for index, ref in enumerate(refs):
        k = index % per_step

        @pl.when(step == index // per_step)
        def _(ref=ref, k=k):
            ref[...] = scratch[k * rows : (k + 1) * rows, :]


def take_pieces(refs, scratch):
    step = pl.program_id(0)
    rows = refs[0].shape[0]
    per_step = scratch.shape[0] // rows
    for index, ref in enumerate(refs):
        k = index % per_step

        @pl.when(step == index // per_step)
        def _(ref=ref, k=k):
            scratch[k * rows : (k + 1) * rows, :] = ref[...]


def attention_kernel(
    count, x_ref, mod_ref, w_ref, proj_ref, bias_ref, hidden_ref, heads_ref, attended_ref, *refs
):
    quarter = proj_ref.shape[0]
    normed, _ = normed_of(x_ref[...].astype(F32))
    hidden = (normed * (1.0 + mod_ref[0, 1:2, :]) + mod_ref[0, 0:1, :]).astype(BF)
    hidden_ref[...] = hidden
    queries = (dot_t(hidden, w_ref[:quarter, :]) + bias_ref[0:1, :]).astype(BF)
    keys = dot_t(hidden, w_ref[quarter : 2 * quarter, :]).astype(BF)
    values = (dot_t(hidden, w_ref[2 * quarter :, :]) + bias_ref[1:2, :]).astype(BF)
    heads_ref[0] = queries
    heads_ref[1] = keys
    heads_ref[2] = values
    attended = []
    for start in range(0, quarter, HEAD_DIM):
        head = slice(start, start + HEAD_DIM)
        probs = softmax_of(queries[:, head], keys[:, head]).astype(BF)
        attended.append(dot(probs, values[:, head]))
    attended = jnp.concatenate(attended, axis=1).astype(BF)
    attended_ref[...] = attended
    part = refs[-1]
    part[...] = dot(attended, proj_ref[...]).astype(BF)
    put_pieces(refs[:-1], part)


def softmax_of(queries, keys):
    scores = dot_t(queries, keys) * (1.0 / math.sqrt(HEAD_DIM))
    raised = jnp.exp(scores - jnp.max(scores, axis=-1, keepdims=True))
    return raised * (1.0 / jnp.sum(raised, axis=-1, keepdims=True))


def attention(tokens_in, modulation, qkv_low, proj_low, bias_rows, seq_length, count):
    tokens, width = tokens_in.shape
    quarter = proj_low.shape[0]
    rows = lambda last: pl.BlockSpec((seq_length, last), lambda i: (i, 0))
    whole = lambda shape: pl.BlockSpec(shape, lambda i: (0,) * len(shape))
    piece = (tokens // count, width)
    out = pl.pallas_call(
        functools.partial(attention_kernel, count),
        grid=(tokens // seq_length,),
        in_specs=[
            rows(width),
            pl.BlockSpec((1, 6, width), lambda i: (i, 0, 0)),
            whole(qkv_low.shape),
            whole(proj_low.shape),
            whole(bias_rows.shape),
        ],
        out_specs=[
            rows(width),
            pl.BlockSpec((3, seq_length, quarter), lambda i: (0, i, 0)),
            rows(quarter),
        ]
        + [whole(piece)] * count,
        out_shape=[
            jax.ShapeDtypeStruct((tokens, width), BF),
            jax.ShapeDtypeStruct((3, tokens, quarter), BF),
            jax.ShapeDtypeStruct((tokens, quarter), BF),
        ]
        + [jax.ShapeDtypeStruct(piece, BF)] * count,
        scratch_shapes=[pltpu.VMEM((seq_length, width), BF)],
        compiler_params=pltpu.CompilerParams(vmem_limit_bytes=VMEM_LIMIT),
        cost_estimate=pl.CostEstimate(
            flops=8 * tokens * width * quarter + 4 * tokens * seq_length * quarter,
            bytes_accessed=tokens * width * 8 + qkv_low.size * 3,
            transcendentals=tokens * seq_length * quarter // HEAD_DIM,
        ),
    )(tokens_in, modulation, qkv_low, proj_low, bias_rows)
    return out[0], out[1], out[2], out[3:]


def attention_back_kernel(count, heads_ref, w_ref, proj_ref, *refs):
    grad_refs, (d_heads_ref, sums_ref) = refs[:count], refs[count : count + 2]
    part_refs, grad = refs[count + 2 : -1], refs[-1]
    take_pieces(grad_refs, grad)
    quarter = proj_ref.shape[0]
    scale = 1.0 / math.sqrt(HEAD_DIM)
    d_attended = dot_t(grad[...], proj_ref[...]).astype(BF)
    queries, keys, values = heads_ref[0], heads_ref[1], heads_ref[2]
    d_queries, d_keys, d_values = [], [], []
    for start in range(0, quarter, HEAD_DIM):
        head = slice(start, start + HEAD_DIM)
        probs = softmax_of(queries[:, head], keys[:, head])
        d_out = d_attended[:, head]
        d_values.append(t_dot(probs.astype(BF), d_out))
        d_probs = dot_t(d_out, values[:, head])
        d_scores = (
            probs * (d_probs - jnp.sum(probs * d_probs, axis=-1, keepdims=True))
        ).astype(BF)
        d_queries.append(dot(d_scores, keys[:, head]) * scale)
        d_keys.append(t_dot(d_scores, queries[:, head]) * scale)
    d_queries = jnp.concatenate(d_queries, axis=1)
    d_values = jnp.concatenate(d_values, axis=1)
    sums_ref[0, 0:1, :] = jnp.sum(d_queries, axis=0, keepdims=True)
    sums_ref[0, 1:2, :] = jnp.sum(d_values, axis=0, keepdims=True)
    d_queries = d_queries.astype(BF)
    d_keys = jnp.concatenate(d_keys, axis=1).astype(BF)
    d_values = d_values.astype(BF)
    d_heads_ref[0] = d_queries
    d_heads_ref[1] = d_keys
    d_heads_ref[2] = d_values
    part = (
        dot(d_queries, w_ref[:quarter, :])
        + dot(d_keys, w_ref[quarter : 2 * quarter, :])
        + dot(d_values, w_ref[2 * quarter :, :])
    )
    grad[...] = part.astype(BF)
    put_pieces(part_refs, grad)


def attention_back(grads, heads, qkv_low, proj_low, seq_length):
    count = len(grads)
    rows, width = grads[0].shape
    tokens = rows * count
    quarter = proj_low.shape[0]
    whole = lambda shape: pl.BlockSpec(shape, lambda i: (0,) * len(shape))
    of_heads = pl.BlockSpec((3, seq_length, quarter), lambda i: (0, i, 0))
    out = pl.pallas_call(
        functools.partial(attention_back_kernel, count),
        grid=(tokens // seq_length,),
        in_specs=[of_heads, whole(qkv_low.shape), whole(proj_low.shape)]
        + [whole(grads[0].shape)] * count,
        out_specs=[of_heads, pl.BlockSpec((1, 2, quarter), lambda i: (i, 0, 0))]
        + [whole(grads[0].shape)] * count,
        out_shape=[
            jax.ShapeDtypeStruct(heads.shape, BF),
            jax.ShapeDtypeStruct((tokens // seq_length, 2, quarter), F32),
        ]
        + [jax.ShapeDtypeStruct(grads[0].shape, BF)] * count,
        scratch_shapes=[pltpu.VMEM((seq_length, width), BF)],
        compiler_params=pltpu.CompilerParams(vmem_limit_bytes=VMEM_LIMIT),
        cost_estimate=pl.CostEstimate(
            flops=8 * tokens * width * quarter + 10 * tokens * seq_length * quarter,
            bytes_accessed=tokens * width * 8 + qkv_low.size * 3,
            transcendentals=tokens * seq_length * quarter // HEAD_DIM,
        ),
    )(heads, qkv_low, proj_low, *grads)
    return out[0], out[1], out[2:]


def feed_forward_kernel(count, grad_ref, up_ref, down_ref, bias_ref, *refs):
    hidden_refs, (act_ref, d_pre_ref, sums_ref) = refs[:count], refs[count : count + 3]
    part_refs, hidden = refs[count + 3 : -1], refs[-1]
    take_pieces(hidden_refs, hidden)
    pre = dot_t(hidden[...], up_ref[...]) + bias_ref[...]
    d_act = dot_t(grad_ref[...], down_ref[...])
    root = math.sqrt(2.0 / math.pi)
    square = pre * pre
    bent = jnp.tanh(root * pre * (1.0 + 0.044715 * square))
    half = 0.5 * (1.0 + bent)
    act_ref[...] = (pre * half).astype(BF)
    slope = half + 0.5 * pre * (1.0 - bent * bent) * (root * (1.0 + 0.134145 * square))
    d_pre = d_act * slope

    @pl.when(pl.program_id(0) == 0)
    def _():
        sums_ref[...] = jnp.zeros_like(sums_ref)

    sums_ref[...] += jnp.sum(d_pre, axis=0, keepdims=True)
    d_pre = d_pre.astype(BF)
    d_pre_ref[...] = d_pre
    hidden[...] = dot(d_pre, up_ref[...]).astype(BF)
    put_pieces(part_refs, hidden)


def feed_forward(hidden, grad, up_low, down_low, bias):
    count = len(hidden)
    tokens, width = grad.shape
    units = up_low.shape[0]
    block = tokens // 2
    rows = lambda last: pl.BlockSpec((block, last), lambda i: (i, 0))
    whole = lambda shape: pl.BlockSpec(shape, lambda i: (0,) * len(shape))
    out = pl.pallas_call(
        functools.partial(feed_forward_kernel, count),
        grid=(tokens // block,),
        in_specs=[rows(width), whole(up_low.shape), whole(down_low.shape), whole((1, units))]
        + [whole(hidden[0].shape)] * count,
        out_specs=[rows(units), rows(units), whole((1, units))]
        + [whole(hidden[0].shape)] * count,
        out_shape=[
            jax.ShapeDtypeStruct((tokens, units), BF),
            jax.ShapeDtypeStruct((tokens, units), BF),
            jax.ShapeDtypeStruct((1, units), F32),
        ]
        + [jax.ShapeDtypeStruct(hidden[0].shape, BF)] * count,
        scratch_shapes=[pltpu.VMEM((block, width), BF)],
        compiler_params=pltpu.CompilerParams(vmem_limit_bytes=VMEM_LIMIT),
        cost_estimate=pl.CostEstimate(
            flops=6 * tokens * width * units,
            bytes_accessed=tokens * width * 10 + up_low.size * 4,
            transcendentals=tokens * units,
        ),
    )(grad, up_low, down_low, bias, *hidden)
    return out[0], out[1], out[2], out[3:]


def dp_swap(piece, mask, ranks=None):
    ranks = range(lax.axis_size("dp")) if ranks is None else ranks
    return lax.ppermute(piece, "dp", [(i, i ^ mask) for i in ranks])


def dp_all_to_all(value, ranks):
    shape = value.shape
    for step, radix in dp_levels():
        lower = dp_masks().index(step)
        value = value.reshape((-1, radix, lower) + shape[1:])
        value = jnp.stack(
            [value[:, 0]] + [dp_swap(value[:, j], j * step, ranks) for j in range(1, radix)], axis=1
        )
        ranks = None
    return value.reshape(shape)


def dp_levels():
    size, step, levels = lax.axis_size("dp"), 2, []
    while step < size:
        radix = min(4, size // step)
        levels.append((step, radix))
        step *= radix
    return levels + [(1, 2)]


def bit_levels():
    levels = []
    for step, radix in dp_levels():
        levels += [(step << bit, 2) for bit in range(radix.bit_length() - 1)]
    return levels


def dp_masks():
    masks = [0]
    for step, radix in dp_levels():
        masks = [j * step + mask for j in range(radix) for mask in masks]
    return masks


def dp_collect(piece, levels=None):
    gathered = piece[None]
    for step, radix in dp_levels() if levels is None else levels:
        gathered = jnp.concatenate(
            [gathered] + [dp_swap(gathered, j * step) for j in range(1, radix)], axis=0
        )
    return gathered


def dp_scatter_sum(value, levels):
    for step, radix in reversed(levels):
        value = value.reshape((radix, -1) + value.shape[1:])
        summed = value[0].astype(F32)
        for j in range(1, radix):
            summed = summed + dp_swap(value[j], j * step).astype(F32)
        value = summed.astype(BF)
    return value


def dp_places():
    masks, rank = dp_masks(), place_of("dp")
    place, bit = jnp.uint32(0), 0
    while 1 << bit < len(masks):
        place = place | (((rank >> bit) & 1) * masks.index(1 << bit))
        bit += 1
    return [masks.index(p) for p in range(len(masks))], place


def place_of(axis):
    return lax.axis_index(axis).astype(jnp.uint32)


def swap(piece, mask, ranks=None):
    size = lax.axis_size("tensor")
    if ranks is None:
        return lax.ppermute(piece, "tensor", [(i, i ^ mask) for i in range(size)])
    pairs = [(r * size + i, r * size + (i ^ mask)) for r in ranks for i in range(size)]
    return lax.ppermute(piece, ("dp", "tensor"), pairs)


def split(value, count):
    rows = value.shape[0] // count
    return [value[k * rows : (k + 1) * rows] for k in range(count)]


def scatter(pieces, ranks=None):
    return [pieces[0]] + [swap(pieces[mask], mask, ranks) for mask in range(1, len(pieces))]


def total(pieces):
    return sum([piece.astype(F32) for piece in pieces[1:]], pieces[0].astype(F32))


def halving_first(pieces, ranks=None):
    sent = jnp.concatenate(pieces[1::2], axis=0)
    return swap(sent, 1, ranks)


def halving_kept(pieces, arrived):
    rows = pieces[0].shape[0]
    return [
        total([piece, arrived[k * rows : (k + 1) * rows]]) for k, piece in enumerate(pieces[::2])
    ]


def scatter_halving(pieces, ranks=None):
    kept = halving_kept(pieces, halving_first(pieces, ranks))
    return total([kept[0], swap(kept[1].astype(pieces[0].dtype), 2, ranks)])


def collect_doubling(piece, ranks=None):
    pair = jnp.stack([piece, swap(piece, 2, ranks)])
    pairs = jnp.stack([pair, swap(pair, 1, ranks)], axis=1)
    return pairs.reshape((-1,) + piece.shape[1:])


def collect(piece, ranks=None):
    size = lax.axis_size("tensor")
    return [piece] + [swap(piece, mask, ranks) for mask in range(1, size)]


def reorder(value, masks, index):
    masks = list(range(masks)) if isinstance(masks, int) else masks
    rows = value.shape[0] // len(masks)
    return jnp.concatenate(
        [lax.dynamic_slice_in_dim(value, (index ^ p) * rows, rows, 0) for p in masks], axis=0
    )


def normed_of(values):
    average = jnp.mean(values, axis=-1, keepdims=True)
    centered = values - average
    variance = jnp.mean(centered * centered, axis=-1, keepdims=True)
    inverse = lax.rsqrt(variance + NORM_EPS)
    return centered * inverse, inverse


def norm_back(normed, inverse, grad):
    return (
        grad
        - jnp.mean(grad, axis=-1, keepdims=True)
        - normed * jnp.mean(grad * normed, axis=-1, keepdims=True)
    ) * inverse


def on_device(
    inputs,
    condition,
    cotangent,
    w_ada,
    w_qkv,
    w_proj,
    w_up,
    w_down,
    biases,
    momentum_ada,
    momentum_qkv,
    momentum_proj,
    momentum_up,
    momentum_down,
    bias_first,
    bias_second,
):
    quarter = w_ada.shape[1]
    width = w_ada.shape[-1]
    latent_count = inputs.shape[0]
    seq_length = inputs.shape[1]
    tokens = latent_count * seq_length
    heads_here = quarter // HEAD_DIM
    size = lax.axis_size("tensor")
    me = place_of("tensor")
    dp_size = lax.axis_size("dp")
    dp_rank = place_of("dp")
    chunk = tokens // size
    my_latent = me // (size // latent_count)
    scale_factor = 1.0 / math.sqrt(HEAD_DIM)
    flat = lambda w: w.reshape(-1, width)
    ada_low = flat(w_ada).astype(BF)
    qkv_low = flat(w_qkv).astype(BF)
    proj_low = w_proj.astype(BF)
    up_bias = biases[9:13].reshape(-1)

    cond_act, silu_pull = jax.vjp(jax.nn.silu, condition.astype(F32))
    cond_low = cond_act.astype(BF)
    mod_part = dot_t(cond_low, ada_low).reshape(latent_count * 6, quarter) + jnp.tile(
        biases[0:6], (latent_count, 1)
    )
    mod_part = jnp.concatenate([mod_part, biases[8:9], biases[13:14]], axis=0)
    gathered = jnp.concatenate(collect(mod_part[None]), axis=0)
    gathered = reorder(gathered, size, me)
    gathered = jnp.moveaxis(gathered, 0, 1).reshape(-1, width)
    modulation = reorder(gathered[: latent_count * 6], latent_count, my_latent).reshape(
        latent_count, 6, width
    )
    bias_proj = gathered[latent_count * 6]
    bias_down = gathered[latent_count * 6 + 1]
    shift_first, scale_first, gate_first = modulation[0, 0], modulation[0, 1], modulation[0, 2]
    shift_second, scale_second, gate_second = modulation[0, 3], modulation[0, 4], modulation[0, 5]

    tokens_in = reorder(inputs.reshape(tokens, width), size, me)
    tangent = reorder(cotangent.reshape(tokens, width), size, me)
    first_low, heads, attended_low, partial_first = attention(
        tokens_in, modulation, qkv_low, proj_low, biases[6:8], seq_length, size
    )
    partial_first, w_up, w_down = lax.optimization_barrier((partial_first, w_up, w_down))
    up_low = flat(w_up).astype(BF)
    down_low = flat(w_down).astype(BF)
    own = tokens_in[:chunk].astype(F32)
    tangent_own = tangent[:chunk].astype(F32)

    branch_first = total(scatter(partial_first)) + bias_proj
    middle = own + gate_first * branch_first
    normed_second, inverse_second = normed_of(middle)
    second_pieces = collect((normed_second * (1.0 + scale_second) + shift_second).astype(BF))

    d_branch_second = (
        tangent.astype(F32).reshape(latent_count, seq_length, width)
        * modulation[:, 5][:, None, :]
    ).reshape(tokens, width)
    d_down_bias = jnp.sum(d_branch_second, axis=0)
    d_second_low = d_branch_second.astype(BF)
    act_low, d_pre_low, d_up_bias, second_part = feed_forward(
        second_pieces, d_second_low, up_low, down_low, up_bias[None]
    )
    second_low = jnp.concatenate(second_pieces, axis=0)
    d_up_bias = d_up_bias.reshape(-1, quarter)
    partial_second = dot(act_low, down_low)
    second_latents = partial_second.reshape(latent_count, seq_length, width)
    d_gate_second = jnp.sum(
        tangent.astype(F32).reshape(second_latents.shape) * second_latents, axis=1
    )
    d_gate_second = d_gate_second.at[0].add(bias_down * jnp.sum(tangent_own, axis=0))
    output_part = (second_latents * modulation[:, 5][:, None, :]).reshape(tokens, width)
    output_part = jnp.concatenate(
        [output_part[:chunk] + (middle + gate_second * bias_down), output_part[chunk:]], axis=0
    ).astype(BF)

    d_hidden_second = total(scatter(second_part))
    (
        d_hidden_second,
        cond_low,
        momentum_ada,
        momentum_qkv,
        momentum_proj,
        momentum_up,
        momentum_down,
        w_ada_old,
        w_qkv_old,
        w_proj_old,
        w_up_old,
        w_down_old,
    ) = lax.optimization_barrier(
        (
            d_hidden_second,
            cond_low,
            momentum_ada,
            momentum_qkv,
            momentum_proj,
            momentum_up,
            momentum_down,
            w_ada,
            w_qkv,
            w_proj,
            w_up,
            w_down,
        )
    )

    grad_down = t_dot(act_low, d_second_low).astype(BF)
    grad_up = t_dot(d_pre_low, second_low).astype(BF)
    grad_up, grad_down = lax.psum((grad_up, grad_down), "dp")

    d_shift_second = jnp.sum(d_hidden_second, axis=0)
    d_scale_second = jnp.sum(d_hidden_second * normed_second, axis=0)
    d_middle = tangent_own + norm_back(
        normed_second, inverse_second, d_hidden_second * (1.0 + scale_second)
    )
    d_branch_first = gate_first * d_middle
    d_gate_first = jnp.sum(d_middle * branch_first, axis=0)
    d_proj_bias = jnp.sum(d_branch_first, axis=0)
    d_first_pieces = collect(d_branch_first.astype(BF))

    d_heads, d_head_sums, first_part = attention_back(
        d_first_pieces, heads, qkv_low, proj_low, seq_length
    )
    d_first_low = jnp.concatenate(d_first_pieces, axis=0)
    grad_proj = t_dot(attended_low, d_first_low).astype(BF)
    d_head_bias = jnp.sum(d_head_sums, axis=0)
    grad_qkv = jnp.concatenate([t_dot(d_heads[k], first_low) for k in range(3)], axis=0).astype(BF)
    output_part, first_part = lax.optimization_barrier((output_part, first_part))
    output = lax.psum(reorder(output_part, size, me), "tensor").reshape(inputs.shape)
    late_rows = 3 * quarter + proj_low.shape[0]
    masks, levels = dp_masks(), dp_levels()
    late_momentum = split(
        reorder(jnp.concatenate([flat(momentum_qkv), momentum_proj], axis=0), masks, dp_rank), 2
    )
    of_qkv = (jnp.asarray(masks, jnp.uint32) ^ dp_rank) * (late_rows // dp_size) < 3 * quarter
    of_qkv = jnp.repeat(of_qkv.astype(F32), late_rows // dp_size).reshape(2, -1, 1)
    late_grads = reorder(jnp.concatenate([grad_qkv, grad_proj], axis=0), masks, dp_rank)
    late_grads = late_grads.reshape(dp_size, -1, width)
    late_grads = dp_scatter_sum(late_grads, levels[-1:])
    arrived = halving_first(first_part)
    late_grads, arrived = lax.optimization_barrier((late_grads, arrived))
    late_grads = dp_scatter_sum(late_grads, levels[:-1])[0]
    kept = halving_kept(first_part, arrived)
    arrived = swap(kept[1].astype(BF), 2)
    late_grads, arrived = lax.optimization_barrier((late_grads, arrived))
    late_grads = dp_collect(late_grads, levels[:-1])
    d_hidden_first = total([kept[0], arrived])
    cond_all = dp_collect(cond_low, bit_levels()).reshape(-1, width)

    me_index = me.astype(jnp.int32).reshape(1)
    none = jnp.zeros((len(half_blocks(width // TILE)) * HALF, TILE), F32)
    turn = jnp.where(dp_rank == OWNERS[3], 1, jnp.where(dp_rank == OWNERS[4], 2, 0))
    early = lax.switch(
        turn,
        [
            lambda *rows: none,
            lambda *rows: gram_blocks(rows[0], ["grad"], *rows[1:3]),
            lambda *rows: gram_blocks(rows[0], ["grad"], *rows[3:5]),
        ],
        me_index,
        flat(momentum_up),
        grad_up,
        flat(momentum_down),
        grad_down,
    )
    early, late_grads = lax.optimization_barrier((early, late_grads))
    early_ranks = OWNERS[3:5]
    early = scatter_halving(split(early, size), early_ranks)
    late_grads = [
        grads.reshape(-1, width) for grads in (late_grads, dp_swap(late_grads, levels[-1][0]))
    ]

    normed_own, inverse_own = normed_of(own)
    d_shift_first = jnp.sum(d_hidden_first, axis=0)
    d_scale_first = jnp.sum(d_hidden_first * normed_own, axis=0)
    grad_inputs = d_middle + norm_back(
        normed_own, inverse_own, d_hidden_first * (1.0 + scale_first)
    )
    grad_inputs = collect_doubling(grad_inputs.astype(BF))

    sums = jnp.stack(
        [
            d_shift_first,
            d_scale_first,
            d_gate_first,
            d_shift_second,
            d_scale_second,
            d_proj_bias,
            *d_gate_second,
        ]
    )
    of_device = [
        lax.dynamic_slice_in_dim(sums, (me ^ mask) * quarter, quarter, 1) for mask in range(size)
    ]
    mine, others = halving_kept(of_device, halving_first(of_device))
    others = swap(others, 2)
    d_proj_own = mine[5] + others[5]
    d_mod_own = jnp.stack(
        [
            jnp.concatenate([mine[:5], (mine[6] + others[7])[None]], axis=0),
            jnp.concatenate([others[:5], (mine[7] + others[6])[None]], axis=0),
        ]
    )
    d_mod_own = reorder(d_mod_own, latent_count, my_latent)
    d_cond_part = dot(
        d_mod_own.reshape(latent_count, -1).astype(BF), flat(w_ada_old).astype(BF)
    )
    d_down_own = lax.dynamic_slice_in_dim(d_down_bias, me * quarter, quarter, 0)
    small = jnp.concatenate(
        [
            d_mod_own.reshape(-1, quarter),
            d_head_bias,
            d_proj_own[None],
            d_up_bias,
            d_down_own[None],
        ],
        axis=0,
    )
    small_all = dp_collect(small, bit_levels())
    d_mod_all = small_all[:, : 6 * latent_count].reshape(-1, 6, quarter)
    grad_biases = jnp.concatenate(
        [jnp.sum(d_mod_all, axis=0), jnp.sum(small_all[:, 6 * latent_count :], axis=0)], axis=0
    )
    d_mod_low = d_mod_all.reshape(d_mod_all.shape[0], -1).astype(BF)

    turn = jnp.where(dp_rank == OWNERS[0], 1, jnp.where(dp_rank == OWNERS[1], 2, 0))
    late = lax.switch(
        turn,
        [
            lambda *rows: none,
            lambda *rows: gram_blocks(rows[0], ["outer"], *rows[1:4]),
            lambda *rows: gram_blocks(rows[0], ["masked"] * 2, *rows[4:]),
        ],
        me_index,
        flat(momentum_ada),
        d_mod_low,
        cond_all,
        late_momentum[0],
        late_grads[0],
        of_qkv[0],
        late_momentum[1],
        late_grads[1],
        of_qkv[1],
    )
    late_ranks = OWNERS[:2]
    late, late_grads, grad_up, grad_down, grad_ada = lax.optimization_barrier(
        (late, late_grads, grad_up, grad_down, (d_mod_low, cond_all))
    )
    late = scatter(split(late, size), late_ranks)
    places, place = dp_places()
    late_moments = reorder(
        jnp.concatenate(
            [
                MUON_MOMENTUM * momentum + grads.astype(F32)
                for momentum, grads in zip(late_momentum, late_grads)
            ],
            axis=0,
        ),
        places,
        place,
    )
    moment_qkv, moment_proj = late_moments[: 3 * quarter], late_moments[3 * quarter :]
    proj_rows = collect(moment_proj.astype(BF), OWNERS[2:3])
    moments = (
        MUON_MOMENTUM * flat(momentum_ada) + t_dot(*grad_ada),
        moment_qkv,
        moment_proj,
        MUON_MOMENTUM * flat(momentum_up) + grad_up.astype(F32),
        MUON_MOMENTUM * flat(momentum_down) + grad_down.astype(F32),
    )
    starts = [moment.astype(BF) for moment in moments]

    early = collect_doubling(early, early_ranks)
    late = jnp.concatenate(collect(total(late), late_ranks), axis=0)
    proj_gram = lax.cond(
        dp_rank == OWNERS[2],
        lambda *rows: gram_blocks(rows[0], ["plain"] * size, *rows[1:]),
        lambda *rows: none,
        me_index,
        *proj_rows,
    )
    is_late = (dp_rank == OWNERS[0]) | (dp_rank == OWNERS[1])
    gram = jnp.where(dp_rank == OWNERS[2], proj_gram, jnp.where(is_late, late, early))
    gram, output = lax.optimization_barrier((gram, output))
    factor = newton_schulz_factor(me_index, gram, width)
    factor, grad_inputs, d_cond_part = lax.optimization_barrier(
        (factor, grad_inputs, d_cond_part)
    )
    grad_inputs = reorder(grad_inputs, size, me).reshape(inputs.shape)
    pair_sum = d_cond_part + swap(d_cond_part, 1)
    d_cond_act = pair_sum + swap(pair_sum, 2)
    grad_condition = silu_pull(d_cond_act)[0]
    column_width = width // dp_size
    column_start = dp_rank * column_width
    factors = reorder(factor, masks, dp_rank).reshape(dp_size, column_width, width)
    factors = dp_all_to_all(factors, OWNERS)
    owner_places = jnp.stack(
        [(place ^ places[owner]).astype(jnp.int32) for owner in OWNERS]
    )

    weights_old = (w_ada_old, w_qkv_old, w_proj_old, w_up_old, w_down_old)
    sizes = [max(w.size // width * size, width) for w in weights_old]
    columns = [
        lax.dynamic_slice_in_dim(flat(w), column_start, column_width, 1) for w in weights_old
    ]
    new_weights = update_weights(owner_places, starts, columns, factors, sizes)
    new_weights = [
        new.reshape(old.shape[:-1] + (column_width,))
        for new, old in zip(new_weights, weights_old)
    ]
    new_bias_first = BETA_ONE * bias_first + (1.0 - BETA_ONE) * grad_biases
    new_bias_second = BETA_TWO * bias_second + (1.0 - BETA_TWO) * grad_biases * grad_biases
    first_hat = new_bias_first / (1.0 - BETA_ONE**STEP)
    second_hat = new_bias_second / (1.0 - BETA_TWO**STEP)
    new_biases = biases - ADAM_RATE * first_hat / (jnp.sqrt(second_hat) + ADAM_EPS)
    return (
        output,
        grad_inputs,
        grad_condition,
        *new_weights,
        moments[0].reshape(momentum_ada.shape),
        moments[1].reshape(momentum_qkv.shape),
        moments[2],
        moments[3].reshape(momentum_up.shape),
        moments[4].reshape(momentum_down.shape),
        new_biases,
        new_bias_first,
        new_bias_second,
    )


def solution(mesh):
    placed = (
        P("dp", None, None),
        P("dp", None),
        P("dp", None, None),
        P(None, "tensor", None),
        P(None, "tensor", None),
        P("tensor", None),
        P(None, "tensor", None),
        P(None, "tensor", None),
        P(None, "tensor"),
        P(None, "tensor", None),
        P(None, "tensor", None),
        P("tensor", None),
        P(None, "tensor", None),
        P(None, "tensor", None),
        P(None, "tensor"),
        P(None, "tensor"),
    )
    return jax.shard_map(
        on_device,
        mesh=mesh,
        in_specs=placed,
        out_specs=(
            P("dp", None, None),
            P("dp", None, None),
            P("dp", None),
            P(None, "tensor", "dp"),
            P(None, "tensor", "dp"),
            P("tensor", "dp"),
            P(None, "tensor", "dp"),
            P(None, "tensor", "dp"),
            P(None, "tensor", None),
            P(None, "tensor", None),
            P("tensor", None),
            P(None, "tensor", None),
            P(None, "tensor", None),
            P(None, "tensor"),
            P(None, "tensor"),
            P(None, "tensor"),
        ),
        check_vma=False,
    )
```

```python
import functools
import math

import jax
import jax.numpy as jnp
from jax import lax
from jax.experimental import pallas as pl
from jax.experimental.pallas import tpu as pltpu
from jax.sharding import PartitionSpec as P

HEAD_DIM = 64
NS_ITERS = 5
STEP = 10


NS_A = 3.4445
NS_B = -4.775
NS_C = 2.0315
MUON_RATE = 0.16
MUON_DECAY = 0.01
MUON_MOMENTUM = 0.95
ADAM_RATE = 0.25
BETA_ONE = 0.9
BETA_TWO = 0.999
ADAM_EPS = 1e-08
NORM_EPS = 1e-06

BF = jnp.bfloat16
F32 = jnp.float32
TILE = 256
HALF = 128
VMEM_LIMIT = 28 * 1024 * 1024
OWNERS = (0, 2, 5, 4, 6)


def dot(a, b):
    return jnp.dot(a, b, preferred_element_type=F32)


def dot_t(a, b):
    return lax.dot_general(a, b, (((1,), (1,)), ((), ())), preferred_element_type=F32)


def t_dot(a, b):
    return lax.dot_general(a, b, (((0,), (0,)), ((), ())), preferred_element_type=F32)


def parts(value):
    high = value.astype(BF)
    return high, (value - high.astype(F32)).astype(BF)


def blocks_of(count):
    return [(i, j) for i in range(count) for j in range(i, count)]


def half_blocks(count):
    return [(i, j, half) for i, j in blocks_of(count) for half in range(2)]


def half_rows(index, total, me_ref, size):
    per_chunk = total // size
    place = (index // per_chunk) ^ me_ref[0]
    return pl.ds(pl.multiple_of(place * (per_chunk * HALF) + index % per_chunk * HALF, HALF), HALF)


def gram_kernel(size, kinds, me_ref, *refs):
    out_ref, rows_ref = refs[-2:]
    refs, first = list(refs[:-2]), 0
    for kind in kinds:
        rows = refs.pop(0)[...]
        if kind != "plain":
            grad = refs.pop(0)[...]
            if kind == "outer":
                grad = t_dot(grad, refs.pop(0)[...])
            rows = MUON_MOMENTUM * rows + grad.astype(F32)
            if kind == "masked":
                rows = jnp.where(refs.pop(0)[...] > 0.0, rows, 0.0)
        last = first + rows.shape[0]
        rows_ref[first:last, :] = rows.astype(BF)
        first = last
    halves = half_blocks(rows_ref.shape[1] // TILE)
    for index, (i, j, half) in enumerate(halves):
        left = slice(i * TILE + half * HALF, i * TILE + (half + 1) * HALF)
        right = slice(j * TILE, (j + 1) * TILE)
        out_ref[half_rows(index, len(halves), me_ref, size), :] = t_dot(
            rows_ref[:, left], rows_ref[:, right]
        )


def gram_blocks(me, kinds, *operands):
    taken = {"plain": 1, "grad": 2, "masked": 3, "outer": 3}
    depth, place = 0, 0
    for kind in kinds:
        depth += operands[place].shape[0]
        place += taken[kind]
    width = operands[0].shape[1]
    count = len(half_blocks(width // TILE))
    return pl.pallas_call(
        functools.partial(gram_kernel, lax.axis_size("tensor"), kinds),
        in_specs=[pl.BlockSpec(memory_space=pltpu.SMEM)]
        + [pl.BlockSpec(memory_space=pltpu.VMEM)] * len(operands),
        out_shape=jax.ShapeDtypeStruct((count * HALF, TILE), F32),
        scratch_shapes=[pltpu.VMEM((depth, width), BF)],
        compiler_params=pltpu.CompilerParams(vmem_limit_bytes=VMEM_LIMIT),
        cost_estimate=pl.CostEstimate(
            flops=2 * depth * width * width, bytes_accessed=depth * width * 6, transcendentals=0
        ),
    )(me, *operands)


def newton_schulz_kernel(
    size, me_ref, blocks_ref, out_ref, cur, high, rest, poly, mid_h, mid_l, f_h, f_l, g_h, g_l
):
    width = cur.shape[0]
    spans = [slice(i * TILE, (i + 1) * TILE) for i in range(width // TILE)]
    halves = half_blocks(width // TILE)
    for index, (i, j, half) in enumerate(halves):
        block = blocks_ref[half_rows(index, len(halves), me_ref, size), :]
        left = slice(i * TILE + half * HALF, i * TILE + (half + 1) * HALF)
        cur[left, spans[j]] = block
        if i != j:
            cur[spans[j], left] = block.T
    square_norm = jnp.zeros((1, 1), F32)
    row = lax.broadcasted_iota(jnp.int32, (TILE, TILE), 0)
    col = lax.broadcasted_iota(jnp.int32, (TILE, TILE), 1)
    for span in spans:
        square_norm += jnp.sum(jnp.where(row == col, cur[span, span], 0.0), keepdims=True)
    scale = 1.0 / (jnp.sqrt(square_norm) + 1e-07)
    for span in spans:
        cur[span, :] = cur[span, :] * (scale * scale)

    def make_poly():
        for span in spans:
            high[span, :], rest[span, :] = parts(cur[span, :])
        for span in spans:
            poly[span, :] = (NS_B * cur[span, :] + NS_C * dot(high[span, :], high[...])).astype(BF)

    def step_gram():
        for span in spans:
            half = (
                NS_A * cur[span, :] + dot(high[span, :], poly[...]) + dot(rest[span, :], poly[...])
            )
            mid_h[span, :], mid_l[span, :] = parts(half)
        for span in spans:
            half = mid_h[span, :].astype(F32) + mid_l[span, :].astype(F32)
            cur[span, :] = (
                NS_A * half + dot(poly[span, :], mid_h[...]) + dot(poly[span, :], mid_l[...])
            )

    def stepped_factor(span):
        before = f_h[span, :].astype(F32) + f_l[span, :].astype(F32)
        return NS_A * before + dot(poly[span, :], f_h[...]) + dot(poly[span, :], f_l[...])

    make_poly()
    wide_row = lax.broadcasted_iota(jnp.int32, (TILE, width), 0)
    wide_col = lax.broadcasted_iota(jnp.int32, (TILE, width), 1)
    for i, span in enumerate(spans):
        start = poly[span, :].astype(F32) + jnp.where(wide_row + i * TILE == wide_col, NS_A, 0.0)
        f_h[span, :], f_l[span, :] = parts(start)
    step_gram()

    def middle(_, carry):
        make_poly()
        for span in spans:
            g_h[span, :], g_l[span, :] = parts(stepped_factor(span))
        f_h[...] = g_h[...]
        f_l[...] = g_l[...]
        step_gram()
        return carry

    lax.fori_loop(0, NS_ITERS - 2, middle, 0)
    make_poly()
    for span in spans:
        out_ref[span, :] = (stepped_factor(span) * scale).astype(out_ref.dtype)


def newton_schulz_factor(me, blocks, width):
    whole = lambda kind: pltpu.VMEM((width, width), kind)
    return pl.pallas_call(
        functools.partial(newton_schulz_kernel, lax.axis_size("tensor")),
        in_specs=[
            pl.BlockSpec(memory_space=pltpu.SMEM),
            pl.BlockSpec(memory_space=pltpu.VMEM),
        ],
        out_shape=jax.ShapeDtypeStruct((width, width), BF),
        scratch_shapes=[whole(F32)] + [whole(BF)] * 9,
        compiler_params=pltpu.CompilerParams(vmem_limit_bytes=VMEM_LIMIT),
        cost_estimate=pl.CostEstimate(
            flops=2 * 29 * width**3, bytes_accessed=width * width * 6, transcendentals=0
        ),
    )(me, blocks)


def update_kernel(sizes, place_ref, *refs):
    count = len(sizes)
    rows, weights, factor, outs = refs[:count], refs[count : 2 * count], refs[2 * count], refs[2 * count + 1 :]
    for k, size in enumerate(sizes):
        ortho = dot_t(rows[k][...], factor[place_ref[k]])
        outs[k][...] = (
            weights[k][...] * (1.0 - MUON_RATE * MUON_DECAY)
            - MUON_RATE * 0.2 * math.sqrt(size) * ortho
        )


def update_weights(places, rows, weights, factors, sizes):
    return pl.pallas_call(
        functools.partial(update_kernel, sizes),
        in_specs=[pl.BlockSpec(memory_space=pltpu.SMEM)]
        + [pl.BlockSpec(memory_space=pltpu.VMEM)] * (2 * len(sizes) + 1),
        out_shape=[jax.ShapeDtypeStruct(w.shape, F32) for w in weights],
        compiler_params=pltpu.CompilerParams(vmem_limit_bytes=VMEM_LIMIT),
        cost_estimate=pl.CostEstimate(
            flops=sum(2 * r.size * w.shape[1] for r, w in zip(rows, weights)),
            bytes_accessed=sum(2 * r.size + 12 * w.size for r, w in zip(rows, weights)),
            transcendentals=0,
        ),
    )(places, *rows, *weights, factors)


def put_pieces(refs, scratch):
    step = pl.program_id(0)
    rows = refs[0].shape[0]
    per_step = scratch.shape[0] // rows
    for index, ref in enumerate(refs):
        k = index % per_step

        @pl.when(step == index // per_step)
        def _(ref=ref, k=k):
            ref[...] = scratch[k * rows : (k + 1) * rows, :]


def take_pieces(refs, scratch):
    step = pl.program_id(0)
    rows = refs[0].shape[0]
    per_step = scratch.shape[0] // rows
    for index, ref in enumerate(refs):
        k = index % per_step

        @pl.when(step == index // per_step)
        def _(ref=ref, k=k):
            scratch[k * rows : (k + 1) * rows, :] = ref[...]


def attention_kernel(
    count, x_ref, mod_ref, w_ref, proj_ref, bias_ref, hidden_ref, heads_ref, attended_ref, *refs
):
    quarter = proj_ref.shape[0]
    normed, _ = normed_of(x_ref[...].astype(F32))
    hidden = (normed * (1.0 + mod_ref[0, 1:2, :]) + mod_ref[0, 0:1, :]).astype(BF)
    hidden_ref[...] = hidden
    queries = (dot_t(hidden, w_ref[:quarter, :]) + bias_ref[0:1, :]).astype(BF)
    keys = dot_t(hidden, w_ref[quarter : 2 * quarter, :]).astype(BF)
    values = (dot_t(hidden, w_ref[2 * quarter :, :]) + bias_ref[1:2, :]).astype(BF)
    heads_ref[0] = queries
    heads_ref[1] = keys
    heads_ref[2] = values
    attended = []
    for start in range(0, quarter, HEAD_DIM):
        head = slice(start, start + HEAD_DIM)
        probs = softmax_of(queries[:, head], keys[:, head]).astype(BF)
        attended.append(dot(probs, values[:, head]))
    attended = jnp.concatenate(attended, axis=1).astype(BF)
    attended_ref[...] = attended
    part = refs[-1]
    part[...] = dot(attended, proj_ref[...]).astype(BF)
    put_pieces(refs[:-1], part)


def softmax_of(queries, keys):
    scores = dot_t(queries, keys) * (1.0 / math.sqrt(HEAD_DIM))
    raised = jnp.exp(scores - jnp.max(scores, axis=-1, keepdims=True))
    return raised * (1.0 / jnp.sum(raised, axis=-1, keepdims=True))


def attention(tokens_in, modulation, qkv_low, proj_low, bias_rows, seq_length, count):
    tokens, width = tokens_in.shape
    quarter = proj_low.shape[0]
    rows = lambda last: pl.BlockSpec((seq_length, last), lambda i: (i, 0))
    whole = lambda shape: pl.BlockSpec(shape, lambda i: (0,) * len(shape))
    piece = (tokens // count, width)
    out = pl.pallas_call(
        functools.partial(attention_kernel, count),
        grid=(tokens // seq_length,),
        in_specs=[
            rows(width),
            pl.BlockSpec((1, 6, width), lambda i: (i, 0, 0)),
            whole(qkv_low.shape),
            whole(proj_low.shape),
            whole(bias_rows.shape),
        ],
        out_specs=[
            rows(width),
            pl.BlockSpec((3, seq_length, quarter), lambda i: (0, i, 0)),
            rows(quarter),
        ]
        + [whole(piece)] * count,
        out_shape=[
            jax.ShapeDtypeStruct((tokens, width), BF),
            jax.ShapeDtypeStruct((3, tokens, quarter), BF),
            jax.ShapeDtypeStruct((tokens, quarter), BF),
        ]
        + [jax.ShapeDtypeStruct(piece, BF)] * count,
        scratch_shapes=[pltpu.VMEM((seq_length, width), BF)],
        compiler_params=pltpu.CompilerParams(vmem_limit_bytes=VMEM_LIMIT),
        cost_estimate=pl.CostEstimate(
            flops=8 * tokens * width * quarter + 4 * tokens * seq_length * quarter,
            bytes_accessed=tokens * width * 8 + qkv_low.size * 3,
            transcendentals=tokens * seq_length * quarter // HEAD_DIM,
        ),
    )(tokens_in, modulation, qkv_low, proj_low, bias_rows)
    return out[0], out[1], out[2], out[3:]


def attention_back_kernel(count, heads_ref, w_ref, proj_ref, *refs):
    grad_refs, (d_heads_ref, sums_ref) = refs[:count], refs[count : count + 2]
    part_refs, grad = refs[count + 2 : -1], refs[-1]
    take_pieces(grad_refs, grad)
    quarter = proj_ref.shape[0]
    scale = 1.0 / math.sqrt(HEAD_DIM)
    d_attended = dot_t(grad[...], proj_ref[...]).astype(BF)
    queries, keys, values = heads_ref[0], heads_ref[1], heads_ref[2]
    d_queries, d_keys, d_values = [], [], []
    for start in range(0, quarter, HEAD_DIM):
        head = slice(start, start + HEAD_DIM)
        probs = softmax_of(queries[:, head], keys[:, head])
        d_out = d_attended[:, head]
        d_values.append(t_dot(probs.astype(BF), d_out))
        d_probs = dot_t(d_out, values[:, head])
        d_scores = (
            probs * (d_probs - jnp.sum(probs * d_probs, axis=-1, keepdims=True))
        ).astype(BF)
        d_queries.append(dot(d_scores, keys[:, head]) * scale)
        d_keys.append(t_dot(d_scores, queries[:, head]) * scale)
    d_queries = jnp.concatenate(d_queries, axis=1)
    d_values = jnp.concatenate(d_values, axis=1)
    sums_ref[0, 0:1, :] = jnp.sum(d_queries, axis=0, keepdims=True)
    sums_ref[0, 1:2, :] = jnp.sum(d_values, axis=0, keepdims=True)
    d_queries = d_queries.astype(BF)
    d_keys = jnp.concatenate(d_keys, axis=1).astype(BF)
    d_values = d_values.astype(BF)
    d_heads_ref[0] = d_queries
    d_heads_ref[1] = d_keys
    d_heads_ref[2] = d_values
    part = (
        dot(d_queries, w_ref[:quarter, :])
        + dot(d_keys, w_ref[quarter : 2 * quarter, :])
        + dot(d_values, w_ref[2 * quarter :, :])
    )
    grad[...] = part.astype(BF)
    put_pieces(part_refs, grad)


def attention_back(grads, heads, qkv_low, proj_low, seq_length):
    count = len(grads)
    rows, width = grads[0].shape
    tokens = rows * count
    quarter = proj_low.shape[0]
    whole = lambda shape: pl.BlockSpec(shape, lambda i: (0,) * len(shape))
    of_heads = pl.BlockSpec((3, seq_length, quarter), lambda i: (0, i, 0))
    out = pl.pallas_call(
        functools.partial(attention_back_kernel, count),
        grid=(tokens // seq_length,),
        in_specs=[of_heads, whole(qkv_low.shape), whole(proj_low.shape)]
        + [whole(grads[0].shape)] * count,
        out_specs=[of_heads, pl.BlockSpec((1, 2, quarter), lambda i: (i, 0, 0))]
        + [whole(grads[0].shape)] * count,
        out_shape=[
            jax.ShapeDtypeStruct(heads.shape, BF),
            jax.ShapeDtypeStruct((tokens // seq_length, 2, quarter), F32),
        ]
        + [jax.ShapeDtypeStruct(grads[0].shape, BF)] * count,
        scratch_shapes=[pltpu.VMEM((seq_length, width), BF)],
        compiler_params=pltpu.CompilerParams(vmem_limit_bytes=VMEM_LIMIT),
        cost_estimate=pl.CostEstimate(
            flops=8 * tokens * width * quarter + 10 * tokens * seq_length * quarter,
            bytes_accessed=tokens * width * 8 + qkv_low.size * 3,
            transcendentals=tokens * seq_length * quarter // HEAD_DIM,
        ),
    )(heads, qkv_low, proj_low, *grads)
    return out[0], out[1], out[2:]


def feed_forward_kernel(count, grad_ref, up_ref, down_ref, bias_ref, *refs):
    hidden_refs, (act_ref, d_pre_ref, sums_ref) = refs[:count], refs[count : count + 3]
    part_refs, hidden = refs[count + 3 : -1], refs[-1]
    take_pieces(hidden_refs, hidden)
    pre = dot_t(hidden[...], up_ref[...]) + bias_ref[...]
    d_act = dot_t(grad_ref[...], down_ref[...])
    root = math.sqrt(2.0 / math.pi)
    square = pre * pre
    bent = jnp.tanh(root * pre * (1.0 + 0.044715 * square))
    half = 0.5 * (1.0 + bent)
    act_ref[...] = (pre * half).astype(BF)
    slope = half + 0.5 * pre * (1.0 - bent * bent) * (root * (1.0 + 0.134145 * square))
    d_pre = d_act * slope

    @pl.when(pl.program_id(0) == 0)
    def _():
        sums_ref[...] = jnp.zeros_like(sums_ref)

    sums_ref[...] += jnp.sum(d_pre, axis=0, keepdims=True)
    d_pre = d_pre.astype(BF)
    d_pre_ref[...] = d_pre
    hidden[...] = dot(d_pre, up_ref[...]).astype(BF)
    put_pieces(part_refs, hidden)


def feed_forward(hidden, grad, up_low, down_low, bias):
    count = len(hidden)
    tokens, width = grad.shape
    units = up_low.shape[0]
    block = tokens // 2
    rows = lambda last: pl.BlockSpec((block, last), lambda i: (i, 0))
    whole = lambda shape: pl.BlockSpec(shape, lambda i: (0,) * len(shape))
    out = pl.pallas_call(
        functools.partial(feed_forward_kernel, count),
        grid=(tokens // block,),
        in_specs=[rows(width), whole(up_low.shape), whole(down_low.shape), whole((1, units))]
        + [whole(hidden[0].shape)] * count,
        out_specs=[rows(units), rows(units), whole((1, units))]
        + [whole(hidden[0].shape)] * count,
        out_shape=[
            jax.ShapeDtypeStruct((tokens, units), BF),
            jax.ShapeDtypeStruct((tokens, units), BF),
            jax.ShapeDtypeStruct((1, units), F32),
        ]
        + [jax.ShapeDtypeStruct(hidden[0].shape, BF)] * count,
        scratch_shapes=[pltpu.VMEM((block, width), BF)],
        compiler_params=pltpu.CompilerParams(vmem_limit_bytes=VMEM_LIMIT),
        cost_estimate=pl.CostEstimate(
            flops=6 * tokens * width * units,
            bytes_accessed=tokens * width * 10 + up_low.size * 4,
            transcendentals=tokens * units,
        ),
    )(grad, up_low, down_low, bias, *hidden)
    return out[0], out[1], out[2], out[3:]


def dp_swap(piece, mask, ranks=None):
    ranks = range(lax.axis_size("dp")) if ranks is None else ranks
    return lax.ppermute(piece, "dp", [(i, i ^ mask) for i in ranks])


def dp_all_to_all(value, ranks):
    shape = value.shape
    for step, radix in dp_levels():
        lower = dp_masks().index(step)
        value = value.reshape((-1, radix, lower) + shape[1:])
        value = jnp.stack(
            [value[:, 0]] + [dp_swap(value[:, j], j * step, ranks) for j in range(1, radix)], axis=1
        )
        ranks = None
    return value.reshape(shape)


def dp_levels():
    size, step, levels = lax.axis_size("dp"), 2, []
    while step < size:
        radix = min(4, size // step)
        levels.append((step, radix))
        step *= radix
    return levels + [(1, 2)]


def bit_levels():
    levels = []
    for step, radix in dp_levels():
        levels += [(step << bit, 2) for bit in range(radix.bit_length() - 1)]
    return levels


def dp_masks():
    masks = [0]
    for step, radix in dp_levels():
        masks = [j * step + mask for j in range(radix) for mask in masks]
    return masks


def dp_collect(piece, levels=None):
    gathered = piece[None]
    for step, radix in dp_levels() if levels is None else levels:
        gathered = jnp.concatenate(
            [gathered] + [dp_swap(gathered, j * step) for j in range(1, radix)], axis=0
        )
    return gathered


def dp_scatter_sum(value, levels):
    for step, radix in reversed(levels):
        value = value.reshape((radix, -1) + value.shape[1:])
        summed = value[0].astype(F32)
        for j in range(1, radix):
            summed = summed + dp_swap(value[j], j * step).astype(F32)
        value = summed.astype(BF)
    return value


def dp_places():
    masks, rank = dp_masks(), place_of("dp")
    place, bit = jnp.uint32(0), 0
    while 1 << bit < len(masks):
        place = place | (((rank >> bit) & 1) * masks.index(1 << bit))
        bit += 1
    return [masks.index(p) for p in range(len(masks))], place


def place_of(axis):
    return lax.axis_index(axis).astype(jnp.uint32)


def swap(piece, mask, ranks=None):
    size = lax.axis_size("tensor")
    if ranks is None:
        return lax.ppermute(piece, "tensor", [(i, i ^ mask) for i in range(size)])
    pairs = [(r * size + i, r * size + (i ^ mask)) for r in ranks for i in range(size)]
    return lax.ppermute(piece, ("dp", "tensor"), pairs)


def split(value, count):
    rows = value.shape[0] // count
    return [value[k * rows : (k + 1) * rows] for k in range(count)]


def scatter(pieces, ranks=None):
    return [pieces[0]] + [swap(pieces[mask], mask, ranks) for mask in range(1, len(pieces))]


def total(pieces):
    return sum([piece.astype(F32) for piece in pieces[1:]], pieces[0].astype(F32))


def halving_first(pieces, ranks=None):
    sent = jnp.concatenate(pieces[1::2], axis=0)
    return swap(sent, 1, ranks)


def halving_kept(pieces, arrived):
    rows = pieces[0].shape[0]
    return [
        total([piece, arrived[k * rows : (k + 1) * rows]]) for k, piece in enumerate(pieces[::2])
    ]


def scatter_halving(pieces, ranks=None):
    kept = halving_kept(pieces, halving_first(pieces, ranks))
    return total([kept[0], swap(kept[1].astype(pieces[0].dtype), 2, ranks)])


def collect_doubling(piece, ranks=None):
    pair = jnp.stack([piece, swap(piece, 2, ranks)])
    pairs = jnp.stack([pair, swap(pair, 1, ranks)], axis=1)
    return pairs.reshape((-1,) + piece.shape[1:])


def collect(piece, ranks=None):
    size = lax.axis_size("tensor")
    return [piece] + [swap(piece, mask, ranks) for mask in range(1, size)]


def reorder(value, masks, index):
    masks = list(range(masks)) if isinstance(masks, int) else masks
    rows = value.shape[0] // len(masks)
    return jnp.concatenate(
        [lax.dynamic_slice_in_dim(value, (index ^ p) * rows, rows, 0) for p in masks], axis=0
    )


def normed_of(values):
    average = jnp.mean(values, axis=-1, keepdims=True)
    centered = values - average
    variance = jnp.mean(centered * centered, axis=-1, keepdims=True)
    inverse = lax.rsqrt(variance + NORM_EPS)
    return centered * inverse, inverse


def norm_back(normed, inverse, grad):
    return (
        grad
        - jnp.mean(grad, axis=-1, keepdims=True)
        - normed * jnp.mean(grad * normed, axis=-1, keepdims=True)
    ) * inverse


def on_device(
    inputs,
    condition,
    cotangent,
    w_ada,
    w_qkv,
    w_proj,
    w_up,
    w_down,
    biases,
    momentum_ada,
    momentum_qkv,
    momentum_proj,
    momentum_up,
    momentum_down,
    bias_first,
    bias_second,
):
    quarter = w_ada.shape[1]
    width = w_ada.shape[-1]
    latent_count = inputs.shape[0]
    seq_length = inputs.shape[1]
    tokens = latent_count * seq_length
    heads_here = quarter // HEAD_DIM
    size = lax.axis_size("tensor")
    me = place_of("tensor")
    dp_size = lax.axis_size("dp")
    dp_rank = place_of("dp")
    chunk = tokens // size
    my_latent = me // (size // latent_count)
    scale_factor = 1.0 / math.sqrt(HEAD_DIM)
    flat = lambda w: w.reshape(-1, width)
    ada_low = flat(w_ada).astype(BF)
    qkv_low = flat(w_qkv).astype(BF)
    proj_low = w_proj.astype(BF)
    up_bias = biases[9:13].reshape(-1)

    cond_act, silu_pull = jax.vjp(jax.nn.silu, condition.astype(F32))
    cond_low = cond_act.astype(BF)
    mod_part = dot_t(cond_low, ada_low).reshape(latent_count * 6, quarter) + jnp.tile(
        biases[0:6], (latent_count, 1)
    )
    mod_part = jnp.concatenate([mod_part, biases[8:9], biases[13:14]], axis=0)
    gathered = jnp.concatenate(collect(mod_part[None]), axis=0)
    gathered = reorder(gathered, size, me)
    gathered = jnp.moveaxis(gathered, 0, 1).reshape(-1, width)
    modulation = reorder(gathered[: latent_count * 6], latent_count, my_latent).reshape(
        latent_count, 6, width
    )
    bias_proj = gathered[latent_count * 6]
    bias_down = gathered[latent_count * 6 + 1]
    shift_first, scale_first, gate_first = modulation[0, 0], modulation[0, 1], modulation[0, 2]
    shift_second, scale_second, gate_second = modulation[0, 3], modulation[0, 4], modulation[0, 5]

    tokens_in = reorder(inputs.reshape(tokens, width), size, me)
    tangent = reorder(cotangent.reshape(tokens, width), size, me)
    first_low, heads, attended_low, partial_first = attention(
        tokens_in, modulation, qkv_low, proj_low, biases[6:8], seq_length, size
    )
    partial_first, w_up, w_down = lax.optimization_barrier((partial_first, w_up, w_down))
    up_low = flat(w_up).astype(BF)
    down_low = flat(w_down).astype(BF)
    own = tokens_in[:chunk].astype(F32)
    tangent_own = tangent[:chunk].astype(F32)

    branch_first = total(scatter(partial_first)) + bias_proj
    middle = own + gate_first * branch_first
    normed_second, inverse_second = normed_of(middle)
    second_pieces = collect((normed_second * (1.0 + scale_second) + shift_second).astype(BF))

    d_branch_second = (
        tangent.astype(F32).reshape(latent_count, seq_length, width)
        * modulation[:, 5][:, None, :]
    ).reshape(tokens, width)
    d_down_bias = jnp.sum(d_branch_second, axis=0)
    d_second_low = d_branch_second.astype(BF)
    act_low, d_pre_low, d_up_bias, second_part = feed_forward(
        second_pieces, d_second_low, up_low, down_low, up_bias[None]
    )
    second_low = jnp.concatenate(second_pieces, axis=0)
    d_up_bias = d_up_bias.reshape(-1, quarter)
    partial_second = dot(act_low, down_low)
    second_latents = partial_second.reshape(latent_count, seq_length, width)
    d_gate_second = jnp.sum(
        tangent.astype(F32).reshape(second_latents.shape) * second_latents, axis=1
    )
    d_gate_second = d_gate_second.at[0].add(bias_down * jnp.sum(tangent_own, axis=0))
    output_part = (second_latents * modulation[:, 5][:, None, :]).reshape(tokens, width)
    output_part = jnp.concatenate(
        [output_part[:chunk] + (middle + gate_second * bias_down), output_part[chunk:]], axis=0
    ).astype(BF)

    d_hidden_second = total(scatter(second_part))
    (
        d_hidden_second,
        cond_low,
        momentum_ada,
        momentum_qkv,
        momentum_proj,
        momentum_up,
        momentum_down,
        w_ada_old,
        w_qkv_old,
        w_proj_old,
        w_up_old,
        w_down_old,
    ) = lax.optimization_barrier(
        (
            d_hidden_second,
            cond_low,
            momentum_ada,
            momentum_qkv,
            momentum_proj,
            momentum_up,
            momentum_down,
            w_ada,
            w_qkv,
            w_proj,
            w_up,
            w_down,
        )
    )

    grad_down = t_dot(act_low, d_second_low).astype(BF)
    grad_up = t_dot(d_pre_low, second_low).astype(BF)
    grad_up, grad_down = lax.psum((grad_up, grad_down), "dp")

    d_shift_second = jnp.sum(d_hidden_second, axis=0)
    d_scale_second = jnp.sum(d_hidden_second * normed_second, axis=0)
    d_middle = tangent_own + norm_back(
        normed_second, inverse_second, d_hidden_second * (1.0 + scale_second)
    )
    d_branch_first = gate_first * d_middle
    d_gate_first = jnp.sum(d_middle * branch_first, axis=0)
    d_proj_bias = jnp.sum(d_branch_first, axis=0)
    d_first_pieces = collect(d_branch_first.astype(BF))

    output_part, d_first_pieces = lax.optimization_barrier(
        (reorder(output_part, size, me), d_first_pieces)
    )
    output = lax.psum(output_part, "tensor").reshape(inputs.shape)
    d_heads, d_head_sums, first_part = attention_back(
        d_first_pieces, heads, qkv_low, proj_low, seq_length
    )
    d_first_low = jnp.concatenate(d_first_pieces, axis=0)
    grad_proj = t_dot(attended_low, d_first_low).astype(BF)
    d_head_bias = jnp.sum(d_head_sums, axis=0)
    grad_qkv = jnp.concatenate([t_dot(d_heads[k], first_low) for k in range(3)], axis=0).astype(BF)
    late_rows = 3 * quarter + proj_low.shape[0]
    masks, levels = dp_masks(), dp_levels()
    late_momentum = split(
        reorder(jnp.concatenate([flat(momentum_qkv), momentum_proj], axis=0), masks, dp_rank), 2
    )
    of_qkv = (jnp.asarray(masks, jnp.uint32) ^ dp_rank) * (late_rows // dp_size) < 3 * quarter
    of_qkv = jnp.repeat(of_qkv.astype(F32), late_rows // dp_size).reshape(2, -1, 1)
    late_grads = reorder(jnp.concatenate([grad_qkv, grad_proj], axis=0), masks, dp_rank)
    late_grads = late_grads.reshape(dp_size, -1, width)
    late_grads = dp_scatter_sum(late_grads, levels[-1:])
    late_grads, first_part = lax.optimization_barrier((late_grads, first_part))
    late_grads = dp_collect(dp_scatter_sum(late_grads, levels[:-1])[0], levels[:-1])
    d_hidden_first = scatter_halving(first_part)
    cond_all = dp_collect(cond_low, bit_levels()).reshape(-1, width)

    me_index = me.astype(jnp.int32).reshape(1)
    none = jnp.zeros((len(half_blocks(width // TILE)) * HALF, TILE), F32)
    turn = jnp.where(dp_rank == OWNERS[3], 1, jnp.where(dp_rank == OWNERS[4], 2, 0))
    early = lax.switch(
        turn,
        [
            lambda *rows: none,
            lambda *rows: gram_blocks(rows[0], ["grad"], *rows[1:3]),
            lambda *rows: gram_blocks(rows[0], ["grad"], *rows[3:5]),
        ],
        me_index,
        flat(momentum_up),
        grad_up,
        flat(momentum_down),
        grad_down,
    )
    early, late_grads = lax.optimization_barrier((early, late_grads))
    early_ranks = OWNERS[3:5]
    early = scatter_halving(split(early, size), early_ranks)
    late_grads = [
        grads.reshape(-1, width) for grads in (late_grads, dp_swap(late_grads, levels[-1][0]))
    ]

    normed_own, inverse_own = normed_of(own)
    d_shift_first = jnp.sum(d_hidden_first, axis=0)
    d_scale_first = jnp.sum(d_hidden_first * normed_own, axis=0)
    grad_inputs = d_middle + norm_back(
        normed_own, inverse_own, d_hidden_first * (1.0 + scale_first)
    )
    grad_inputs = grad_inputs.astype(BF)

    sums = jnp.stack(
        [
            d_shift_first,
            d_scale_first,
            d_gate_first,
            d_shift_second,
            d_scale_second,
            d_proj_bias,
            *d_gate_second,
        ]
    )
    of_device = [
        lax.dynamic_slice_in_dim(sums, (me ^ mask) * quarter, quarter, 1) for mask in range(size)
    ]
    mine, others = halving_kept(of_device, halving_first(of_device))
    others = swap(others, 2)
    d_proj_own = mine[5] + others[5]
    d_mod_own = jnp.stack(
        [
            jnp.concatenate([mine[:5], (mine[6] + others[7])[None]], axis=0),
            jnp.concatenate([others[:5], (mine[7] + others[6])[None]], axis=0),
        ]
    )
    d_mod_own = reorder(d_mod_own, latent_count, my_latent)
    d_cond_part = dot(
        d_mod_own.reshape(latent_count, -1).astype(BF), flat(w_ada_old).astype(BF)
    )
    d_down_own = lax.dynamic_slice_in_dim(d_down_bias, me * quarter, quarter, 0)
    small = jnp.concatenate(
        [
            d_mod_own.reshape(-1, quarter),
            d_head_bias,
            d_proj_own[None],
            d_up_bias,
            d_down_own[None],
        ],
        axis=0,
    )
    small_all = dp_collect(small, bit_levels())
    d_mod_all = small_all[:, : 6 * latent_count].reshape(-1, 6, quarter)
    grad_biases = jnp.concatenate(
        [jnp.sum(d_mod_all, axis=0), jnp.sum(small_all[:, 6 * latent_count :], axis=0)], axis=0
    )
    d_mod_low = d_mod_all.reshape(d_mod_all.shape[0], -1).astype(BF)

    turn = jnp.where(dp_rank == OWNERS[0], 1, jnp.where(dp_rank == OWNERS[1], 2, 0))
    late = lax.switch(
        turn,
        [
            lambda *rows: none,
            lambda *rows: gram_blocks(rows[0], ["outer"], *rows[1:4]),
            lambda *rows: gram_blocks(rows[0], ["masked"] * 2, *rows[4:]),
        ],
        me_index,
        flat(momentum_ada),
        d_mod_low,
        cond_all,
        late_momentum[0],
        late_grads[0],
        of_qkv[0],
        late_momentum[1],
        late_grads[1],
        of_qkv[1],
    )
    late_ranks = OWNERS[:2]
    late, late_grads, grad_up, grad_down, grad_ada = lax.optimization_barrier(
        (late, late_grads, grad_up, grad_down, (d_mod_low, cond_all))
    )
    late = scatter(split(late, size), late_ranks)
    late_moments = [
        MUON_MOMENTUM * momentum + grads.astype(F32)
        for momentum, grads in zip(late_momentum, late_grads)
    ]
    block = late_rows // dp_size
    start_proj = [
        late_moments[k * 2 // dp_size][k % (dp_size // 2) * block :][:block]
        for k, mask in enumerate(masks)
        if (mask ^ OWNERS[2]) * block >= 3 * quarter
    ]
    proj_rows = collect(jnp.concatenate(start_proj, axis=0).astype(BF), OWNERS[2:3])
    places, place = dp_places()
    late_moments = reorder(jnp.concatenate(late_moments, axis=0), places, place)
    moment_qkv, moment_proj = late_moments[: 3 * quarter], late_moments[3 * quarter :]
    moments = (
        MUON_MOMENTUM * flat(momentum_ada) + t_dot(*grad_ada),
        moment_qkv,
        moment_proj,
        MUON_MOMENTUM * flat(momentum_up) + grad_up.astype(F32),
        MUON_MOMENTUM * flat(momentum_down) + grad_down.astype(F32),
    )
    starts = [moment.astype(BF) for moment in moments]

    early = collect_doubling(early, early_ranks)
    late = collect(total(late), late_ranks)
    late[1], grad_inputs, d_cond_part = lax.optimization_barrier(
        (late[1], grad_inputs, d_cond_part)
    )
    late = jnp.concatenate(late, axis=0)
    no_rows = jnp.zeros((16 - 2 * latent_count, width), BF)
    outgoing = collect(jnp.concatenate([grad_inputs, *parts(d_cond_part), no_rows], axis=0))
    proj_gram = lax.cond(
        dp_rank == OWNERS[2],
        lambda *rows: gram_blocks(rows[0], ["plain"] * size, *rows[1:]),
        lambda *rows: none,
        me_index,
        *proj_rows,
    )
    is_late = (dp_rank == OWNERS[0]) | (dp_rank == OWNERS[1])
    gram = jnp.where(dp_rank == OWNERS[2], proj_gram, jnp.where(is_late, late, early))
    gram, output = lax.optimization_barrier((gram, output))
    factor = newton_schulz_factor(me_index, gram, width)
    factor, outgoing = lax.optimization_barrier((factor, outgoing))
    grad_inputs = jnp.concatenate([piece[:chunk] for piece in outgoing], axis=0)
    grad_inputs = reorder(grad_inputs, size, me).reshape(inputs.shape)
    d_cond_act = sum(
        total(split(piece[chunk : chunk + 2 * latent_count], 2)) for piece in outgoing
    )
    grad_condition = silu_pull(d_cond_act)[0]
    column_width = width // dp_size
    column_start = dp_rank * column_width
    factors = reorder(factor, masks, dp_rank).reshape(dp_size, column_width, width)
    factors = dp_all_to_all(factors, OWNERS)
    owner_places = jnp.stack(
        [(place ^ places[owner]).astype(jnp.int32) for owner in OWNERS]
    )

    weights_old = (w_ada_old, w_qkv_old, w_proj_old, w_up_old, w_down_old)
    sizes = [max(w.size // width * size, width) for w in weights_old]
    columns = [
        lax.dynamic_slice_in_dim(flat(w), column_start, column_width, 1) for w in weights_old
    ]
    new_weights = update_weights(owner_places, starts, columns, factors, sizes)
    new_weights = [
        new.reshape(old.shape[:-1] + (column_width,))
        for new, old in zip(new_weights, weights_old)
    ]
    new_bias_first = BETA_ONE * bias_first + (1.0 - BETA_ONE) * grad_biases
    new_bias_second = BETA_TWO * bias_second + (1.0 - BETA_TWO) * grad_biases * grad_biases
    first_hat = new_bias_first / (1.0 - BETA_ONE**STEP)
    second_hat = new_bias_second / (1.0 - BETA_TWO**STEP)
    new_biases = biases - ADAM_RATE * first_hat / (jnp.sqrt(second_hat) + ADAM_EPS)
    return (
        output,
        grad_inputs,
        grad_condition,
        *new_weights,
        moments[0].reshape(momentum_ada.shape),
        moments[1].reshape(momentum_qkv.shape),
        moments[2],
        moments[3].reshape(momentum_up.shape),
        moments[4].reshape(momentum_down.shape),
        new_biases,
        new_bias_first,
        new_bias_second,
    )


def solution(mesh):
    placed = (
        P("dp", None, None),
        P("dp", None),
        P("dp", None, None),
        P(None, "tensor", None),
        P(None, "tensor", None),
        P("tensor", None),
        P(None, "tensor", None),
        P(None, "tensor", None),
        P(None, "tensor"),
        P(None, "tensor", None),
        P(None, "tensor", None),
        P("tensor", None),
        P(None, "tensor", None),
        P(None, "tensor", None),
        P(None, "tensor"),
        P(None, "tensor"),
    )
    return jax.shard_map(
        on_device,
        mesh=mesh,
        in_specs=placed,
        out_specs=(
            P("dp", None, None),
            P("dp", None, None),
            P("dp", None),
            P(None, "tensor", "dp"),
            P(None, "tensor", "dp"),
            P("tensor", "dp"),
            P(None, "tensor", "dp"),
            P(None, "tensor", "dp"),
            P(None, "tensor", None),
            P(None, "tensor", None),
            P("tensor", None),
            P(None, "tensor", None),
            P(None, "tensor", None),
            P(None, "tensor"),
            P(None, "tensor"),
            P(None, "tensor"),
        ),
        check_vma=False,
    )
```

```python
import functools
import math

import jax
import jax.numpy as jnp
from jax import lax
from jax.experimental import pallas as pl
from jax.experimental.pallas import tpu as pltpu
from jax.sharding import PartitionSpec as P

HEAD_DIM = 64
NS_ITERS = 5
STEP = 10


NS_A = 3.4445
NS_B = -4.775
NS_C = 2.0315
MUON_RATE = 0.16
MUON_DECAY = 0.01
MUON_MOMENTUM = 0.95
ADAM_RATE = 0.25
BETA_ONE = 0.9
BETA_TWO = 0.999
ADAM_EPS = 1e-08
NORM_EPS = 1e-06

BF = jnp.bfloat16
F32 = jnp.float32
TILE = 256
HALF = 128
VMEM_LIMIT = 28 * 1024 * 1024
OWNERS = (0, 2, 5, 4, 6)


def dot(a, b):
    return jnp.dot(a, b, preferred_element_type=F32)


def dot_t(a, b):
    return lax.dot_general(a, b, (((1,), (1,)), ((), ())), preferred_element_type=F32)


def t_dot(a, b):
    return lax.dot_general(a, b, (((0,), (0,)), ((), ())), preferred_element_type=F32)


def parts(value):
    high = value.astype(BF)
    return high, (value - high.astype(F32)).astype(BF)


def blocks_of(count):
    return [(i, j) for i in range(count) for j in range(i, count)]


def half_blocks(count):
    return [(i, j, half) for i, j in blocks_of(count) for half in range(2)]


def half_rows(index, total, me_ref, size):
    per_chunk = total // size
    place = (index // per_chunk) ^ me_ref[0]
    return pl.ds(pl.multiple_of(place * (per_chunk * HALF) + index % per_chunk * HALF, HALF), HALF)


def gram_kernel(size, kinds, me_ref, *refs):
    out_ref, rows_ref = refs[-2:]
    refs, first = list(refs[:-2]), 0
    for kind in kinds:
        rows = refs.pop(0)[...]
        if kind != "plain":
            grad = refs.pop(0)[...]
            if kind == "outer":
                grad = t_dot(grad, refs.pop(0)[...])
            rows = MUON_MOMENTUM * rows + grad.astype(F32)
            if kind == "masked":
                rows = jnp.where(refs.pop(0)[...] > 0.0, rows, 0.0)
        last = first + rows.shape[0]
        rows_ref[first:last, :] = rows.astype(BF)
        first = last
    halves = half_blocks(rows_ref.shape[1] // TILE)
    for index, (i, j, half) in enumerate(halves):
        left = slice(i * TILE + half * HALF, i * TILE + (half + 1) * HALF)
        right = slice(j * TILE, (j + 1) * TILE)
        out_ref[half_rows(index, len(halves), me_ref, size), :] = t_dot(
            rows_ref[:, left], rows_ref[:, right]
        )


def gram_blocks(me, kinds, *operands):
    taken = {"plain": 1, "grad": 2, "masked": 3, "outer": 3}
    depth, place = 0, 0
    for kind in kinds:
        depth += operands[place].shape[0]
        place += taken[kind]
    width = operands[0].shape[1]
    count = len(half_blocks(width // TILE))
    return pl.pallas_call(
        functools.partial(gram_kernel, lax.axis_size("tensor"), kinds),
        in_specs=[pl.BlockSpec(memory_space=pltpu.SMEM)]
        + [pl.BlockSpec(memory_space=pltpu.VMEM)] * len(operands),
        out_shape=jax.ShapeDtypeStruct((count * HALF, TILE), F32),
        scratch_shapes=[pltpu.VMEM((depth, width), BF)],
        compiler_params=pltpu.CompilerParams(vmem_limit_bytes=VMEM_LIMIT),
        cost_estimate=pl.CostEstimate(
            flops=2 * depth * width * width, bytes_accessed=depth * width * 6, transcendentals=0
        ),
    )(me, *operands)


def newton_schulz_kernel(size, pick_ref, *refs):
    (blocks, cur, high, rest, poly, mid_h, mid_l, f_h, f_l, g_h, g_l) = refs[-11:]
    early_ref, proj_ref, *late_refs, out_ref = refs[:-11]
    width = cur.shape[0]
    spans = [slice(i * TILE, (i + 1) * TILE) for i in range(width // TILE)]
    halves = half_blocks(width // TILE)
    rows = blocks.shape[0] // size
    sources = [
        lambda p: early_ref[p * rows : (p + 1) * rows, :],
        lambda p: late_refs[p][...],
        lambda p: proj_ref[p * rows : (p + 1) * rows, :],
    ]
    for index, source in enumerate(sources):

        @pl.when(pick_ref[1] == index)
        def _(source=source):
            for p in range(size):
                place = pl.multiple_of((pick_ref[0] ^ p) * rows, rows)
                blocks[pl.ds(place, rows), :] = source(p)

    for index, (i, j, half) in enumerate(halves):
        block = blocks[index * HALF : (index + 1) * HALF, :]
        left = slice(i * TILE + half * HALF, i * TILE + (half + 1) * HALF)
        cur[left, spans[j]] = block
        if i != j:
            cur[spans[j], left] = block.T
    square_norm = jnp.zeros((1, 1), F32)
    row = lax.broadcasted_iota(jnp.int32, (TILE, TILE), 0)
    col = lax.broadcasted_iota(jnp.int32, (TILE, TILE), 1)
    for span in spans:
        square_norm += jnp.sum(jnp.where(row == col, cur[span, span], 0.0), keepdims=True)
    scale = 1.0 / (jnp.sqrt(square_norm) + 1e-07)
    for span in spans:
        cur[span, :] = cur[span, :] * (scale * scale)

    def make_poly():
        for span in spans:
            high[span, :], rest[span, :] = parts(cur[span, :])
        for span in spans:
            poly[span, :] = (NS_B * cur[span, :] + NS_C * dot(high[span, :], high[...])).astype(BF)

    def step_gram():
        for span in spans:
            half = (
                NS_A * cur[span, :] + dot(high[span, :], poly[...]) + dot(rest[span, :], poly[...])
            )
            mid_h[span, :], mid_l[span, :] = parts(half)
        for span in spans:
            half = mid_h[span, :].astype(F32) + mid_l[span, :].astype(F32)
            cur[span, :] = (
                NS_A * half + dot(poly[span, :], mid_h[...]) + dot(poly[span, :], mid_l[...])
            )

    def stepped_factor(span):
        before = f_h[span, :].astype(F32) + f_l[span, :].astype(F32)
        return NS_A * before + dot(poly[span, :], f_h[...]) + dot(poly[span, :], f_l[...])

    make_poly()
    wide_row = lax.broadcasted_iota(jnp.int32, (TILE, width), 0)
    wide_col = lax.broadcasted_iota(jnp.int32, (TILE, width), 1)
    for i, span in enumerate(spans):
        start = poly[span, :].astype(F32) + jnp.where(wide_row + i * TILE == wide_col, NS_A, 0.0)
        f_h[span, :], f_l[span, :] = parts(start)
    step_gram()

    def middle(_, carry):
        make_poly()
        for span in spans:
            g_h[span, :], g_l[span, :] = parts(stepped_factor(span))
        f_h[...] = g_h[...]
        f_l[...] = g_l[...]
        step_gram()
        return carry

    lax.fori_loop(0, NS_ITERS - 2, middle, 0)
    make_poly()
    for span in spans:
        out_ref[span, :] = (stepped_factor(span) * scale).astype(out_ref.dtype)


def newton_schulz_factor(pick, early, proj, late, width):
    whole = lambda kind: pltpu.VMEM((width, width), kind)
    return pl.pallas_call(
        functools.partial(newton_schulz_kernel, lax.axis_size("tensor")),
        in_specs=[pl.BlockSpec(memory_space=pltpu.SMEM)]
        + [pl.BlockSpec(memory_space=pltpu.VMEM)] * (2 + len(late)),
        out_shape=jax.ShapeDtypeStruct((width, width), BF),
        scratch_shapes=[pltpu.VMEM(proj.shape, F32), whole(F32)] + [whole(BF)] * 9,
        compiler_params=pltpu.CompilerParams(vmem_limit_bytes=VMEM_LIMIT),
        cost_estimate=pl.CostEstimate(
            flops=2 * 29 * width**3, bytes_accessed=width * width * 6, transcendentals=0
        ),
    )(pick, early, proj, *late)


def update_kernel(sizes, place_ref, *refs):
    count = len(sizes)
    rows, weights, factor, outs = refs[:count], refs[count : 2 * count], refs[2 * count], refs[2 * count + 1 :]
    for k, size in enumerate(sizes):
        ortho = dot_t(rows[k][...], factor[place_ref[k]])
        outs[k][...] = (
            weights[k][...] * (1.0 - MUON_RATE * MUON_DECAY)
            - MUON_RATE * 0.2 * math.sqrt(size) * ortho
        )


def update_weights(places, rows, weights, factors, sizes):
    return pl.pallas_call(
        functools.partial(update_kernel, sizes),
        in_specs=[pl.BlockSpec(memory_space=pltpu.SMEM)]
        + [pl.BlockSpec(memory_space=pltpu.VMEM)] * (2 * len(sizes) + 1),
        out_shape=[jax.ShapeDtypeStruct(w.shape, F32) for w in weights],
        compiler_params=pltpu.CompilerParams(vmem_limit_bytes=VMEM_LIMIT),
        cost_estimate=pl.CostEstimate(
            flops=sum(2 * r.size * w.shape[1] for r, w in zip(rows, weights)),
            bytes_accessed=sum(2 * r.size + 12 * w.size for r, w in zip(rows, weights)),
            transcendentals=0,
        ),
    )(places, *rows, *weights, factors)


def put_pieces(refs, scratch):
    step = pl.program_id(0)
    rows = refs[0].shape[0]
    per_step = scratch.shape[0] // rows
    for index, ref in enumerate(refs):
        k = index % per_step

        @pl.when(step == index // per_step)
        def _(ref=ref, k=k):
            ref[...] = scratch[k * rows : (k + 1) * rows, :]


def take_pieces(refs, scratch):
    step = pl.program_id(0)
    rows = refs[0].shape[0]
    per_step = scratch.shape[0] // rows
    for index, ref in enumerate(refs):
        k = index % per_step

        @pl.when(step == index // per_step)
        def _(ref=ref, k=k):
            scratch[k * rows : (k + 1) * rows, :] = ref[...]


def attention_kernel(
    count, x_ref, mod_ref, w_ref, proj_ref, bias_ref, hidden_ref, heads_ref, attended_ref, *refs
):
    quarter = proj_ref.shape[0]
    normed, _ = normed_of(x_ref[...].astype(F32))
    hidden = (normed * (1.0 + mod_ref[0, 1:2, :]) + mod_ref[0, 0:1, :]).astype(BF)
    hidden_ref[...] = hidden
    queries = (dot_t(hidden, w_ref[:quarter, :]) + bias_ref[0:1, :]).astype(BF)
    keys = dot_t(hidden, w_ref[quarter : 2 * quarter, :]).astype(BF)
    values = (dot_t(hidden, w_ref[2 * quarter :, :]) + bias_ref[1:2, :]).astype(BF)
    heads_ref[0] = queries
    heads_ref[1] = keys
    heads_ref[2] = values
    attended = []
    for start in range(0, quarter, HEAD_DIM):
        head = slice(start, start + HEAD_DIM)
        probs = softmax_of(queries[:, head], keys[:, head]).astype(BF)
        attended.append(dot(probs, values[:, head]))
    attended = jnp.concatenate(attended, axis=1).astype(BF)
    attended_ref[...] = attended
    part = refs[-1]
    part[...] = dot(attended, proj_ref[...]).astype(BF)
    put_pieces(refs[:-1], part)


def softmax_of(queries, keys):
    scores = dot_t(queries, keys) * (1.0 / math.sqrt(HEAD_DIM))
    raised = jnp.exp(scores - jnp.max(scores, axis=-1, keepdims=True))
    return raised * (1.0 / jnp.sum(raised, axis=-1, keepdims=True))


def attention(tokens_in, modulation, qkv_low, proj_low, bias_rows, seq_length, count):
    tokens, width = tokens_in.shape
    quarter = proj_low.shape[0]
    rows = lambda last: pl.BlockSpec((seq_length, last), lambda i: (i, 0))
    whole = lambda shape: pl.BlockSpec(shape, lambda i: (0,) * len(shape))
    piece = (tokens // count, width)
    out = pl.pallas_call(
        functools.partial(attention_kernel, count),
        grid=(tokens // seq_length,),
        in_specs=[
            rows(width),
            pl.BlockSpec((1, 6, width), lambda i: (i, 0, 0)),
            whole(qkv_low.shape),
            whole(proj_low.shape),
            whole(bias_rows.shape),
        ],
        out_specs=[
            rows(width),
            pl.BlockSpec((3, seq_length, quarter), lambda i: (0, i, 0)),
            rows(quarter),
        ]
        + [whole(piece)] * count,
        out_shape=[
            jax.ShapeDtypeStruct((tokens, width), BF),
            jax.ShapeDtypeStruct((3, tokens, quarter), BF),
            jax.ShapeDtypeStruct((tokens, quarter), BF),
        ]
        + [jax.ShapeDtypeStruct(piece, BF)] * count,
        scratch_shapes=[pltpu.VMEM((seq_length, width), BF)],
        compiler_params=pltpu.CompilerParams(vmem_limit_bytes=VMEM_LIMIT),
        cost_estimate=pl.CostEstimate(
            flops=8 * tokens * width * quarter + 4 * tokens * seq_length * quarter,
            bytes_accessed=tokens * width * 8 + qkv_low.size * 3,
            transcendentals=tokens * seq_length * quarter // HEAD_DIM,
        ),
    )(tokens_in, modulation, qkv_low, proj_low, bias_rows)
    return out[0], out[1], out[2], out[3:]


def attention_back_kernel(count, heads_ref, w_ref, proj_ref, *refs):
    grad_refs, (d_heads_ref, sums_ref) = refs[:count], refs[count : count + 2]
    part_refs, grad = refs[count + 2 : -1], refs[-1]
    take_pieces(grad_refs, grad)
    quarter = proj_ref.shape[0]
    scale = 1.0 / math.sqrt(HEAD_DIM)
    d_attended = dot_t(grad[...], proj_ref[...]).astype(BF)
    queries, keys, values = heads_ref[0], heads_ref[1], heads_ref[2]
    d_queries, d_keys, d_values = [], [], []
    for start in range(0, quarter, HEAD_DIM):
        head = slice(start, start + HEAD_DIM)
        probs = softmax_of(queries[:, head], keys[:, head])
        d_out = d_attended[:, head]
        d_values.append(t_dot(probs.astype(BF), d_out))
        d_probs = dot_t(d_out, values[:, head])
        d_scores = (
            probs * (d_probs - jnp.sum(probs * d_probs, axis=-1, keepdims=True))
        ).astype(BF)
        d_queries.append(dot(d_scores, keys[:, head]) * scale)
        d_keys.append(t_dot(d_scores, queries[:, head]) * scale)
    d_queries = jnp.concatenate(d_queries, axis=1)
    d_values = jnp.concatenate(d_values, axis=1)
    sums_ref[0, 0:1, :] = jnp.sum(d_queries, axis=0, keepdims=True)
    sums_ref[0, 1:2, :] = jnp.sum(d_values, axis=0, keepdims=True)
    d_queries = d_queries.astype(BF)
    d_keys = jnp.concatenate(d_keys, axis=1).astype(BF)
    d_values = d_values.astype(BF)
    d_heads_ref[0] = d_queries
    d_heads_ref[1] = d_keys
    d_heads_ref[2] = d_values
    part = (
        dot(d_queries, w_ref[:quarter, :])
        + dot(d_keys, w_ref[quarter : 2 * quarter, :])
        + dot(d_values, w_ref[2 * quarter :, :])
    )
    grad[...] = part.astype(BF)
    put_pieces(part_refs, grad)


def attention_back(grads, heads, qkv_low, proj_low, seq_length):
    count = len(grads)
    rows, width = grads[0].shape
    tokens = rows * count
    quarter = proj_low.shape[0]
    whole = lambda shape: pl.BlockSpec(shape, lambda i: (0,) * len(shape))
    of_heads = pl.BlockSpec((3, seq_length, quarter), lambda i: (0, i, 0))
    out = pl.pallas_call(
        functools.partial(attention_back_kernel, count),
        grid=(tokens // seq_length,),
        in_specs=[of_heads, whole(qkv_low.shape), whole(proj_low.shape)]
        + [whole(grads[0].shape)] * count,
        out_specs=[of_heads, pl.BlockSpec((1, 2, quarter), lambda i: (i, 0, 0))]
        + [whole(grads[0].shape)] * count,
        out_shape=[
            jax.ShapeDtypeStruct(heads.shape, BF),
            jax.ShapeDtypeStruct((tokens // seq_length, 2, quarter), F32),
        ]
        + [jax.ShapeDtypeStruct(grads[0].shape, BF)] * count,
        scratch_shapes=[pltpu.VMEM((seq_length, width), BF)],
        compiler_params=pltpu.CompilerParams(vmem_limit_bytes=VMEM_LIMIT),
        cost_estimate=pl.CostEstimate(
            flops=8 * tokens * width * quarter + 10 * tokens * seq_length * quarter,
            bytes_accessed=tokens * width * 8 + qkv_low.size * 3,
            transcendentals=tokens * seq_length * quarter // HEAD_DIM,
        ),
    )(heads, qkv_low, proj_low, *grads)
    return out[0], out[1], out[2:]


def feed_forward_kernel(count, grad_ref, up_ref, down_ref, bias_ref, *refs):
    hidden_refs, (act_ref, d_pre_ref, sums_ref) = refs[:count], refs[count : count + 3]
    part_refs, hidden = refs[count + 3 : -1], refs[-1]
    take_pieces(hidden_refs, hidden)
    pre = dot_t(hidden[...], up_ref[...]) + bias_ref[...]
    d_act = dot_t(grad_ref[...], down_ref[...])
    root = math.sqrt(2.0 / math.pi)
    square = pre * pre
    bent = jnp.tanh(root * pre * (1.0 + 0.044715 * square))
    half = 0.5 * (1.0 + bent)
    act_ref[...] = (pre * half).astype(BF)
    slope = half + 0.5 * pre * (1.0 - bent * bent) * (root * (1.0 + 0.134145 * square))
    d_pre = d_act * slope

    @pl.when(pl.program_id(0) == 0)
    def _():
        sums_ref[...] = jnp.zeros_like(sums_ref)

    sums_ref[...] += jnp.sum(d_pre, axis=0, keepdims=True)
    d_pre = d_pre.astype(BF)
    d_pre_ref[...] = d_pre
    hidden[...] = dot(d_pre, up_ref[...]).astype(BF)
    put_pieces(part_refs, hidden)


def feed_forward(hidden, grad, up_low, down_low, bias):
    count = len(hidden)
    tokens, width = grad.shape
    units = up_low.shape[0]
    block = tokens // 2
    rows = lambda last: pl.BlockSpec((block, last), lambda i: (i, 0))
    whole = lambda shape: pl.BlockSpec(shape, lambda i: (0,) * len(shape))
    out = pl.pallas_call(
        functools.partial(feed_forward_kernel, count),
        grid=(tokens // block,),
        in_specs=[rows(width), whole(up_low.shape), whole(down_low.shape), whole((1, units))]
        + [whole(hidden[0].shape)] * count,
        out_specs=[rows(units), rows(units), whole((1, units))]
        + [whole(hidden[0].shape)] * count,
        out_shape=[
            jax.ShapeDtypeStruct((tokens, units), BF),
            jax.ShapeDtypeStruct((tokens, units), BF),
            jax.ShapeDtypeStruct((1, units), F32),
        ]
        + [jax.ShapeDtypeStruct(hidden[0].shape, BF)] * count,
        scratch_shapes=[pltpu.VMEM((block, width), BF)],
        compiler_params=pltpu.CompilerParams(vmem_limit_bytes=VMEM_LIMIT),
        cost_estimate=pl.CostEstimate(
            flops=6 * tokens * width * units,
            bytes_accessed=tokens * width * 10 + up_low.size * 4,
            transcendentals=tokens * units,
        ),
    )(grad, up_low, down_low, bias, *hidden)
    return out[0], out[1], out[2], out[3:]


def dp_swap(piece, mask, ranks=None):
    ranks = range(lax.axis_size("dp")) if ranks is None else ranks
    return lax.ppermute(piece, "dp", [(i, i ^ mask) for i in ranks])


def dp_all_to_all(value, ranks):
    shape = value.shape
    for step, radix in dp_levels():
        lower = dp_masks().index(step)
        value = value.reshape((-1, radix, lower) + shape[1:])
        value = jnp.stack(
            [value[:, 0]] + [dp_swap(value[:, j], j * step, ranks) for j in range(1, radix)], axis=1
        )
        ranks = None
    return value.reshape(shape)


def dp_levels():
    size, step, levels = lax.axis_size("dp"), 2, []
    while step < size:
        radix = min(4, size // step)
        levels.append((step, radix))
        step *= radix
    return levels + [(1, 2)]


def bit_levels():
    levels = []
    for step, radix in dp_levels():
        levels += [(step << bit, 2) for bit in range(radix.bit_length() - 1)]
    return levels


def dp_masks():
    masks = [0]
    for step, radix in dp_levels():
        masks = [j * step + mask for j in range(radix) for mask in masks]
    return masks


def dp_collect(piece, levels=None):
    gathered = piece[None]
    for step, radix in dp_levels() if levels is None else levels:
        gathered = jnp.concatenate(
            [gathered] + [dp_swap(gathered, j * step) for j in range(1, radix)], axis=0
        )
    return gathered


def dp_scatter_sum(value, levels):
    for step, radix in reversed(levels):
        value = value.reshape((radix, -1) + value.shape[1:])
        summed = value[0].astype(F32)
        for j in range(1, radix):
            summed = summed + dp_swap(value[j], j * step).astype(F32)
        value = summed.astype(BF)
    return value


def dp_places():
    masks, rank = dp_masks(), place_of("dp")
    place, bit = jnp.uint32(0), 0
    while 1 << bit < len(masks):
        place = place | (((rank >> bit) & 1) * masks.index(1 << bit))
        bit += 1
    return [masks.index(p) for p in range(len(masks))], place


def place_of(axis):
    return lax.axis_index(axis).astype(jnp.uint32)


def swap(piece, mask, ranks=None):
    size = lax.axis_size("tensor")
    if ranks is None:
        return lax.ppermute(piece, "tensor", [(i, i ^ mask) for i in range(size)])
    pairs = [(r * size + i, r * size + (i ^ mask)) for r in ranks for i in range(size)]
    return lax.ppermute(piece, ("dp", "tensor"), pairs)


def split(value, count):
    rows = value.shape[0] // count
    return [value[k * rows : (k + 1) * rows] for k in range(count)]


def scatter(pieces, ranks=None):
    return [pieces[0]] + [swap(pieces[mask], mask, ranks) for mask in range(1, len(pieces))]


def total(pieces):
    return sum([piece.astype(F32) for piece in pieces[1:]], pieces[0].astype(F32))


def halving_first(pieces, ranks=None):
    sent = jnp.concatenate(pieces[1::2], axis=0)
    return swap(sent, 1, ranks)


def halving_kept(pieces, arrived):
    rows = pieces[0].shape[0]
    return [
        total([piece, arrived[k * rows : (k + 1) * rows]]) for k, piece in enumerate(pieces[::2])
    ]


def scatter_halving(pieces, ranks=None):
    kept = halving_kept(pieces, halving_first(pieces, ranks))
    return total([kept[0], swap(kept[1].astype(pieces[0].dtype), 2, ranks)])


def collect_doubling(piece, ranks=None):
    pair = jnp.stack([piece, swap(piece, 2, ranks)])
    pairs = jnp.stack([pair, swap(pair, 1, ranks)], axis=1)
    return pairs.reshape((-1,) + piece.shape[1:])


def collect(piece, ranks=None):
    size = lax.axis_size("tensor")
    return [piece] + [swap(piece, mask, ranks) for mask in range(1, size)]


def reorder(value, masks, index):
    masks = list(range(masks)) if isinstance(masks, int) else masks
    rows = value.shape[0] // len(masks)
    return jnp.concatenate(
        [lax.dynamic_slice_in_dim(value, (index ^ p) * rows, rows, 0) for p in masks], axis=0
    )


def normed_of(values):
    average = jnp.mean(values, axis=-1, keepdims=True)
    centered = values - average
    variance = jnp.mean(centered * centered, axis=-1, keepdims=True)
    inverse = lax.rsqrt(variance + NORM_EPS)
    return centered * inverse, inverse


def norm_back(normed, inverse, grad):
    return (
        grad
        - jnp.mean(grad, axis=-1, keepdims=True)
        - normed * jnp.mean(grad * normed, axis=-1, keepdims=True)
    ) * inverse


def on_device(
    inputs,
    condition,
    cotangent,
    w_ada,
    w_qkv,
    w_proj,
    w_up,
    w_down,
    biases,
    momentum_ada,
    momentum_qkv,
    momentum_proj,
    momentum_up,
    momentum_down,
    bias_first,
    bias_second,
):
    quarter = w_ada.shape[1]
    width = w_ada.shape[-1]
    latent_count = inputs.shape[0]
    seq_length = inputs.shape[1]
    tokens = latent_count * seq_length
    heads_here = quarter // HEAD_DIM
    size = lax.axis_size("tensor")
    me = place_of("tensor")
    dp_size = lax.axis_size("dp")
    dp_rank = place_of("dp")
    chunk = tokens // size
    my_latent = me // (size // latent_count)
    scale_factor = 1.0 / math.sqrt(HEAD_DIM)
    flat = lambda w: w.reshape(-1, width)
    ada_low = flat(w_ada).astype(BF)
    qkv_low = flat(w_qkv).astype(BF)
    proj_low = w_proj.astype(BF)
    up_bias = biases[9:13].reshape(-1)

    cond_act, silu_pull = jax.vjp(jax.nn.silu, condition.astype(F32))
    cond_low = cond_act.astype(BF)
    mod_part = dot_t(cond_low, ada_low).reshape(latent_count * 6, quarter) + jnp.tile(
        biases[0:6], (latent_count, 1)
    )
    mod_part = jnp.concatenate([mod_part, biases[8:9], biases[13:14]], axis=0)
    gathered = jnp.concatenate(collect(mod_part[None]), axis=0)
    gathered = reorder(gathered, size, me)
    gathered = jnp.moveaxis(gathered, 0, 1).reshape(-1, width)
    modulation = reorder(gathered[: latent_count * 6], latent_count, my_latent).reshape(
        latent_count, 6, width
    )
    bias_proj = gathered[latent_count * 6]
    bias_down = gathered[latent_count * 6 + 1]
    shift_first, scale_first, gate_first = modulation[0, 0], modulation[0, 1], modulation[0, 2]
    shift_second, scale_second, gate_second = modulation[0, 3], modulation[0, 4], modulation[0, 5]

    tokens_in = reorder(inputs.reshape(tokens, width), size, me)
    tangent = reorder(cotangent.reshape(tokens, width), size, me)
    first_low, heads, attended_low, partial_first = attention(
        tokens_in, modulation, qkv_low, proj_low, biases[6:8], seq_length, size
    )
    partial_first, w_up, w_down = lax.optimization_barrier((partial_first, w_up, w_down))
    up_low = flat(w_up).astype(BF)
    down_low = flat(w_down).astype(BF)
    own = tokens_in[:chunk].astype(F32)
    tangent_own = tangent[:chunk].astype(F32)

    branch_first = total(scatter(partial_first)) + bias_proj
    middle = own + gate_first * branch_first
    normed_second, inverse_second = normed_of(middle)
    second_pieces = collect((normed_second * (1.0 + scale_second) + shift_second).astype(BF))

    d_branch_second = (
        tangent.astype(F32).reshape(latent_count, seq_length, width)
        * modulation[:, 5][:, None, :]
    ).reshape(tokens, width)
    d_down_bias = jnp.sum(d_branch_second, axis=0)
    d_second_low = d_branch_second.astype(BF)
    act_low, d_pre_low, d_up_bias, second_part = feed_forward(
        second_pieces, d_second_low, up_low, down_low, up_bias[None]
    )
    second_low = jnp.concatenate(second_pieces, axis=0)
    d_up_bias = d_up_bias.reshape(-1, quarter)
    partial_second = dot(act_low, down_low)
    second_latents = partial_second.reshape(latent_count, seq_length, width)
    d_gate_second = jnp.sum(
        tangent.astype(F32).reshape(second_latents.shape) * second_latents, axis=1
    )
    d_gate_second = d_gate_second.at[0].add(bias_down * jnp.sum(tangent_own, axis=0))
    output_part = (second_latents * modulation[:, 5][:, None, :]).reshape(tokens, width)
    output_part = jnp.concatenate(
        [output_part[:chunk] + (middle + gate_second * bias_down), output_part[chunk:]], axis=0
    ).astype(BF)

    d_hidden_second = total(scatter(second_part))
    (
        d_hidden_second,
        cond_low,
        momentum_ada,
        momentum_qkv,
        momentum_proj,
        momentum_up,
        momentum_down,
        w_ada_old,
        w_qkv_old,
        w_proj_old,
        w_up_old,
        w_down_old,
    ) = lax.optimization_barrier(
        (
            d_hidden_second,
            cond_low,
            momentum_ada,
            momentum_qkv,
            momentum_proj,
            momentum_up,
            momentum_down,
            w_ada,
            w_qkv,
            w_proj,
            w_up,
            w_down,
        )
    )

    grad_down = t_dot(act_low, d_second_low).astype(BF)
    grad_up = t_dot(d_pre_low, second_low).astype(BF)
    grad_up, grad_down = lax.psum((grad_up, grad_down), "dp")

    d_shift_second = jnp.sum(d_hidden_second, axis=0)
    d_scale_second = jnp.sum(d_hidden_second * normed_second, axis=0)
    d_middle = tangent_own + norm_back(
        normed_second, inverse_second, d_hidden_second * (1.0 + scale_second)
    )
    d_branch_first = gate_first * d_middle
    d_gate_first = jnp.sum(d_middle * branch_first, axis=0)
    d_proj_bias = jnp.sum(d_branch_first, axis=0)
    d_first_pieces = collect(d_branch_first.astype(BF))

    output_part, d_first_pieces = lax.optimization_barrier(
        (reorder(output_part, size, me), d_first_pieces)
    )
    output = lax.psum(output_part, "tensor").reshape(inputs.shape)
    d_heads, d_head_sums, first_part = attention_back(
        d_first_pieces, heads, qkv_low, proj_low, seq_length
    )
    d_first_low = jnp.concatenate(d_first_pieces, axis=0)
    grad_proj = t_dot(attended_low, d_first_low).astype(BF)
    d_head_bias = jnp.sum(d_head_sums, axis=0)
    grad_qkv = jnp.concatenate([t_dot(d_heads[k], first_low) for k in range(3)], axis=0).astype(BF)
    late_rows = 3 * quarter + proj_low.shape[0]
    masks, levels = dp_masks(), dp_levels()
    late_momentum = split(
        reorder(jnp.concatenate([flat(momentum_qkv), momentum_proj], axis=0), masks, dp_rank), 2
    )
    of_qkv = (jnp.asarray(masks, jnp.uint32) ^ dp_rank) * (late_rows // dp_size) < 3 * quarter
    of_qkv = jnp.repeat(of_qkv.astype(F32), late_rows // dp_size).reshape(2, -1, 1)
    late_grads = reorder(jnp.concatenate([grad_qkv, grad_proj], axis=0), masks, dp_rank)
    late_grads = late_grads.reshape(dp_size, -1, width)
    late_grads = dp_scatter_sum(late_grads, levels[-1:])
    late_grads, first_part = lax.optimization_barrier((late_grads, first_part))
    late_grads = dp_collect(dp_scatter_sum(late_grads, levels[:-1])[0], levels[:-1])
    d_hidden_first = scatter_halving(first_part)
    cond_all = dp_collect(cond_low, bit_levels()).reshape(-1, width)

    me_index = me.astype(jnp.int32).reshape(1)
    none = jnp.zeros((len(half_blocks(width // TILE)) * HALF, TILE), F32)
    turn = jnp.where(dp_rank == OWNERS[3], 1, jnp.where(dp_rank == OWNERS[4], 2, 0))
    early = lax.switch(
        turn,
        [
            lambda *rows: none,
            lambda *rows: gram_blocks(rows[0], ["grad"], *rows[1:3]),
            lambda *rows: gram_blocks(rows[0], ["grad"], *rows[3:5]),
        ],
        me_index,
        flat(momentum_up),
        grad_up,
        flat(momentum_down),
        grad_down,
    )
    early, late_grads = lax.optimization_barrier((early, late_grads))
    early_ranks = OWNERS[3:5]
    early = scatter_halving(split(early, size), early_ranks)
    late_grads = [
        grads.reshape(-1, width) for grads in (late_grads, dp_swap(late_grads, levels[-1][0]))
    ]

    normed_own, inverse_own = normed_of(own)
    d_shift_first = jnp.sum(d_hidden_first, axis=0)
    d_scale_first = jnp.sum(d_hidden_first * normed_own, axis=0)
    grad_inputs = d_middle + norm_back(
        normed_own, inverse_own, d_hidden_first * (1.0 + scale_first)
    )
    grad_inputs = grad_inputs.astype(BF)

    sums = jnp.stack(
        [
            d_shift_first,
            d_scale_first,
            d_gate_first,
            d_shift_second,
            d_scale_second,
            d_proj_bias,
            *d_gate_second,
        ]
    )
    of_device = [
        lax.dynamic_slice_in_dim(sums, (me ^ mask) * quarter, quarter, 1) for mask in range(size)
    ]
    mine, others = halving_kept(of_device, halving_first(of_device))
    others = swap(others, 2)
    d_proj_own = mine[5] + others[5]
    d_mod_own = jnp.stack(
        [
            jnp.concatenate([mine[:5], (mine[6] + others[7])[None]], axis=0),
            jnp.concatenate([others[:5], (mine[7] + others[6])[None]], axis=0),
        ]
    )
    d_mod_own = reorder(d_mod_own, latent_count, my_latent)
    d_cond_part = dot(
        d_mod_own.reshape(latent_count, -1).astype(BF), flat(w_ada_old).astype(BF)
    )
    d_down_own = lax.dynamic_slice_in_dim(d_down_bias, me * quarter, quarter, 0)
    small = jnp.concatenate(
        [
            d_mod_own.reshape(-1, quarter),
            d_head_bias,
            d_proj_own[None],
            d_up_bias,
            d_down_own[None],
        ],
        axis=0,
    )
    small_all = dp_collect(small, bit_levels())
    d_mod_all = small_all[:, : 6 * latent_count].reshape(-1, 6, quarter)
    grad_biases = jnp.concatenate(
        [jnp.sum(d_mod_all, axis=0), jnp.sum(small_all[:, 6 * latent_count :], axis=0)], axis=0
    )
    d_mod_low = d_mod_all.reshape(d_mod_all.shape[0], -1).astype(BF)

    turn = jnp.where(dp_rank == OWNERS[0], 1, jnp.where(dp_rank == OWNERS[1], 2, 0))
    late = lax.switch(
        turn,
        [
            lambda *rows: none,
            lambda *rows: gram_blocks(rows[0], ["outer"], *rows[1:4]),
            lambda *rows: gram_blocks(rows[0], ["masked"] * 2, *rows[4:]),
        ],
        me_index,
        flat(momentum_ada),
        d_mod_low,
        cond_all,
        late_momentum[0],
        late_grads[0],
        of_qkv[0],
        late_momentum[1],
        late_grads[1],
        of_qkv[1],
    )
    late_ranks = OWNERS[:2]
    late, late_grads, grad_up, grad_down, grad_ada = lax.optimization_barrier(
        (late, late_grads, grad_up, grad_down, (d_mod_low, cond_all))
    )
    late = scatter(split(late, size), late_ranks)
    late_moments = [
        MUON_MOMENTUM * momentum + grads.astype(F32)
        for momentum, grads in zip(late_momentum, late_grads)
    ]
    block = late_rows // dp_size
    start_proj = [
        late_moments[k * 2 // dp_size][k % (dp_size // 2) * block :][:block]
        for k, mask in enumerate(masks)
        if (mask ^ OWNERS[2]) * block >= 3 * quarter
    ]
    proj_rows = collect(jnp.concatenate(start_proj, axis=0).astype(BF), OWNERS[2:3])
    places, place = dp_places()
    late_moments = reorder(jnp.concatenate(late_moments, axis=0), places, place)
    moment_qkv, moment_proj = late_moments[: 3 * quarter], late_moments[3 * quarter :]
    moments = (
        MUON_MOMENTUM * flat(momentum_ada) + t_dot(*grad_ada),
        moment_qkv,
        moment_proj,
        MUON_MOMENTUM * flat(momentum_up) + grad_up.astype(F32),
        MUON_MOMENTUM * flat(momentum_down) + grad_down.astype(F32),
    )
    starts = [moment.astype(BF) for moment in moments]

    early = collect_doubling(early, early_ranks).reshape(-1, TILE)
    late = collect(total(late), late_ranks)
    late[1], proj_rows = lax.optimization_barrier((late[1], proj_rows))
    proj_gram = lax.cond(
        dp_rank == OWNERS[2],
        lambda *rows: gram_blocks(rows[0], ["plain"] * size, *rows[1:]),
        lambda *rows: none,
        me_index,
        *proj_rows,
    )
    late[2], output = lax.optimization_barrier((late[2], output))
    is_late = (dp_rank == OWNERS[0]) | (dp_rank == OWNERS[1])
    pick = jnp.where(is_late, 1, jnp.where(dp_rank == OWNERS[2], 2, 0)).astype(jnp.int32)
    pick = jnp.concatenate([me_index, pick.reshape(1)])
    no_rows = jnp.zeros((16 - 2 * latent_count, width), BF)
    outgoing = jnp.concatenate([grad_inputs, *parts(d_cond_part), no_rows], axis=0)
    factor = newton_schulz_factor(pick, early, proj_gram, late, width)
    factor, outgoing = lax.optimization_barrier((factor, outgoing))
    outgoing = collect(outgoing)
    grad_inputs = jnp.concatenate([piece[:chunk] for piece in outgoing], axis=0)
    grad_inputs = reorder(grad_inputs, size, me).reshape(inputs.shape)
    d_cond_act = sum(
        total(split(piece[chunk : chunk + 2 * latent_count], 2)) for piece in outgoing
    )
    grad_condition = silu_pull(d_cond_act)[0]
    column_width = width // dp_size
    column_start = dp_rank * column_width
    factors = reorder(factor, masks, dp_rank).reshape(dp_size, column_width, width)
    factors = dp_all_to_all(factors, OWNERS)
    owner_places = jnp.stack(
        [(place ^ places[owner]).astype(jnp.int32) for owner in OWNERS]
    )

    weights_old = (w_ada_old, w_qkv_old, w_proj_old, w_up_old, w_down_old)
    sizes = [max(w.size // width * size, width) for w in weights_old]
    columns = [
        lax.dynamic_slice_in_dim(flat(w), column_start, column_width, 1) for w in weights_old
    ]
    new_weights = update_weights(owner_places, starts, columns, factors, sizes)
    new_weights = [
        new.reshape(old.shape[:-1] + (column_width,))
        for new, old in zip(new_weights, weights_old)
    ]
    new_bias_first = BETA_ONE * bias_first + (1.0 - BETA_ONE) * grad_biases
    new_bias_second = BETA_TWO * bias_second + (1.0 - BETA_TWO) * grad_biases * grad_biases
    first_hat = new_bias_first / (1.0 - BETA_ONE**STEP)
    second_hat = new_bias_second / (1.0 - BETA_TWO**STEP)
    new_biases = biases - ADAM_RATE * first_hat / (jnp.sqrt(second_hat) + ADAM_EPS)
    return (
        output,
        grad_inputs,
        grad_condition,
        *new_weights,
        moments[0].reshape(momentum_ada.shape),
        moments[1].reshape(momentum_qkv.shape),
        moments[2],
        moments[3].reshape(momentum_up.shape),
        moments[4].reshape(momentum_down.shape),
        new_biases,
        new_bias_first,
        new_bias_second,
    )


def solution(mesh):
    placed = (
        P("dp", None, None),
        P("dp", None),
        P("dp", None, None),
        P(None, "tensor", None),
        P(None, "tensor", None),
        P("tensor", None),
        P(None, "tensor", None),
        P(None, "tensor", None),
        P(None, "tensor"),
        P(None, "tensor", None),
        P(None, "tensor", None),
        P("tensor", None),
        P(None, "tensor", None),
        P(None, "tensor", None),
        P(None, "tensor"),
        P(None, "tensor"),
    )
    return jax.shard_map(
        on_device,
        mesh=mesh,
        in_specs=placed,
        out_specs=(
            P("dp", None, None),
            P("dp", None, None),
            P("dp", None),
            P(None, "tensor", "dp"),
            P(None, "tensor", "dp"),
            P("tensor", "dp"),
            P(None, "tensor", "dp"),
            P(None, "tensor", "dp"),
            P(None, "tensor", None),
            P(None, "tensor", None),
            P("tensor", None),
            P(None, "tensor", None),
            P(None, "tensor", None),
            P(None, "tensor"),
            P(None, "tensor"),
            P(None, "tensor"),
        ),
        check_vma=False,
    )
```
